32 devices in a mesh: dp: 8 (over z, x), ctx: 4 (over y, core).
Axes of the slice: x: 2, y: 2, z: 4, core: 2. Of those that a mesh axis runs over, the one named last changes fastest.
Arguments:
- inputs: bfloat16 [2, 8, 1024, 1024], P(None, 'dp', 'ctx'), may hold values from -6 to 6
- cotangent: bfloat16 [2, 8, 1024, 1024], P(None, 'dp', 'ctx'), may hold values from -6 to 6
- image_lengths: int32 [2, 8, 16], P(None, 'dp'), may hold values from 0 to 1024, as said below
- norm1_gain: bfloat16 [1024], replicated, may hold values from 0.25 to 1.75
- norm1_bias: bfloat16 [1024], replicated, may hold values from -1 to 1
- qkv_weight: bfloat16 [1024, 3072], replicated, may hold values from -0.1875 to 0.1875
- qv_bias: bfloat16 [2, 1024], replicated, may hold values from -1.5 to 1.5
- out_weight: bfloat16 [1024, 1024], replicated, may hold values from -0.75 to 0.75
- out_bias: bfloat16 [1024], replicated, may hold values from -1 to 1
- norm2_gain: bfloat16 [1024], replicated, may hold values from 0.25 to 1.75
- norm2_bias: bfloat16 [1024], replicated, may hold values from -1 to 1
- up_weight: bfloat16 [1024, 4096], replicated, may hold values from -0.1875 to 0.1875
- up_bias: bfloat16 [4096], replicated, may hold values from -1.5 to 1.5
- down_weight: bfloat16 [4096, 1024], replicated, may hold values from -0.09375 to 0.09375
- down_bias: bfloat16 [1024], replicated, may hold values from -1 to 1
Outputs:
- block_output: bfloat16 [2, 8, 1024, 1024], P(None, 'dp', 'ctx')
- input_grad: bfloat16 [2, 8, 1024, 1024], P(None, 'dp', 'ctx')
- grad_norm1_gain: float32 [1024], P(('dp', 'ctx'))
- grad_norm1_bias: float32 [1024], P(('dp', 'ctx'))
- grad_qkv_weight: float32 [1024, 3072], P(('dp', 'ctx'))
- grad_qv_bias: float32 [2, 1024], P(None, ('dp', 'ctx'))
- grad_out_weight: float32 [1024, 1024], P(('dp', 'ctx'))
- grad_out_bias: float32 [1024], P(('dp', 'ctx'))
- grad_norm2_gain: float32 [1024], P(('dp', 'ctx'))
- grad_norm2_bias: float32 [1024], P(('dp', 'ctx'))
- grad_up_weight: float32 [1024, 4096], P(('dp', 'ctx'))
- grad_up_bias: float32 [4096], P(('dp', 'ctx'))
- grad_down_weight: float32 [4096, 1024], P(('dp', 'ctx'))
- grad_down_bias: float32 [1024], P(('dp', 'ctx'))
The draws below stay inside these ranges and needn't reach their ends.
Inputs may be any that keep to these rules, and one draw needn't show every extreme that they name: `image_lengths`: in each row the lengths are positive up to the row's last image and zero after it; they sum to 1024 or less, and the rest of the sequence is padding.
All inputs are finite; a program needn't handle non-finite values.
Results may differ from the reference program's by a relative error of at most 0.015.
Values may be sent and summed in bfloat16 or wider, within the bound.
No kernel may reach another device: no remote copies, remote signals or barrier semaphores. Data moves between devices by JAX's collectives and lax.ppermute only.
A program may use at most 256 MiB of HBM per device.

```python
import jax
import jax.numpy as jnp
from jax import lax

D = 1024
HEADS = 16
HEAD_DIM = 64
FF = 4096
MICRO = 2
MAXIMG = 16
PACKS = 1
BATCH = 8
LENGTH = 1024


def draw_image_lengths(key, part):
    key = jax.random.fold_in(key, 11)
    pick_key, size_key = jax.random.split(key)
    sizes = jax.random.randint(size_key, (MICRO, BATCH, MAXIMG), LENGTH // 16, LENGTH // 4 + 1)
    ends = jnp.cumsum(sizes, axis=-1)
    kept = jnp.where(ends <= LENGTH, sizes, 0)
    groups = BATCH // PACKS
    chosen = jax.random.randint(pick_key, (groups,), 0, MICRO * PACKS)
    flat_index = jnp.arange(MICRO)[:, None] * PACKS + (jnp.arange(BATCH) % PACKS)[None, :]
    single_full = flat_index == chosen[jnp.arange(BATCH) // PACKS][None, :]
    single_row = jnp.where(jnp.arange(MAXIMG) == 0, LENGTH, 0)
    return jnp.where(single_full[..., None], single_row[None, None, :], kept).astype(jnp.int32)


def block_levels(own_key, dims, shards, least, high):
    level = 1.0
    for position, shards_of in shards:
        steps = jax.random.uniform(jax.random.fold_in(jax.random.fold_in(own_key, 6), position), (shards_of,), jnp.float32, least / len(shards), high / len(shards))
        level = level * jnp.repeat(jnp.exp(steps), dims[position] // shards_of).reshape((-1,) + (1,) * (len(dims) - 1 - position))
    return level


def normal_values(stream_key, extent, scale, reach, cuts=(), kind=jnp.bfloat16):
    array = scale * jax.random.normal(stream_key, extent, jnp.float32)
    if cuts:
        array = array * block_levels(stream_key, extent, cuts, -0.22, 0.18)
    return jnp.clip(array, -reach, reach).astype(kind)


def setup_inputs(seed: int = 0) -> dict:
    streams_of = jax.random.split(jax.random.key(seed), 16)
    return {
        "inputs": normal_values(streams_of[0], (MICRO, BATCH, LENGTH, D), 1.0, 6.0, ((1, 8), (2, 4))),
        "cotangent": normal_values(streams_of[1], (MICRO, BATCH, LENGTH, D), 1.0, 6.0, ((1, 8), (2, 4))),
        "image_lengths": draw_image_lengths(jax.random.fold_in(streams_of[15], 71), 0),
        "norm1_gain": jnp.clip(1.0 + 0.15 * jax.random.normal(streams_of[3], (D,), jnp.float32), 0.25, 1.75).astype(jnp.bfloat16),
        "norm1_bias": normal_values(streams_of[4], (D,), 0.2, 1.0),
        "qkv_weight": normal_values(streams_of[5], (D, 3 * D), D ** -0.5, 0.1875),
        "qv_bias": normal_values(streams_of[6], (2, D), 0.3, 1.5),
        "out_weight": normal_values(streams_of[7], (D, D), (D // 16) ** -0.5, 0.75),
        "out_bias": normal_values(streams_of[8], (D,), 0.2, 1.0),
        "norm2_gain": jnp.clip(1.0 + 0.15 * jax.random.normal(streams_of[9], (D,), jnp.float32), 0.25, 1.75).astype(jnp.bfloat16),
        "norm2_bias": normal_values(streams_of[10], (D,), 0.2, 1.0),
        "up_weight": normal_values(streams_of[11], (D, FF), D ** -0.5, 0.1875),
        "up_bias": normal_values(streams_of[12], (FF,), 0.3, 1.5),
        "down_weight": normal_values(streams_of[13], (FF, D), FF ** -0.5, 0.09375),
        "down_bias": normal_values(streams_of[14], (D,), 0.2, 1.0),
    }


@jax.custom_vjp
def low(v):
    return lax.optimization_barrier(v.astype(jnp.bfloat16)).astype(jnp.float32)

@jax.custom_vjp
def low_back(v):
    return v

def low_keep(v):
    return (low(v), None)

def low_pass(kept, grad):
    return (grad,)

def back_keep(v):
    return (v, None)

def back_low(kept, grad):
    return (low(grad),)
low.defvjp(low_keep, low_pass)
low_back.defvjp(back_keep, back_low)
NEG = -1e+30
EPS = 1e-06

def layer_norm(values, gain, shift):
    centred = values - lax.optimization_barrier(jnp.mean(values, axis=-1, keepdims=True))
    inverse = lax.rsqrt(lax.optimization_barrier(jnp.mean(centred * centred, axis=-1, keepdims=True)) + EPS)
    return centred * inverse * gain + shift

def product(left, right):
    return jnp.dot(left, right, precision=lax.Precision.HIGHEST, preferred_element_type=jnp.float32)

def segments(lengths):
    ends = jnp.cumsum(lengths)
    positions = jnp.arange(LENGTH, dtype=jnp.int32)
    return lax.optimization_barrier(jnp.sum((positions[:, None] >= ends[None, :]).astype(jnp.int32), axis=1))

def attention(query, keys, values, segment):
    block = min(512, LENGTH)
    scale = HEAD_DIM ** (-0.5)

    def one_block(pair):
        block_rows, block_segs = pair
        allowed = ((block_segs[:, None] == segment[None, :]) & (block_segs[:, None] < MAXIMG))[None]
        scores = low_back(jnp.einsum('qhd,khd->hqk', block_rows, keys, precision=lax.Precision.HIGHEST) * scale)
        scores = jnp.where(allowed, scores, NEG)
        largest = lax.optimization_barrier(jnp.max(scores, axis=-1, keepdims=True))
        weights = jnp.where(allowed, jnp.exp(scores - largest), 0.0)
        totals = lax.optimization_barrier(jnp.sum(weights, axis=-1, keepdims=True))
        chances = low(weights / jnp.where(totals > 0, totals, 1.0))
        return jnp.einsum('hqk,khd->qhd', chances, values, precision=lax.Precision.HIGHEST)
    blocks = lax.map(jax.checkpoint(one_block), (query.reshape(LENGTH // block, block, HEADS, HEAD_DIM), segment.reshape(LENGTH // block, block)))
    return blocks.reshape(LENGTH, HEADS * HEAD_DIM)

def layer(inputs, params, segment):
    gain_one, bias_one, w_qkv, b_qv, w_out, b_out, gain_two, bias_two, w_up, b_up, w_down, b_down = params
    hidden1 = low(layer_norm(inputs, gain_one, bias_one))
    qkv = product(hidden1, w_qkv)
    query = low_back(low(qkv[:, :D] + b_qv[0]))
    keys = low_back(low(qkv[:, D:2 * D]))
    values = low_back(low(qkv[:, 2 * D:] + b_qv[1]))
    head_shape = (LENGTH, HEADS, HEAD_DIM)
    mixed = low_back(low(attention(query.reshape(head_shape), keys.reshape(head_shape), values.reshape(head_shape), segment)))
    middle = inputs + low_back(product(mixed, w_out) + b_out)
    hidden2 = low(layer_norm(middle, gain_two, bias_two))
    upper = low_back(product(hidden2, w_up) + b_up)
    active = low(jax.nn.gelu(upper, approximate=False))
    return middle + product(active, w_down) + b_down

def reference(inputs, cotangent, image_lengths, norm1_gain, norm1_bias, qkv_weight, qv_bias, out_weight, out_bias, norm2_gain, norm2_bias, up_weight, up_bias, down_weight, down_bias):
    params = tuple((weight_arr.astype(jnp.float32) for weight_arr in (norm1_gain, norm1_bias, qkv_weight, qv_bias, out_weight, out_bias, norm2_gain, norm2_bias, up_weight, up_bias, down_weight, down_bias)))
    seq_inputs = inputs.astype(jnp.float32).reshape(MICRO * BATCH, LENGTH, D)
    seq_cotangents = cotangent.astype(jnp.float32).reshape(MICRO * BATCH, LENGTH, D)
    seq_lengths = image_lengths.reshape(MICRO * BATCH, MAXIMG)

    def one_sequence(totals, entry):
        seq_in, seq_cot, seq_len = entry
        segment = segments(seq_len)
        result, pullback = jax.vjp(lambda values_in, params_in: layer(values_in, params_in, segment), seq_in, params)
        grad_in, grad_params = pullback(seq_cot)
        totals = tuple((left + right for left, right in zip(totals, grad_params)))
        return (totals, (result.astype(jnp.bfloat16), grad_in.astype(jnp.bfloat16)))
    zeros_init = tuple((jnp.zeros_like(weight_arr) for weight_arr in params))
    totals, (results, grads_in) = lax.scan(one_sequence, zeros_init, (seq_inputs, seq_cotangents, seq_lengths))
    full_shape = (MICRO, BATCH, LENGTH, D)
    return (results.reshape(full_shape), grads_in.reshape(full_shape), totals[0], totals[1], totals[2], totals[3], totals[4], totals[5], totals[6], totals[7], totals[8], totals[9], totals[10], totals[11])
```

```python
import functools

import jax
import jax.numpy as jnp
from jax import lax
from jax.experimental import pallas as pl
from jax.experimental.pallas import tpu as pltpu
from jax.sharding import PartitionSpec as P

HEADS = 16
HEAD_DIM = 64
NEG = -1e30
EPS = 1e-06
LOG2E = 1.4426950408889634
BF16 = jnp.bfloat16
F32 = jnp.float32
VMEM = 56 * 1024 * 1024

NT = (((1,), (1,)), ((), ()))
NN = (((1,), (0,)), ((), ()))
TN = (((0,), (0,)), ((), ()))


def dot(left, right, dims=NN):
    return lax.dot_general(left, right, dims, preferred_element_type=F32)


def attend_kernel(limit, q_ref, k_ref, v_ref, segq_ref, segk_ref, mixed_ref, inv_ref, w_ref, vt_ref):
    block, wide = q_ref.shape
    heads = wide // HEAD_DIM

    @pl.when(pl.program_id(1) == 0)
    def _():
        values = v_ref[...]
        ones = jnp.ones(values.shape, BF16)
        vt_ref[...] = jnp.concatenate([values, ones], axis=1).T

    scaled = q_ref[...].astype(F32) * (HEAD_DIM ** (-0.5) * LOG2E)
    high = scaled.astype(BF16)
    low = (scaled - high.astype(F32)).astype(BF16)
    keys = k_ref[...]
    keys = jnp.concatenate([keys, keys], axis=1)
    lane = lax.broadcasted_iota(jnp.int32, (block, wide), 1)
    segq = segq_ref[...]
    bias = jnp.where((segk_ref[...] == segq) & (segq < limit), 0.0, NEG)
    mixed_rows = []
    inv_rows = []
    for head in range(heads):
        own = (lane >= head * HEAD_DIM) & (lane < (head + 1) * HEAD_DIM)
        zero = jnp.zeros((), BF16)
        query = jnp.concatenate([jnp.where(own, high, zero), jnp.where(own, low, zero)], axis=1)
        scores = dot(keys, query, NT) + bias
        largest = jnp.max(scores, axis=0, keepdims=True)
        weights = jnp.exp2(scores - largest).astype(BF16)
        w_ref[head] = weights
        summed = dot(vt_ref[...], weights)
        inverse = jnp.where(segq < limit, 1.0 / summed[wide : wide + 1], 0.0)
        mixed_rows.append(summed[head * HEAD_DIM : (head + 1) * HEAD_DIM] * inverse)
        inv_rows.append(jnp.broadcast_to(inverse, (HEAD_DIM, block)))
    mixed_ref[...] = jnp.concatenate(mixed_rows, axis=0).T.astype(BF16)
    inv_ref[...] = jnp.concatenate(inv_rows, axis=0).T


def attend(query, keys, values, segment, limit):
    length, width = query.shape
    heads = width // HEAD_DIM
    pair = min(2, heads)
    wide = pair * HEAD_DIM
    block = min(256, length)
    tile = pl.BlockSpec((block, wide), lambda p, j: (j, p))
    whole = pl.BlockSpec((length, wide), lambda p, j: (0, p))
    return pl.pallas_call(
        functools.partial(attend_kernel, limit),
        grid=(heads // pair, length // block),
        in_specs=[
            tile,
            whole,
            whole,
            pl.BlockSpec((1, block), lambda p, j: (0, j)),
            pl.BlockSpec((length, 1), lambda p, j: (0, 0)),
        ],
        out_specs=[tile, tile, pl.BlockSpec((pair, length, block), lambda p, j: (p, 0, j))],
        out_shape=[
            jax.ShapeDtypeStruct((length, width), BF16),
            jax.ShapeDtypeStruct((length, width), F32),
            jax.ShapeDtypeStruct((heads, length, length), BF16),
        ],
        scratch_shapes=[pltpu.VMEM((2 * wide, length), BF16)],
        compiler_params=pltpu.CompilerParams(vmem_limit_bytes=VMEM),
        name="attend",
    )(query, keys, values, segment.reshape(1, length), segment.reshape(length, 1))


def attend_back_kernel(
    q_ref, k_ref, v_ref, do_ref, mixed_ref, inv_ref, w_ref, dq_ref, dk_ref, dv_ref, kt_ref, dk_sum, dv_sum
):
    block, wide = q_ref.shape
    heads = wide // HEAD_DIM
    length = k_ref.shape[0]
    step = pl.program_id(1)

    @pl.when(step == 0)
    def _():
        kt_ref[...] = k_ref[...].T
        dk_sum[...] = jnp.zeros_like(dk_sum)
        dv_sum[...] = jnp.zeros_like(dv_sum)

    grad = do_ref[...].astype(F32)
    inverse = inv_ref[...]
    product = grad * mixed_ref[...].astype(F32)
    grad = (grad * inverse).astype(BF16)
    query = q_ref[...]
    lane = lax.broadcasted_iota(jnp.int32, (block, wide), 1)
    key_lane = lax.broadcasted_iota(jnp.int32, (length, wide), 1)
    zero = jnp.zeros((), BF16)
    minus = jnp.where(key_lane < 2, -jnp.ones((), BF16), zero)
    values = jnp.concatenate([v_ref[...], minus], axis=1)
    dq_rows = []
    for head in range(heads):
        own = (lane >= head * HEAD_DIM) & (lane < (head + 1) * HEAD_DIM)
        delta = jnp.sum(jnp.where(own, product * inverse, 0.0), axis=1, keepdims=True)
        high = delta.astype(BF16)
        low = (delta - high.astype(F32)).astype(BF16)
        extra = jnp.where(lane == 0, high, jnp.where(lane == 1, low, zero))
        own_grad = jnp.where(own, grad, zero)
        weights = w_ref[head]
        d_probs = dot(values, jnp.concatenate([own_grad, extra], axis=1), NT)
        d_scores = weights * d_probs.astype(BF16)
        dv_sum[...] += dot(weights, own_grad)
        dk_sum[...] += dot(d_scores, jnp.where(own, query, zero))
        dq_rows.append(dot(kt_ref[head * HEAD_DIM : (head + 1) * HEAD_DIM], d_scores))
    scale = HEAD_DIM ** (-0.5)
    dq_ref[...] = (jnp.concatenate(dq_rows, axis=0).T * scale).astype(BF16)

    @pl.when(step == pl.num_programs(1) - 1)
    def _():
        dk_ref[...] = (dk_sum[...] * scale).astype(BF16)
        dv_ref[...] = dv_sum[...].astype(BF16)


def attend_back(query, keys, values, d_mixed, mixed, inverse, weights):
    length, width = query.shape
    heads = width // HEAD_DIM
    pair = min(2, heads)
    wide = pair * HEAD_DIM
    block = min(256, length)
    tile = pl.BlockSpec((block, wide), lambda p, j: (j, p))
    whole = pl.BlockSpec((length, wide), lambda p, j: (0, p))
    shape = jax.ShapeDtypeStruct((length, width), BF16)
    return pl.pallas_call(
        attend_back_kernel,
        grid=(heads // pair, length // block),
        in_specs=[
            tile,
            whole,
            whole,
            tile,
            tile,
            tile,
            pl.BlockSpec((pair, length, block), lambda p, j: (p, 0, j)),
        ],
        out_specs=[tile, whole, whole],
        out_shape=[shape, shape, shape],
        scratch_shapes=[
            pltpu.VMEM((wide, length), BF16),
            pltpu.VMEM((length, wide), F32),
            pltpu.VMEM((length, wide), F32),
        ],
        compiler_params=pltpu.CompilerParams(vmem_limit_bytes=VMEM),
        name="attend_back",
    )(query, keys, values, d_mixed, mixed, inverse, weights)


def feed_kernel(
    h_ref, cot_ref, up_ref, upb_ref, down_ref, active_ref, dup_ref, dub_ref, out_ref, dh_ref, out_sum, dh_sum
):
    step = pl.program_id(1)

    @pl.when(step == 0)
    def _():
        out_sum[...] = jnp.zeros_like(out_sum)
        dh_sum[...] = jnp.zeros_like(dh_sum)

    up = up_ref[...]
    down = down_ref[...]
    upper = dot(h_ref[...], up) + upb_ref[...].astype(F32)
    d_active = dot(cot_ref[...], down, NT)
    half = 0.5 + 0.5 * lax.erf(upper * 0.7071067811865476)
    bell = jnp.exp2(upper * upper * (-0.5 * LOG2E)) * 0.3989422804014327
    active = (upper * half).astype(BF16)
    d_upper = d_active * (half + upper * bell)
    d_low = d_upper.astype(BF16)
    active_ref[...] = active
    dup_ref[...] = d_low
    dub_ref[...] = jnp.sum(d_low.astype(F32), axis=0, keepdims=True)[None]
    out_sum[...] += dot(active, down)
    dh_sum[...] += dot(d_low, up, NT)

    @pl.when(step == pl.num_programs(1) - 1)
    def _():
        out_ref[...] = out_sum[...].astype(out_ref.dtype)
        dh_ref[...] = dh_sum[...].astype(dh_ref.dtype)


def feed(hidden, cotangent, up, up_bias, down):
    length, width = hidden.shape
    ff = up.shape[1]
    rows = min(length, 1024)
    tile = min(256, ff)
    row_spec = pl.BlockSpec((rows, width), lambda i, t: (i, 0))
    ff_spec = pl.BlockSpec((rows, tile), lambda i, t: (i, t))
    return pl.pallas_call(
        feed_kernel,
        grid=(length // rows, ff // tile),
        in_specs=[
            row_spec,
            row_spec,
            pl.BlockSpec((width, tile), lambda i, t: (0, t)),
            pl.BlockSpec((1, tile), lambda i, t: (0, t)),
            pl.BlockSpec((tile, width), lambda i, t: (t, 0)),
        ],
        out_specs=[
            ff_spec,
            ff_spec,
            pl.BlockSpec((1, 1, tile), lambda i, t: (i, 0, t)),
            row_spec,
            row_spec,
        ],
        out_shape=[
            jax.ShapeDtypeStruct((length, ff), BF16),
            jax.ShapeDtypeStruct((length, ff), BF16),
            jax.ShapeDtypeStruct((length // rows, 1, ff), F32),
            jax.ShapeDtypeStruct((length, width), BF16),
            jax.ShapeDtypeStruct((length, width), BF16),
        ],
        scratch_shapes=[pltpu.VMEM((rows, width), F32), pltpu.VMEM((rows, width), F32)],
        compiler_params=pltpu.CompilerParams(vmem_limit_bytes=VMEM),
        name="feed",
    )(hidden, cotangent, up, up_bias, down)


def norm_parts(values):
    centred = values - jnp.mean(values, axis=-1, keepdims=True)
    inverse = lax.rsqrt(jnp.mean(centred * centred, axis=-1, keepdims=True) + EPS)
    return centred * inverse, inverse


def norm_back(grad, normal, inverse, gain):
    scaled = grad * gain
    inner = (
        scaled
        - jnp.mean(scaled, axis=-1, keepdims=True)
        - normal * jnp.mean(scaled * normal, axis=-1, keepdims=True)
    )
    return inverse * inner


def body(
    inputs,
    cotangent,
    image_lengths,
    norm1_gain,
    norm1_bias,
    qkv_weight,
    qv_bias,
    out_weight,
    out_bias,
    norm2_gain,
    norm2_bias,
    up_weight,
    up_bias,
    down_weight,
    down_bias,
):
    rows, width = inputs.shape[2:]
    limit = image_lengths.shape[-1]
    ff = up_weight.shape[1]
    dp_size = lax.axis_size("dp")
    ctx_size = lax.axis_size("ctx")
    group = ctx_size // 2
    dp_index = lax.axis_index("dp")
    ctx_index = lax.axis_index("ctx")
    half = ctx_index // group
    member = ctx_index % group
    length = rows * ctx_size
    chips = dp_size * 2
    dp_bits = dp_size.bit_length() - 1
    own_heads = HEADS // group
    own_width = own_heads * HEAD_DIM
    block_rows = ff // (chips * group)

    def across(value):
        pairs = [(i, (i + group) % ctx_size) for i in range(ctx_size)]
        return lax.ppermute(value, "ctx", pairs)

    def around(value, steps):
        pairs = [
            (h * group + g, h * group + (g + steps) % group) for h in range(2) for g in range(group)
        ]
        return lax.ppermute(value, "ctx", pairs)

    def gather(value):
        parts = [value] + [around(value, steps) for steps in range(1, group)]
        if group == 2:
            first = member == 0
            return jnp.stack(
                [jnp.where(first, parts[0], parts[1]), jnp.where(first, parts[1], parts[0])]
            )
        stacked = jnp.stack(parts[::-1])
        return jnp.roll(stacked, member + 1, axis=0)

    def pick(value, index, axis):
        return lax.dynamic_index_in_dim(value, index, axis, keepdims=False)

    def group_sum_scatter(value, axis):
        total = pick(value, member, axis).astype(F32)
        for steps in range(1, group):
            total = total + around(pick(value, (member + steps) % group, axis), steps).astype(F32)
        return total

    def group_sum(value):
        total = value.astype(F32)
        for steps in range(1, group):
            total = total + around(value, steps).astype(F32)
        return total

    def swap_bit(value, bit):
        if bit < 0:
            return across(value)
        return lax.ppermute(value, "dp", [(i, i ^ (1 << bit)) for i in range(dp_size)])

    def bit_of(bit):
        return half if bit < 0 else (dp_index >> bit) & 1

    def chip_scatter(value, order, dtype=BF16):
        rest = value.shape[1:]
        value = value.reshape((2,) * (dp_bits + 1) + rest)
        left = list(range(dp_bits - 1, -1, -1)) + [-1]
        keep = send = None
        for number, bit in enumerate(order):
            axis = left.index(bit)
            mine = bit_of(bit)
            if number == 0:
                keep = pick(value, mine, axis)
                send = pick(value, 1 - mine, axis)
            else:
                keep, send = (
                    pick(keep, mine, axis).astype(F32) + pick(came, mine, axis).astype(F32),
                    pick(keep, 1 - mine, axis).astype(F32) + pick(came, 1 - mine, axis).astype(F32),
                )
                keep = keep.astype(dtype)
                send = send.astype(dtype)
            left.pop(axis)
            came = swap_bit(send, bit)
        return keep.astype(F32) + came.astype(F32)

    own_inputs = pick(inputs, half, 0)[0]
    other_inputs = across(pick(inputs, 1 - half, 0)[0])
    own_cot = pick(cotangent, half, 0)[0]
    other_cot = across(pick(cotangent, 1 - half, 0)[0])
    x_rows = jnp.concatenate([gather(own_inputs), gather(other_inputs)]).reshape(length, width)
    cot_rows = jnp.concatenate([gather(own_cot), gather(other_cot)]).reshape(length, width)

    place = jnp.arange(length, dtype=jnp.int32).reshape(2, length // 2)
    positions = jnp.where(half == 0, place, place[::-1]).reshape(length)
    ends = jnp.cumsum(pick(image_lengths, half, 0)[0])
    segment = jnp.sum((positions[:, None] >= ends[None, :]).astype(jnp.int32), axis=1)

    qkv_own = pick(qkv_weight.reshape(width, 3, group, own_width), member, 2).reshape(width, 3 * own_width)
    up_own = pick(up_weight.reshape(width, chips, group, block_rows), member, 2).reshape(width, ff // group)
    upb_own = pick(up_bias.reshape(chips, group, block_rows), member, 1).reshape(1, ff // group)
    down_own = pick(down_weight.reshape(chips, group, block_rows, width), member, 1).reshape(ff // group, width)
    bias_own = pick(qv_bias.reshape(2, group, own_width), member, 1)

    normal1, _ = norm_parts(x_rows.astype(F32))
    hidden1 = (normal1 * norm1_gain + norm1_bias).astype(BF16)
    qkv = dot(hidden1, qkv_own)
    query = (qkv[:, :own_width] + bias_own[0]).astype(BF16)
    keys = qkv[:, own_width : 2 * own_width].astype(BF16)
    values = (qkv[:, 2 * own_width :] + bias_own[1]).astype(BF16)
    mixed, inverse, weights = attend(query, keys, values, segment, limit)
    mixed_all = jnp.swapaxes(gather(mixed), 0, 1).reshape(length, width)
    middle = x_rows.astype(F32) + dot(mixed_all, out_weight) + out_bias
    normal2, inverse2 = norm_parts(middle)
    hidden2 = (normal2 * norm2_gain + norm2_bias).astype(BF16)
    active, d_upper, upb_grad, out_part, dh_part = feed(hidden2, cot_rows, up_own, upb_own, down_own)

    d_hidden2 = group_sum(dh_part)
    down_grad = dot(active, cot_rows, TN).astype(BF16).reshape(chips, block_rows, width)
    up_grad = dot(hidden2, d_upper, TN).astype(BF16).reshape(chips, width // chips, ff // group)

    order_a = [0] + list(range(1, dp_bits)) + [-1]
    order_b = [-1, 0] + list(range(1, dp_bits))
    order_c = list(range(1, dp_bits)) + [0, -1]

    def spread(value, cuts, orders):
        parts = []
        start = 0
        for cut, order in zip(cuts, orders):
            parts.append(chip_scatter(value[:, :, start : start + cut], order))
            start += cut
        return jnp.concatenate(parts, axis=-1) if len(parts) > 1 else parts[0]

    def thirds(columns):
        first = columns * 3 // 8 // 128 * 128
        if first == 0:
            return [columns], [order_a]
        return [first, first, columns - 2 * first], [order_a, order_b, order_c]

    down_total = spread(down_grad, *thirds(width))
    up_total = spread(up_grad, *thirds(ff // group))

    own_rows = (2, group, rows, width)
    out_sum = group_sum_scatter(out_part.reshape(own_rows), 1)
    middle_own = pick(middle.reshape(own_rows), member, 1)
    result = (out_sum + middle_own + down_bias).astype(BF16)

    def hand_back(value):
        came = across(value[1])
        first = half == 0
        return jnp.stack(
            [jnp.where(first, value[0], came), jnp.where(first, came, value[0])]
        )[:, None]

    block_output = hand_back(result)

    d_middle = cot_rows.astype(F32) + norm_back(d_hidden2, normal2, inverse2, norm2_gain)
    d_branch = d_middle.astype(BF16)
    wo_own = pick(out_weight.reshape(group, own_width, width), member, 0)
    d_mixed = dot(d_branch, wo_own, NT).astype(BF16)
    d_branch_own = pick(d_branch.reshape(length, group, width // group), member, 1)
    out_grad = dot(mixed_all, d_branch_own, TN).astype(BF16).reshape(chips, width // chips, width // group)
    out_total = spread(out_grad, [width // group], [order_c])
    d_query, d_keys, d_values = attend_back(query, keys, values, d_mixed, mixed, inverse, weights)
    d_qkv = jnp.concatenate([d_query, d_keys, d_values], axis=1)
    qkv_grad = dot(hidden1, d_qkv, TN).astype(BF16).reshape(chips, width // chips, 3 * own_width)
    qkv_total = spread(qkv_grad, *thirds(3 * own_width))
    dh1_part = dot(d_qkv, qkv_own, NT).astype(BF16)
    d_hidden1 = group_sum_scatter(dh1_part.reshape(own_rows), 1)
    x_own = pick(x_rows.reshape(own_rows), member, 1).astype(F32)
    n1_own, i1_own = norm_parts(x_own)
    d_middle_own = pick(d_middle.reshape(own_rows), member, 1)
    input_grad = hand_back((d_middle_own + norm_back(d_hidden1, n1_own, i1_own, norm1_gain)).astype(BF16))

    both = 1.0 / group
    member_is = (jnp.arange(group, dtype=jnp.int32) == member).astype(F32)

    def at_member(vector):
        return (member_is[:, None] * vector[None, :]).reshape(-1)

    upb_sum = jnp.sum(upb_grad, axis=(0, 1)).reshape(chips, 1, block_rows)
    upb_full = (member_is[None, :, None] * upb_sum).reshape(chips, group, block_rows)
    vectors = [
        jnp.sum(d_hidden1 * n1_own, axis=(0, 1)),
        jnp.sum(d_hidden1, axis=(0, 1)),
        at_member(jnp.sum(d_query.astype(F32), axis=0)),
        at_member(jnp.sum(d_values.astype(F32), axis=0)),
        jnp.sum(d_branch.astype(F32), axis=0) * both,
        jnp.sum(d_hidden2 * normal2, axis=0) * both,
        jnp.sum(d_hidden2, axis=0) * both,
        jnp.sum(cotangent[:, 0].astype(F32), axis=(0, 1)),
    ]
    small = jnp.stack(vectors).reshape(len(vectors), chips, group, width // (chips * group))
    small = jnp.transpose(small, (1, 2, 0, 3)).reshape(chips, group, -1)
    small = jnp.concatenate([small, upb_full], axis=-1)
    small = chip_scatter(small, order_a, F32)
    small = group_sum_scatter(small, 0)
    own_cols = width // (chips * group)
    small_rows = small[: len(vectors) * own_cols].reshape(len(vectors), own_cols)
    upb_out = small[len(vectors) * own_cols :]

    def exchange(value):
        own = value.shape[0] // group
        value = value.reshape(group, own, value.shape[1])
        parts = [pick(value, member, 0)] + [
            around(pick(value, (member + steps) % group, 0).astype(BF16), steps).astype(F32)
            for steps in range(1, group)
        ]
        if group == 2:
            first = member == 0
            return jnp.stack(
                [jnp.where(first, parts[0], parts[1]), jnp.where(first, parts[1], parts[0])], axis=1
            )
        return jnp.swapaxes(jnp.roll(jnp.stack(parts[::-1]), member + 1, axis=0), 0, 1)

    own = width // (chips * group)
    up_out = exchange(up_total).reshape(own, group, chips, block_rows)
    up_out = jnp.swapaxes(up_out, 1, 2).reshape(own, ff)
    qkv_out = exchange(qkv_total).reshape(own, group, 3, own_width)
    qkv_out = jnp.swapaxes(qkv_out, 1, 2).reshape(own, 3 * width)
    out_out = exchange(out_total).reshape(own, width)
    return (
        block_output,
        input_grad,
        small_rows[0],
        small_rows[1],
        qkv_out,
        small_rows[2:4],
        out_out,
        small_rows[4],
        small_rows[5],
        small_rows[6],
        up_out,
        upb_out,
        down_total,
        small_rows[7],
    )


def solution(mesh):
    split = P(None, "dp", "ctx", None)
    both = ("dp", "ctx")
    return jax.shard_map(
        body,
        mesh=mesh,
        in_specs=(split, split, P(None, "dp", None)) + (P(),) * 12,
        out_specs=(
            split,
            split,
            P(both),
            P(both),
            P(both, None),
            P(None, both),
            P(both, None),
            P(both),
            P(both),
            P(both),
            P(both, None),
            P(both),
            P(both, None),
            P(both),
        ),
        check_vma=False,
    )
```

```python
import functools

import jax
import jax.numpy as jnp
from jax import lax
from jax.experimental import pallas as pl
from jax.experimental.pallas import tpu as pltpu
from jax.sharding import PartitionSpec as P

HEADS = 16
HEAD_DIM = 64
PAIR = 2 * HEAD_DIM
NEG = -1e30
EPS = 1e-06
LOG2E = 1.4426950408889634
SCALE = HEAD_DIM ** (-0.5)
BF16 = jnp.bfloat16
F32 = jnp.float32
VMEM = 60 * 1024 * 1024

NT = (((1,), (1,)), ((), ()))
NN = (((1,), (0,)), ((), ()))
TN = (((0,), (0,)), ((), ()))


def dot(left, right, dims=NN):
    return lax.dot_general(left, right, dims, preferred_element_type=F32)


def call(kernel, name, place, args, grid, in_specs, outs, scratch=(), flops=0, moved=0):
    return pl.pallas_call(
        kernel,
        grid_spec=pltpu.PrefetchScalarGridSpec(
            num_scalar_prefetch=1,
            grid=grid,
            in_specs=in_specs,
            out_specs=[spec for _, _, spec in outs],
            scratch_shapes=list(scratch),
        ),
        out_shape=[jax.ShapeDtypeStruct(shape, dtype) for shape, dtype, _ in outs],
        compiler_params=pltpu.CompilerParams(vmem_limit_bytes=VMEM),
        cost_estimate=pl.CostEstimate(flops=flops, bytes_accessed=moved, transcendentals=0),
        name=name,
    )(place, *args)


def norm_parts(values):
    centred = values - jnp.mean(values, axis=-1, keepdims=True)
    inverse = lax.rsqrt(jnp.mean(centred * centred, axis=-1, keepdims=True) + EPS)
    return centred * inverse, inverse


def norm_back(grad, normal, inverse, gain):
    scaled = grad * gain
    inner = (
        scaled
        - jnp.mean(scaled, axis=-1, keepdims=True)
        - normal * jnp.mean(scaled * normal, axis=-1, keepdims=True)
    )
    return inverse * inner


def project_kernel(
    sub, place, x_ref, gain_ref, shift_ref, wq_ref, wk_ref, wv_ref, qvb_ref, ht_ref, q_ref, k_ref, v_ref
):
    gain = gain_ref[...].astype(F32)
    shift = shift_ref[...].astype(F32)
    qvb = qvb_ref[...].astype(F32)
    for start in range(0, x_ref.shape[0], sub):
        part = pl.ds(start, sub)
        normal, _ = norm_parts(x_ref[part].astype(F32))
        hidden = (normal * gain + shift).astype(BF16)
        ht_ref[:, part] = hidden.T
        q_ref[part] = (dot(hidden, wq_ref[...]) + qvb[0:1]).astype(BF16)
        k_ref[part] = dot(hidden, wk_ref[...]).astype(BF16)
        v_ref[part] = (dot(hidden, wv_ref[...]) + qvb[1:2]).astype(BF16)


def project(place, x_rows, gain, shift, qkv_weight, qv_bias, group):
    length, width = x_rows.shape
    own = width // group
    rows = min(512, length)
    vector = pl.BlockSpec((1, width), lambda i, s: (0, 0))
    row = pl.BlockSpec((rows, own), lambda i, s: (i, 0))
    weights = [
        pl.BlockSpec((width, own), functools.partial(lambda t, i, s: (0, t * group + s[0]), t))
        for t in range(3)
    ]
    return call(
        functools.partial(project_kernel, min(256, rows)),
        "project",
        place,
        (x_rows, gain.reshape(1, width), shift.reshape(1, width), qkv_weight, qkv_weight, qkv_weight, qv_bias),
        (length // rows,),
        [pl.BlockSpec((rows, width), lambda i, s: (i, 0)), vector, vector]
        + weights
        + [pl.BlockSpec((2, own), lambda i, s: (0, s[0]))],
        [((width, length), BF16, pl.BlockSpec((width, rows), lambda i, s: (0, i)))]
        + [((length, own), BF16, row)] * 3,
        flops=6 * length * width * own,
        moved=2 * (2 * length * width + 3 * width * own + 3 * length * own),
    )


def attend_kernel(limit, sub, place, q_ref, k_ref, v_ref, segc_ref, segr_ref, mixed_ref, lse_ref):
    keys = k_ref[...]
    keys = jnp.concatenate([keys, keys], axis=1)
    values = v_ref[...]
    values = jnp.concatenate([values, jnp.ones(values.shape, BF16)], axis=1)
    lane = lax.broadcasted_iota(jnp.int32, (sub, PAIR), 1)
    zero = jnp.zeros((), BF16)
    segr = segr_ref[...]
    for start in range(0, q_ref.shape[0], sub):
        part = pl.ds(start, sub)
        scaled = q_ref[part].astype(F32) * (SCALE * LOG2E)
        high = scaled.astype(BF16)
        low = (scaled - high.astype(F32)).astype(BF16)
        segc = segc_ref[part]
        valid = segc < limit
        bias = jnp.where(jnp.where(valid, segc, -1)[:, :1] == segr, 0.0, NEG)
        mixed = []
        logs = []
        for head in range(2):
            own = (lane < HEAD_DIM) == (head == 0)
            query = jnp.concatenate([jnp.where(own, high, zero), jnp.where(own, low, zero)], axis=1)
            scores = dot(query, keys, NT) + bias
            largest = jnp.max(scores, axis=1, keepdims=True)
            weights = jnp.exp2(scores - largest).astype(BF16)
            summed = dot(weights, values)
            total = summed[:, PAIR:]
            mixed.append(summed[:, :PAIR] / total)
            logs.append(largest + jnp.log2(total))
        first = lane < HEAD_DIM
        mixed_ref[part] = jnp.where(valid, jnp.where(first, mixed[0], mixed[1]), 0.0).astype(BF16)
        lse_ref[part] = jnp.where(valid, jnp.where(first, logs[0], logs[1]), 0.0)


def attend(place, query, keys, values, seg_cols, seg_row, limit):
    length, width = query.shape
    block = min(1024, length)
    tile = pl.BlockSpec((block, PAIR), lambda p, j, s: (j, p))
    whole = pl.BlockSpec((length, PAIR), lambda p, j, s: (0, p))
    return call(
        functools.partial(attend_kernel, limit, min(256, block)),
        "attend",
        place,
        (query, keys, values, seg_cols, seg_row),
        (width // PAIR, length // block),
        [
            tile,
            whole,
            whole,
            pl.BlockSpec((block, PAIR), lambda p, j, s: (j, 0)),
            pl.BlockSpec((1, length), lambda p, j, s: (0, 0)),
        ],
        [((length, width), BF16, tile), ((length, width), F32, tile)],
        flops=16 * length * length * width,
        moved=14 * length * width,
    )


def attend_back_kernel(
    limit,
    sub,
    place,
    q_ref,
    k_ref,
    v_ref,
    do_ref,
    mixed_ref,
    lse_ref,
    segc_ref,
    segr_ref,
    dq_ref,
    dk_ref,
    dv_ref,
    kt_ref,
    dk_sum,
    dv_sum,
):
    step = pl.program_id(0)
    steps = pl.num_programs(0)
    length = k_ref.shape[0]
    keys = k_ref[...]
    kt_ref[...] = keys.T
    zero = jnp.zeros((), BF16)
    minus = -jnp.ones((), BF16)
    values = v_ref[...]
    key_lane = lax.broadcasted_iota(jnp.int32, (length, PAIR), 1)
    lane = lax.broadcasted_iota(jnp.int32, (sub, PAIR), 1)
    spot = lane & (HEAD_DIM - 1)
    ones = jnp.where((key_lane & (HEAD_DIM - 1)) < 3, minus, zero)
    key_sides = []
    value_sides = []
    for head in range(2):
        own = (key_lane < HEAD_DIM) == (head == 0)
        key_sides.append(jnp.concatenate([jnp.where(own, keys, ones), keys], axis=1))
        value_sides.append(jnp.where(own, values, ones))
    segc = segc_ref[...]
    segc = jnp.where(segc < limit, segc, -1)[:, :1]

    def in_three(value):
        high = value.astype(BF16)
        rest = value - high.astype(F32)
        middle = rest.astype(BF16)
        low = (rest - middle.astype(F32)).astype(BF16)
        return jnp.where(spot == 0, high, jnp.where(spot == 1, middle, jnp.where(spot == 2, low, zero)))

    dk_all = dv_all = None
    for start in range(0, q_ref.shape[0], sub):
        part = pl.ds(start, sub)
        query = q_ref[part]
        scaled = query.astype(F32) * (SCALE * LOG2E)
        high = scaled.astype(BF16)
        low = (scaled - high.astype(F32)).astype(BF16)
        grad = do_ref[part]
        product = grad.astype(F32) * mixed_ref[part].astype(F32)
        logs = lse_ref[part]
        same = segc == segr_ref[:, part]
        dq_rows = []
        for head in range(2):
            own = (lane < HEAD_DIM) == (head == 0)
            log = jnp.broadcast_to(logs[:, head * HEAD_DIM : head * HEAD_DIM + 1], logs.shape)
            delta = jnp.sum(jnp.where(own, product, 0.0), axis=1, keepdims=True)
            delta = jnp.broadcast_to(delta, logs.shape)
            query_side = jnp.concatenate(
                [jnp.where(own, high, in_three(log)), jnp.where(own, low, zero)], axis=1
            )
            grad_side = jnp.where(own, grad, in_three(delta))
            scores = dot(key_sides[head], query_side, NT)
            probs = jnp.where(same, jnp.exp2(scores), 0.0).astype(BF16)
            d_probs = dot(value_sides[head], grad_side, NT)
            d_scores = probs * d_probs.astype(BF16)
            dv_part = dot(probs, jnp.where(own, grad, zero))
            dk_part = dot(d_scores, jnp.where(own, query, zero))
            dv_all = dv_part if dv_all is None else dv_all + dv_part
            dk_all = dk_part if dk_all is None else dk_all + dk_part
            dq_rows.append(dot(kt_ref[head * HEAD_DIM : (head + 1) * HEAD_DIM], d_scores))
        dq_ref[part] = (jnp.concatenate(dq_rows, axis=0).T * SCALE).astype(BF16)
    dk_all = dk_all * SCALE

    @pl.when(step == 0)
    def _():
        dk_sum[...] = dk_all
        dv_sum[...] = dv_all

    @pl.when(step > 0)
    def _():
        dk_sum[...] += dk_all
        dv_sum[...] += dv_all

    @pl.when(step == steps - 1)
    def _():
        dk_ref[...] = dk_sum[...].astype(BF16)
        dv_ref[...] = dv_sum[...].astype(BF16)


def attend_back(place, pair, query, keys, values, d_mixed, mixed, logs, seg_cols, seg_row, limit):
    length = query.shape[0]
    block = min(1024, length)
    tile = pl.BlockSpec((block, PAIR), lambda j, s: (j, pair))
    whole = pl.BlockSpec((length, PAIR), lambda j, s: (0, pair))
    out_tile = pl.BlockSpec((block, PAIR), lambda j, s: (j, 0))
    out_whole = pl.BlockSpec((length, PAIR), lambda j, s: (0, 0))
    return call(
        functools.partial(attend_back_kernel, limit, min(256, block)),
        "attend_back",
        place,
        (query, keys, values, d_mixed, mixed, logs, seg_cols, seg_row),
        (length // block,),
        [
            tile,
            whole,
            whole,
            tile,
            tile,
            tile,
            pl.BlockSpec((length, PAIR), lambda j, s: (0, 0)),
            pl.BlockSpec((1, block), lambda j, s: (0, j)),
        ],
        [
            ((length, PAIR), BF16, out_tile),
            ((length, PAIR), BF16, out_whole),
            ((length, PAIR), BF16, out_whole),
        ],
        [pltpu.VMEM((PAIR, length), BF16), pltpu.VMEM((length, PAIR), F32), pltpu.VMEM((length, PAIR), F32)],
        flops=40 * length * length * PAIR,
        moved=20 * length * PAIR,
    )


def close_kernel(group, place, x_ref, gain_ref, shift_ref, bias_ref, *refs):
    mixed_refs = refs[:group]
    weight_refs = refs[group : 2 * group]
    middle_ref, hidden_ref, ht_ref = refs[2 * group :]
    middle = x_ref[...].astype(F32) + bias_ref[...].astype(F32)
    for mixed_ref, weight_ref in zip(mixed_refs, weight_refs):
        middle = middle + dot(mixed_ref[...], weight_ref[...])
    middle_ref[...] = middle
    normal, _ = norm_parts(middle)
    hidden = (normal * gain_ref[...].astype(F32) + shift_ref[...].astype(F32)).astype(BF16)
    hidden_ref[...] = hidden
    ht_ref[...] = hidden.T


def close(place, x_rows, mixed_parts, out_weight, out_bias, gain, shift):
    length, width = x_rows.shape
    group = len(mixed_parts)
    own = width // group
    rows = min(256, length)
    vector = pl.BlockSpec((1, width), lambda i, s: (0, 0))
    row = pl.BlockSpec((rows, width), lambda i, s: (i, 0))
    weights = [
        pl.BlockSpec((own, width), functools.partial(lambda t, i, s: ((s[0] + group - t) % group, 0), t))
        for t in range(group)
    ]
    return call(
        functools.partial(close_kernel, group),
        "close",
        place,
        (x_rows, gain.reshape(1, width), shift.reshape(1, width), out_bias.reshape(1, width))
        + tuple(mixed_parts)
        + (out_weight,) * group,
        (length // rows,),
        [row, vector, vector, vector] + [pl.BlockSpec((rows, own), lambda i, s: (i, 0))] * group + weights,
        [
            ((length, width), F32, row),
            ((length, width), BF16, row),
            ((width, length), BF16, pl.BlockSpec((width, rows), lambda i, s: (0, i))),
        ],
        flops=2 * length * width * width,
        moved=12 * length * width,
    )


def up_specs(width, tile, block, group, number):
    return [
        pl.BlockSpec((width, block), functools.partial(lambda n, t, s: (0, (t * number + n) * group + s[0]), n))
        for n in range(number)
    ]


def feed_up_kernel(number, parts, place, h_ref, cot_ref, upb_ref, *refs):
    up_refs = refs[:number]
    active_ref, slope_ref, grad_ref = refs[number:]
    up = jnp.concatenate([ref[...] for ref in up_refs], axis=1) if number > 1 else up_refs[0][...]
    upper = dot(h_ref[...], up) + upb_ref[...].astype(F32)
    half = 0.5 + 0.5 * lax.erf(upper * 0.7071067811865476)
    bell = jnp.exp2(upper * upper * (-0.5 * LOG2E)) * 0.3989422804014327
    active = (upper * half).astype(BF16)
    active_ref[...] = active
    slope_ref[...] = (half + upper * bell).astype(BF16)
    grad = dot(active, cot_ref[...], TN).astype(BF16)
    rows = grad.shape[0] // parts
    for part in range(parts):
        spot = jnp.bitwise_xor(jnp.int32(part), place[1] % parts)
        grad_ref[spot] = grad[part * rows : (part + 1) * rows]


def feed_up(place, hidden, cotangent, up_arrays, up_blocks, upb_own, chips):
    length, width = hidden.shape
    ff = upb_own.shape[1]
    chunk = ff // chips
    tile = min(512 if length <= 1024 else 128, ff)
    parts = tile // chunk
    whole = pl.BlockSpec((length, width), lambda t, s: (0, 0), pipeline_mode=pl.Buffered(1))
    tiled = pl.BlockSpec((length, tile), lambda t, s: (0, t))
    number, specs = up_blocks(tile)
    return call(
        functools.partial(feed_up_kernel, number, parts),
        "feed_up",
        place,
        (hidden, cotangent, upb_own) + (up_arrays,) * number,
        (ff // tile,),
        [whole, whole, pl.BlockSpec((1, tile), lambda t, s: (0, t))] + specs,
        [
            ((length, ff), BF16, tiled),
            ((length, ff), BF16, tiled),
            (
                (chips, chunk, width),
                BF16,
                pl.BlockSpec((parts, chunk, width), lambda t, s: (jnp.bitwise_xor(t, s[1] // parts), 0, 0)),
            ),
        ],
        flops=4 * length * width * ff,
        moved=4 * (width * ff + length * ff + length * width),
    )


def feed_back_kernel(number, chips, place, ht_ref, cot_ref, slope_ref, down_ref, *refs):
    up_refs = refs[:number]
    dh_ref, grad_ref, dub_ref, dh_sum = refs[number:]
    step = pl.program_id(0)
    up = jnp.concatenate([ref[...] for ref in up_refs], axis=1) if number > 1 else up_refs[0][...]
    down = down_ref[...]
    down = down.reshape(down.shape[0] * down.shape[2], down.shape[3])
    d_upper = (dot(cot_ref[...], down, NT) * slope_ref[...].astype(F32)).astype(BF16)
    dub_ref[...] = jnp.sum(d_upper.astype(F32), axis=0, keepdims=True)
    length = d_upper.shape[0]
    rows = min(1024, length)

    def add(start):
        part = dot(d_upper[start : start + rows], up, NT)

        @pl.when(step == 0)
        def _():
            dh_sum[start : start + rows] = part

        @pl.when(step > 0)
        def _():
            dh_sum[start : start + rows] += part

    for start in range(0, length, rows):
        add(start)

    rows = ht_ref.shape[0] // chips
    many = max(1, 256 // rows)
    for start in range(0, chips, many):
        grad = dot(ht_ref[start * rows : (start + many) * rows], d_upper).astype(BF16)
        for chip in range(many):
            spot = jnp.bitwise_xor(jnp.int32(start + chip), place[1])
            grad_ref[spot] = grad[chip * rows : (chip + 1) * rows]

    @pl.when(step == pl.num_programs(0) - 1)
    def _():
        dh_ref[...] = dh_sum[...].astype(BF16)


def feed_back(place, hidden_t, cotangent, slope, down_weight, up_arrays, up_blocks, group, chips):
    width, length = hidden_t.shape
    ff = slope.shape[1]
    chunk = ff // chips
    tile = min(512 if length <= 1024 else 128, ff)
    parts = tile // chunk
    number, specs = up_blocks(tile)
    return call(
        functools.partial(feed_back_kernel, number, chips),
        "feed_back",
        place,
        (hidden_t, cotangent, slope, down_weight.reshape(chips, group, chunk, width)) + (up_arrays,) * number,
        (ff // tile,),
        [
            pl.BlockSpec((width, length), lambda t, s: (0, 0), pipeline_mode=pl.Buffered(1)),
            pl.BlockSpec((length, width), lambda t, s: (0, 0), pipeline_mode=pl.Buffered(1)),
            pl.BlockSpec((length, tile), lambda t, s: (0, t)),
            pl.BlockSpec((parts, 1, chunk, width), lambda t, s: (t, s[0], 0, 0)),
        ]
        + specs,
        [
            ((length, width), BF16, pl.BlockSpec((length, width), lambda t, s: (0, 0))),
            ((chips, width // chips, ff), BF16, pl.BlockSpec((chips, width // chips, tile), lambda t, s: (0, 0, t))),
            ((1, ff), F32, pl.BlockSpec((1, tile), lambda t, s: (0, t))),
        ],
        [pltpu.VMEM((length, width), F32)],
        flops=6 * length * width * ff,
        moved=6 * width * ff + 2 * length * ff + 6 * length * width,
    )


def feed_down_kernel(place, active_ref, down_ref, out_ref):
    down = down_ref[...]
    down = down.reshape(down.shape[0] * down.shape[2], down.shape[3])
    out_ref[...] = dot(active_ref[...], down).astype(BF16)


def feed_down(place, active, down_weight, group, chips):
    length, ff = active.shape
    width = down_weight.shape[1]
    chunk = ff // chips
    rows = min(512, length)
    return call(
        feed_down_kernel,
        "feed_down",
        place,
        (active, down_weight.reshape(chips, group, chunk, width)),
        (length // rows,),
        [
            pl.BlockSpec((rows, ff), lambda i, s: (i, 0)),
            pl.BlockSpec((chips, 1, chunk, width), lambda i, s: (0, s[0], 0, 0)),
        ],
        [((length, width), BF16, pl.BlockSpec((rows, width), lambda i, s: (i, 0)))],
        flops=2 * length * width * ff,
        moved=2 * (length * ff + width * ff + length * width),
    )[0]


def middle_back_kernel(group, place, middle_ref, cot_ref, gain_ref, weight_ref, *refs):
    part_refs = refs[:group]
    branch_ref, d_middle_ref, d_mixed_ref, sums_ref = refs[group:]
    d_hidden = part_refs[0][...].astype(F32)
    for ref in part_refs[1:]:
        d_hidden = d_hidden + ref[...].astype(F32)
    normal, inverse = norm_parts(middle_ref[...])
    d_middle = cot_ref[...].astype(F32) + norm_back(d_hidden, normal, inverse, gain_ref[...].astype(F32))
    branch = d_middle.astype(BF16)
    branch_ref[...] = branch
    d_middle_ref[...] = d_middle
    d_mixed_ref[...] = dot(branch, weight_ref[...], NT).astype(BF16)
    sums = jnp.concatenate(
        [
            jnp.sum(d_hidden * normal, axis=0, keepdims=True),
            jnp.sum(d_hidden, axis=0, keepdims=True),
            jnp.sum(branch.astype(F32), axis=0, keepdims=True),
            jnp.zeros((5, branch.shape[1]), F32),
        ],
        axis=0,
    )

    @pl.when(pl.program_id(0) == 0)
    def _():
        sums_ref[...] = sums

    @pl.when(pl.program_id(0) > 0)
    def _():
        sums_ref[...] += sums


def middle_back(place, middle, cotangent, gain, out_weight, parts):
    length, width = middle.shape
    group = len(parts)
    own = width // group
    rows = min(256, length)
    row = pl.BlockSpec((rows, width), lambda i, s: (i, 0))
    return call(
        functools.partial(middle_back_kernel, group),
        "middle_back",
        place,
        (middle, cotangent, gain.reshape(1, width), out_weight) + tuple(parts),
        (length // rows,),
        [
            row,
            row,
            pl.BlockSpec((1, width), lambda i, s: (0, 0)),
            pl.BlockSpec((own, width), lambda i, s: (s[0], 0)),
        ]
        + [row] * group,
        [
            ((length, width), BF16, row),
            ((length, width), F32, row),
            ((length, own), BF16, pl.BlockSpec((rows, own), lambda i, s: (i, 0))),
            ((8, width), F32, pl.BlockSpec((8, width), lambda i, s: (0, 0))),
        ],
        flops=2 * length * width * own,
        moved=length * width * (12 + 2 * group),
    )


def out_grad_kernel(group, chips, place, branch_ref, *refs):
    mixed_refs = refs[:group]
    grad_ref = refs[group]
    branch = branch_ref[...]
    share = chips // group
    for steps in range(group):
        owner = (place[0] + group - steps) % group
        grad = dot(mixed_refs[steps][...], branch, TN).astype(BF16)
        rows = grad.shape[0] // share
        for chip in range(share):
            spot = jnp.bitwise_xor(owner * share + chip, place[1])
            grad_ref[spot] = grad[chip * rows : (chip + 1) * rows]


def out_grad(place, branch, mixed_parts, chips):
    length, width = branch.shape
    group = len(mixed_parts)
    own = width // group
    return call(
        functools.partial(out_grad_kernel, group, chips),
        "out_grad",
        place,
        (branch,) + tuple(mixed_parts),
        (1,),
        [pl.BlockSpec((length, own), lambda i, s: (0, s[0]))]
        + [pl.BlockSpec((length, own), lambda i, s: (0, 0))] * group,
        [
            (
                (chips, width // chips, own),
                BF16,
                pl.BlockSpec((chips, width // chips, own), lambda i, s: (0, 0, 0)),
            )
        ],
        flops=2 * length * width * own,
        moved=4 * length * width,
    )[0]


def qkv_grad_kernel(chips, place, ht_ref, *refs):
    grad_ref = refs[-1]
    side = jnp.concatenate([ref[...] for ref in refs[:-1]], axis=1)
    rows = ht_ref.shape[0] // chips
    many = max(1, 256 // rows)
    for start in range(0, chips, many):
        grad = dot(ht_ref[start * rows : (start + many) * rows], side).astype(BF16)
        for chip in range(many):
            spot = jnp.bitwise_xor(jnp.int32(start + chip), place[1])
            grad_ref[spot] = grad[chip * rows : (chip + 1) * rows]


def qkv_grad(place, hidden_t, pieces, chips):
    width, length = hidden_t.shape
    columns = len(pieces) * PAIR
    return call(
        functools.partial(qkv_grad_kernel, chips),
        "qkv_grad",
        place,
        (hidden_t,) + tuple(pieces),
        (1,),
        [pl.BlockSpec((width, length), lambda i, s: (0, 0))]
        + [pl.BlockSpec((length, PAIR), lambda i, s: (0, 0))] * len(pieces),
        [
            (
                (chips, width // chips, columns),
                BF16,
                pl.BlockSpec((chips, width // chips, columns), lambda i, s: (0, 0, 0)),
            )
        ],
        flops=2 * length * width * columns,
        moved=2 * length * (width + columns) + 2 * width * columns,
    )[0]


def hidden_back_kernel(count, place, wq_ref, wk_ref, wv_ref, *refs):
    out_ref = refs[-1]
    total = None
    for index, weight_ref in enumerate((wq_ref, wk_ref, wv_ref)):
        pieces = [ref[...] for ref in refs[index * count : (index + 1) * count]]
        side = jnp.concatenate(pieces, axis=1) if count > 1 else pieces[0]
        part = dot(side, weight_ref[...], NT)
        total = part if total is None else total + part
    out_ref[...] = total.astype(BF16)


def hidden_back(place, pieces, qkv_weight, group):
    length = pieces[0].shape[0]
    width = qkv_weight.shape[0]
    own = width // group
    count = own // PAIR
    rows = min(512, length)
    weights = [
        pl.BlockSpec((width, own), functools.partial(lambda t, i, s: (0, t * group + s[0]), t))
        for t in range(3)
    ]
    return call(
        functools.partial(hidden_back_kernel, count),
        "hidden_back",
        place,
        (qkv_weight,) * 3 + tuple(pieces),
        (length // rows,),
        weights + [pl.BlockSpec((rows, PAIR), lambda i, s: (i, 0))] * len(pieces),
        [((length, width), BF16, pl.BlockSpec((rows, width), lambda i, s: (i, 0)))],
        flops=6 * length * width * own,
        moved=2 * (3 * width * own + 3 * length * own + length * width),
    )[0]


def body(
    inputs,
    cotangent,
    image_lengths,
    norm1_gain,
    norm1_bias,
    qkv_weight,
    qv_bias,
    out_weight,
    out_bias,
    norm2_gain,
    norm2_bias,
    up_weight,
    up_bias,
    down_weight,
    down_bias,
):
    rows, width = inputs.shape[2:]
    limit = image_lengths.shape[-1]
    ff = up_weight.shape[1]
    dp_size = lax.axis_size("dp")
    ctx_size = lax.axis_size("ctx")
    group = ctx_size // 2
    dp_index = lax.axis_index("dp")
    ctx_index = lax.axis_index("ctx")
    half = ctx_index // group
    member = ctx_index % group
    length = rows * ctx_size
    chips = dp_size * 2
    dp_bits = dp_size.bit_length() - 1
    own_width = width // group
    own_ff = ff // group
    chunk = own_ff // chips
    place = jnp.stack([member, dp_index * 2 + half]).astype(jnp.int32)

    def across(value):
        pairs = [(i, (i + group) % ctx_size) for i in range(ctx_size)]
        return lax.ppermute(value, "ctx", pairs)

    def around(value, steps):
        pairs = [
            (h * group + g, h * group + (g + steps) % group) for h in range(2) for g in range(group)
        ]
        return lax.ppermute(value, "ctx", pairs)

    def all_around(value):
        return [value] + [around(value, steps) for steps in range(1, group)]

    def in_order(parts, axis=0):
        if group == 2:
            first = member == 0
            return jnp.stack(
                [jnp.where(first, parts[0], parts[1]), jnp.where(first, parts[1], parts[0])], axis=axis
            )
        return jnp.roll(jnp.stack(parts[::-1], axis=axis), member + 1, axis=axis)

    def gather(value):
        return in_order(all_around(value))

    def pick(value, index, axis):
        return lax.dynamic_index_in_dim(value, index, axis, keepdims=False)

    def group_sum_scatter(value, axis):
        total = pick(value, member, axis).astype(F32)
        for steps in range(1, group):
            total = total + around(pick(value, (member + steps) % group, axis), steps).astype(F32)
        return total

    def swap_bit(value, bit):
        if bit < 0:
            return across(value)
        return lax.ppermute(value, "dp", [(i, i ^ (1 << bit)) for i in range(dp_size)])

    def chip_scatter(value, order, dtype=BF16):
        value = value.reshape((2,) * (dp_bits + 1) + value.shape[1:])
        left = list(range(dp_bits - 1, -1, -1)) + [-1]
        for number, bit in enumerate(order):
            axis = left.index(bit)
            keep = lax.index_in_dim(value, 0, axis, keepdims=False)
            send = lax.index_in_dim(value, 1, axis, keepdims=False)
            left.pop(axis)
            value = keep.astype(F32) + swap_bit(send, bit).astype(F32)
            if number < len(order) - 1:
                value = value.astype(dtype)
        return value

    order_a = [0] + list(range(1, dp_bits)) + [-1]
    order_b = [-1, 0] + list(range(1, dp_bits))

    def spread(value, cut):
        if cut == 0 or cut == value.shape[2]:
            return chip_scatter(value, order_a)
        return jnp.concatenate(
            [chip_scatter(value[:, :, :cut], order_a), chip_scatter(value[:, :, cut:], order_b)], axis=-1
        )

    def cut_of(columns):
        return columns // 2 // 128 * 128

    own_inputs = pick(inputs, half, 0)[0]
    other_inputs = across(pick(inputs, 1 - half, 0)[0])
    own_cot = pick(cotangent, half, 0)[0]
    other_cot = across(pick(cotangent, 1 - half, 0)[0])
    x_rows = jnp.concatenate([gather(own_inputs), gather(other_inputs)]).reshape(length, width)
    cot_rows = jnp.concatenate([gather(own_cot), gather(other_cot)]).reshape(length, width)

    spots = jnp.arange(length, dtype=jnp.int32).reshape(2, length // 2)
    positions = jnp.where(half == 0, spots, spots[::-1]).reshape(length)
    ends = jnp.cumsum(pick(image_lengths, half, 0)[0])
    segment = jnp.sum((positions[:, None] >= ends[None, :]).astype(jnp.int32), axis=1)
    seg_row = segment.reshape(1, length)
    seg_cols = jnp.broadcast_to(segment[:, None], (length, PAIR))

    if chunk % 128 == 0:
        up_arrays = up_weight

        def up_blocks(tile):
            return tile // chunk, up_specs(width, tile, chunk, group, tile // chunk)

    else:
        up_arrays = pick(up_weight.reshape(width, chips, group, chunk), member, 2).reshape(width, own_ff)

        def up_blocks(tile):
            return 1, [pl.BlockSpec((width, tile), lambda t, s: (0, t))]

    upb_own = pick(up_bias.reshape(chips, group, chunk), member, 1).reshape(1, own_ff)

    hidden1_t, query, keys, values = project(place, x_rows, norm1_gain, norm1_bias, qkv_weight, qv_bias, group)
    mixed, logs = attend(place, query, keys, values, seg_cols, seg_row, limit)
    mixed_parts = all_around(mixed)
    middle, hidden2, hidden2_t = close(place, x_rows, mixed_parts, out_weight, out_bias, norm2_gain, norm2_bias)
    active, slope, down_part = feed_up(place, hidden2, cot_rows, up_arrays, up_blocks, upb_own, chips)
    down_total = spread(down_part, cut_of(width))
    dh_part, up_part, upb_grad = feed_back(
        place, hidden2_t, cot_rows, slope, down_weight, up_arrays, up_blocks, group, chips
    )
    up_total = spread(up_part, cut_of(own_ff))

    branch, d_middle, d_mixed, sums = middle_back(
        place, middle, cot_rows, norm2_gain, out_weight, all_around(dh_part)
    )
    out_total = chip_scatter(out_grad(place, branch, mixed_parts, chips), order_a)
    pairs = own_width // PAIR
    triples = [
        attend_back(place, p, query, keys, values, d_mixed, mixed, logs, seg_cols, seg_row, limit)
        for p in range(pairs)
    ]
    at_once = min(2, pairs)
    qkv_totals = []
    for start in range(0, pairs, at_once):
        pieces = [triples[p][t] for t in range(3) for p in range(start, start + at_once)]
        part = qkv_grad(place, hidden1_t, pieces, chips)
        qkv_totals.append(spread(part, cut_of(part.shape[2])))
    dh1_part = hidden_back(
        place, [triples[p][t] for t in range(3) for p in range(pairs)], qkv_weight, group
    )
    own_rows = (2, group, rows, width)
    d_hidden1 = group_sum_scatter(dh1_part.reshape(own_rows), 1)
    x_own = pick(x_rows.reshape(own_rows), member, 1).astype(F32)
    n1_own, i1_own = norm_parts(x_own)
    d_middle_own = pick(d_middle.reshape(own_rows), member, 1)
    input_own = (d_middle_own + norm_back(d_hidden1, n1_own, i1_own, norm1_gain)).astype(BF16)

    out_part = feed_down(place, active, down_weight, group, chips)
    out_sum = group_sum_scatter(out_part.reshape(own_rows), 1)
    middle_own = pick(middle.reshape(own_rows), member, 1)
    result = (out_sum + middle_own + down_bias).astype(BF16)

    def hand_back(value):
        came = across(value[1])
        first = half == 0
        return jnp.stack([jnp.where(first, value[0], came), jnp.where(first, came, value[0])])[:, None]

    block_output = hand_back(result)
    input_grad = hand_back(input_own)

    both = 1.0 / group
    member_is = (jnp.arange(group, dtype=jnp.int32) == member).astype(F32)

    def at_member(pieces):
        vector = jnp.concatenate([jnp.sum(piece.astype(F32), axis=0) for piece in pieces])
        return (member_is[:, None] * vector[None, :]).reshape(-1)

    upb_full = (member_is[None, :, None] * upb_grad.reshape(chips, 1, chunk)).reshape(chips, group, chunk)
    vectors = [
        jnp.sum(d_hidden1 * n1_own, axis=(0, 1)),
        jnp.sum(d_hidden1, axis=(0, 1)),
        at_member([triple[0] for triple in triples]),
        at_member([triple[2] for triple in triples]),
        sums[2] * both,
        sums[0] * both,
        sums[1] * both,
        jnp.sum(cotangent[:, 0].astype(F32), axis=(0, 1)),
    ]
    own = width // (chips * group)
    small = jnp.stack(vectors).reshape(len(vectors), chips, group, own)
    small = jnp.transpose(small, (1, 2, 0, 3)).reshape(chips, group, -1)
    small = jnp.concatenate([small, upb_full], axis=-1)
    small = jnp.take(small, jnp.bitwise_xor(jnp.arange(chips, dtype=jnp.int32), place[1]), axis=0)
    small = chip_scatter(small, order_a, F32)
    small = group_sum_scatter(small, 0)
    small_rows = small[: len(vectors) * own].reshape(len(vectors), own)
    upb_out = small[len(vectors) * own :]

    def exchange(value):
        value = value.reshape(group, own, value.shape[1])
        parts = [pick(value, member, 0)] + [
            around(pick(value, (member + steps) % group, 0).astype(BF16), steps).astype(F32)
            for steps in range(1, group)
        ]
        return in_order(parts, 1)

    up_out = exchange(up_total).reshape(own, group, chips, chunk)
    up_out = jnp.swapaxes(up_out, 1, 2).reshape(own, ff)
    rest = exchange(jnp.concatenate([out_total] + qkv_totals, axis=1))
    out_out = rest[:, :, :own_width].reshape(own, width)
    qkv_out = rest[:, :, own_width:].reshape(own, group, pairs // at_once, 3, at_once * PAIR)
    qkv_out = jnp.transpose(qkv_out, (0, 3, 1, 2, 4)).reshape(own, 3 * width)
    return (
        block_output,
        input_grad,
        small_rows[0],
        small_rows[1],
        qkv_out,
        small_rows[2:4],
        out_out,
        small_rows[4],
        small_rows[5],
        small_rows[6],
        up_out,
        upb_out,
        down_total,
        small_rows[7],
    )


def solution(mesh):
    split = P(None, "dp", "ctx", None)
    both = ("dp", "ctx")
    return jax.shard_map(
        body,
        mesh=mesh,
        in_specs=(split, split, P(None, "dp", None)) + (P(),) * 12,
        out_specs=(
            split,
            split,
            P(both),
            P(both),
            P(both, None),
            P(None, both),
            P(both, None),
            P(both),
            P(both),
            P(both),
            P(both, None),
            P(both),
            P(both, None),
            P(both),
        ),
        check_vma=False,
    )
```

```python
import functools

import jax
import jax.numpy as jnp
from jax import lax
from jax.experimental import pallas as pl
from jax.experimental.pallas import tpu as pltpu
from jax.sharding import PartitionSpec as P

HEADS = 16
HEAD_DIM = 64
PAIR = 2 * HEAD_DIM
NEG = -1e30
EPS = 1e-06
LOG2E = 1.4426950408889634
SCALE = HEAD_DIM ** (-0.5)
BF16 = jnp.bfloat16
F32 = jnp.float32
VMEM = 60 * 1024 * 1024
LESS_VMEM = 32 * 1024 * 1024
DH_PIECES = 4

NT = (((1,), (1,)), ((), ()))
NN = (((1,), (0,)), ((), ()))
TN = (((0,), (0,)), ((), ()))


def dot(left, right, dims=NN):
    return lax.dot_general(left, right, dims, preferred_element_type=F32)


def call(kernel, name, place, args, grid, in_specs, outs, scratch=(), after=(), fill=(), vmem=LESS_VMEM):
    known = len(args)
    skipped = len(after) + len(fill)
    stays = [len(out) > 3 and bool(out[3]) for out in outs]

    def settled(array):
        pinned = any(array is other for other in place.pinned)
        return pltpu.with_memory_space_constraint(array, pltpu.VMEM if pinned else pltpu.HBM)

    def inner(place_ref, *refs):
        kernel(place_ref, *refs[:known], *refs[known + skipped :])

    anywhere = pl.BlockSpec(memory_space=pl.ANY)
    first = 1 + known + len(after)
    results = pl.pallas_call(
        inner,
        grid_spec=pltpu.PrefetchScalarGridSpec(
            num_scalar_prefetch=1,
            grid=grid,
            in_specs=list(in_specs) + [anywhere] * skipped,
            out_specs=[out[2] for out in outs],
            scratch_shapes=list(scratch),
        ),
        out_shape=[(pltpu.VMEM if stay else pltpu.HBM)(out[0], out[1]) for out, stay in zip(outs, stays)],
        input_output_aliases={first + index: index for index in range(len(fill))},
        compiler_params=pltpu.CompilerParams(vmem_limit_bytes=vmem),
        cost_estimate=pl.CostEstimate(flops=int(2*1.15e9) if name=="step" else 0, bytes_accessed=0, transcendentals=0),
        name=name,
    )(place.numbers, *[settled(array) for array in (*args, *after, *fill)])
    place.pinned += [array for array, stay in zip(results, stays) if stay]
    return results


class Place:
    def __init__(self, numbers):
        self.numbers = numbers
        self.pinned = []


def without_bit(number, spot):
    return ((number >> (spot + 1)) << spot) | (number & ((1 << spot) - 1))


def deal(stage_ref, me, pieces):
    for relative in range(stage_ref.shape[0]):
        rows = stage_ref[jnp.bitwise_xor(jnp.int32(relative), me)]
        for keep_ref, send_ref, bit, columns in pieces:
            target = send_ref if (relative >> bit) & 1 else keep_ref
            target[without_bit(relative, bit)] = rows[:, columns]


def norm_parts(values):
    centred = values - jnp.mean(values, axis=-1, keepdims=True)
    inverse = lax.rsqrt(jnp.mean(centred * centred, axis=-1, keepdims=True) + EPS)
    return centred * inverse, inverse


def norm_back(grad, normal, inverse, gain):
    scaled = grad * gain
    inner = (
        scaled
        - jnp.mean(scaled, axis=-1, keepdims=True)
        - normal * jnp.mean(scaled * normal, axis=-1, keepdims=True)
    )
    return inverse * inner


def step_kernel(jobs, place, *refs):
    ins = sum(len(layout) for _, layout in jobs) * 2
    sources = refs[:ins]
    targets = refs[ins:]
    for job, (spot, layout) in enumerate(jobs):
        keep_ref, send_ref = targets[2 * job : 2 * job + 2]
        columns = keep_ref.shape[2]
        base = 0
        for rows, width in layout:
            old_ref, came_ref = sources[:2]
            sources = sources[2:]
            for number in range(old_ref.shape[0]):
                value = (old_ref[number].astype(F32) + came_ref[number].astype(F32)).astype(keep_ref.dtype)
                target = send_ref if (number >> spot) & 1 else keep_ref
                spare = without_bit(number, spot)
                for part in range(width // columns):
                    start = base + part * rows
                    target[spare, start : start + rows] = value[:, part * columns : (part + 1) * columns]
            base += rows * (width // columns)


def step_call(place, jobs, after=()):
    ins = []
    outs = []
    layouts = []
    for arrays, spot in jobs:
        columns = min(array.shape[2] for array in arrays)
        layout = [array.shape[1:] for array in arrays[::2]]
        rows = sum(rows * (width // columns) for rows, width in layout)
        shape = (arrays[0].shape[0] // 2, rows, columns)
        layouts.append((spot, layout))
        ins += arrays
        outs += [(shape, arrays[0].dtype, pl.BlockSpec(shape, lambda i, s: (0, 0, 0)))] * 2
    return call(
        functools.partial(step_kernel, layouts),
        "step",
        place,
        tuple(ins),
        (1,),
        [pl.BlockSpec(array.shape, lambda i, s: (0, 0, 0)) for array in ins],
        outs,
        after=after,
    )


def hand_out(stage_ref, member, value, out_refs, start=0):
    group = len(out_refs)
    rows = stage_ref.shape[1]
    stage_ref[...] = value.reshape(stage_ref.shape)
    for steps, out_ref in enumerate(out_refs):
        for block in range(stage_ref.shape[0] // group):
            out_ref[start + block * rows : start + (block + 1) * rows] = stage_ref[
                block * group + (member + steps) % group
            ]


def project_kernel(group, copies, place, *refs):
    part_refs = refs[:group]
    vec_ref, wq_ref, wk_ref, wv_ref, qvb_ref = refs[group : group + 5]
    refs = refs[group + 5 :]
    if copies:
        refs[-2][...] = refs[0][...].reshape(refs[-2].shape)
        refs[-1][...] = refs[1][...].reshape(refs[-1].shape)
        refs = refs[2:-2]
    x_ref, ht_ref, q_ref, k_ref, v_ref = refs
    gain = vec_ref[0:1]
    shift = vec_ref[1:2]
    qvb = qvb_ref[...].astype(F32)
    rows = part_refs[0].shape[0]
    for steps, part_ref in enumerate(part_refs):
        base = ((place[0] + group - steps) % group) * rows
        spot = pl.ds(pl.multiple_of(base, rows), rows)
        values = part_ref[...]
        x_ref[spot] = values
        normal, _ = norm_parts(values.astype(F32))
        hidden = (normal * gain + shift).astype(BF16)
        ht_ref[:, spot] = hidden.T
        q_ref[spot] = (dot(hidden, wq_ref[...]) + qvb[0:1]).astype(BF16)
        k_ref[spot] = dot(hidden, wk_ref[...]).astype(BF16)
        v_ref[spot] = (dot(hidden, wv_ref[...]) + qvb[1:2]).astype(BF16)


def project(place, parts, first_row, length, vectors, qkv_weight, qv_bias, fill, copied=None):
    group = len(parts)
    rows, width = parts[0].shape
    own = width // group
    rows = rows * group
    index = first_row // rows
    extra = ()
    extra_in = []
    extra_out = []
    if copied is not None:
        shape = copied.shape[2:]
        extra = (copied, copied)
        extra_in = [
            pl.BlockSpec((1, 1) + shape, lambda i, s: (s[1] % 2, 0, 0, 0)),
            pl.BlockSpec((1, 1) + shape, lambda i, s: (1 - s[1] % 2, 0, 0, 0)),
        ]
        extra_out = [(shape, BF16, pl.BlockSpec(shape, lambda i, s: (0, 0)))] * 2
    vector = pl.BlockSpec((8, width), lambda i, s: (0, 0))
    part = pl.BlockSpec((rows // group, width), lambda i, s: (0, 0))
    row = pl.BlockSpec((rows, own), lambda i, s: (index, 0))
    weights = [
        pl.BlockSpec((width, own), functools.partial(lambda t, i, s: (0, t * group + s[0]), t))
        for t in range(3)
    ]
    return call(
        functools.partial(project_kernel, group, copied is not None),
        "project",
        place,
        tuple(parts) + (vectors, qkv_weight, qkv_weight, qkv_weight, qv_bias) + extra,
        (1,),
        [part] * group
        + [vector]
        + weights
        + [pl.BlockSpec((2, own), lambda i, s: (0, s[0]))]
        + extra_in,
        [
            ((length, width), BF16, pl.BlockSpec((rows, width), lambda i, s: (index, 0))),
            ((width, length), BF16, pl.BlockSpec((width, rows), lambda i, s: (0, index))),
        ]
        + [((length, own), BF16, row)] * 3
        + extra_out,
        fill=fill,
    )


def attend_kernel(limit, sub, place, q_ref, k_ref, v_ref, segc_ref, segr_ref, mixed_ref, lse_ref):
    keys = k_ref[...]
    keys = jnp.concatenate([keys, keys], axis=1)
    values = v_ref[...]
    values = jnp.concatenate([values, jnp.ones(values.shape, BF16)], axis=1)
    lane = lax.broadcasted_iota(jnp.int32, (sub, PAIR), 1)
    zero = jnp.zeros((), BF16)
    segr = segr_ref[...]
    for start in range(0, q_ref.shape[0], sub):
        part = pl.ds(start, sub)
        scaled = q_ref[part].astype(F32) * (SCALE * LOG2E)
        high = scaled.astype(BF16)
        low = (scaled - high.astype(F32)).astype(BF16)
        segc = segc_ref[part]
        valid = segc < limit
        bias = jnp.where(jnp.where(valid, segc, -1)[:, :1] == segr, 0.0, NEG)
        mixed = []
        logs = []
        for head in range(2):
            own = (lane < HEAD_DIM) == (head == 0)
            query = jnp.concatenate([jnp.where(own, high, zero), jnp.where(own, low, zero)], axis=1)
            scores = dot(query, keys, NT) + bias
            largest = jnp.max(scores, axis=1, keepdims=True)
            weights = jnp.exp2(scores - largest).astype(BF16)
            summed = dot(weights, values)
            total = summed[:, PAIR:]
            mixed.append(summed[:, :PAIR] / total)
            logs.append(largest + jnp.log2(total))
        first = lane < HEAD_DIM
        mixed_ref[part] = jnp.where(valid, jnp.where(first, mixed[0], mixed[1]), 0.0).astype(BF16)
        lse_ref[part] = jnp.where(valid, jnp.where(first, logs[0], logs[1]), 0.0)


def attend(place, first, count, query, keys, values, seg_cols, seg_row, limit, after=()):
    length = query.shape[0]
    width = count * PAIR
    block = min(1024, length)
    tile = pl.BlockSpec((block, PAIR), lambda p, j, s: (j, first + p))
    whole = pl.BlockSpec((length, PAIR), lambda p, j, s: (0, first + p))
    out_tile = pl.BlockSpec((block, PAIR), lambda p, j, s: (j, p))
    return call(
        functools.partial(attend_kernel, limit, min(256, block)),
        "attend",
        place,
        (query, keys, values, seg_cols, seg_row),
        (width // PAIR, length // block),
        [
            tile,
            whole,
            whole,
            pl.BlockSpec((block, PAIR), lambda p, j, s: (j, 0)),
            pl.BlockSpec((1, length), lambda p, j, s: (0, 0)),
        ],
        [((length, width), BF16, out_tile), ((length, width), F32, out_tile)],
        after=after,
        vmem=LESS_VMEM if length <= 1024 else VMEM,
    )


def attend_back_kernel(
    limit,
    sub,
    place,
    q_ref,
    k_ref,
    v_ref,
    do_ref,
    mixed_ref,
    lse_ref,
    segc_ref,
    segr_ref,
    dq_ref,
    dk_ref,
    dv_ref,
    kt_ref,
    dk_sum,
    dv_sum,
):
    step = pl.program_id(1)
    steps = pl.num_programs(1)
    length = k_ref.shape[0]
    keys = k_ref[...]
    kt_ref[...] = keys.T
    zero = jnp.zeros((), BF16)
    minus = -jnp.ones((), BF16)
    values = v_ref[...]
    key_lane = lax.broadcasted_iota(jnp.int32, (length, PAIR), 1)
    lane = lax.broadcasted_iota(jnp.int32, (sub, PAIR), 1)
    spot = lane & (HEAD_DIM - 1)
    ones = jnp.where((key_lane & (HEAD_DIM - 1)) < 3, minus, zero)
    key_sides = []
    value_sides = []
    for head in range(2):
        own = (key_lane < HEAD_DIM) == (head == 0)
        key_sides.append(jnp.concatenate([jnp.where(own, keys, ones), keys], axis=1))
        value_sides.append(jnp.where(own, values, ones))
    segc = segc_ref[...]
    segc = jnp.where(segc < limit, segc, -1)[:, :1]

    def in_three(value):
        high = value.astype(BF16)
        rest = value - high.astype(F32)
        middle = rest.astype(BF16)
        low = (rest - middle.astype(F32)).astype(BF16)
        return jnp.where(spot == 0, high, jnp.where(spot == 1, middle, jnp.where(spot == 2, low, zero)))

    dk_all = dv_all = None
    for start in range(0, q_ref.shape[0], sub):
        part = pl.ds(start, sub)
        query = q_ref[part]
        scaled = query.astype(F32) * (SCALE * LOG2E)
        high = scaled.astype(BF16)
        low = (scaled - high.astype(F32)).astype(BF16)
        grad = do_ref[part]
        product = grad.astype(F32) * mixed_ref[part].astype(F32)
        logs = lse_ref[part]
        same = segc == segr_ref[:, part]
        dq_rows = []
        for head in range(2):
            own = (lane < HEAD_DIM) == (head == 0)
            log = jnp.broadcast_to(logs[:, head * HEAD_DIM : head * HEAD_DIM + 1], logs.shape)
            delta = jnp.sum(jnp.where(own, product, 0.0), axis=1, keepdims=True)
            delta = jnp.broadcast_to(delta, logs.shape)
            query_side = jnp.concatenate(
                [jnp.where(own, high, in_three(log)), jnp.where(own, low, zero)], axis=1
            )
            grad_side = jnp.where(own, grad, in_three(delta))
            scores = dot(key_sides[head], query_side, NT)
            probs = jnp.where(same, jnp.exp2(scores), 0.0).astype(BF16)
            d_probs = dot(value_sides[head], grad_side, NT)
            d_scores = probs * d_probs.astype(BF16)
            dv_part = dot(probs, jnp.where(own, grad, zero))
            dk_part = dot(d_scores, jnp.where(own, query, zero))
            dv_all = dv_part if dv_all is None else dv_all + dv_part
            dk_all = dk_part if dk_all is None else dk_all + dk_part
            dq_rows.append(dot(kt_ref[head * HEAD_DIM : (head + 1) * HEAD_DIM], d_scores))
        dq_ref[part] = (jnp.concatenate(dq_rows, axis=0).T * SCALE).astype(BF16)
    dk_all = dk_all * SCALE

    @pl.when(step == 0)
    def _():
        dk_sum[...] = dk_all
        dv_sum[...] = dv_all

    @pl.when(step > 0)
    def _():
        dk_sum[...] += dk_all
        dv_sum[...] += dv_all

    @pl.when(step == steps - 1)
    def _():
        dk_ref[...] = dk_sum[...].astype(BF16)
        dv_ref[...] = dv_sum[...].astype(BF16)


def attend_back(
    place, first, query, keys, values, d_mixed, mixed, logs, seg_cols, seg_row, limit, after=()
):
    length, width = mixed.shape
    block = min(1024, length)
    tile = pl.BlockSpec((block, PAIR), lambda p, j, s: (j, first + p))
    whole = pl.BlockSpec((length, PAIR), lambda p, j, s: (0, first + p))
    out_tile = pl.BlockSpec((block, PAIR), lambda p, j, s: (j, p))
    out_whole = pl.BlockSpec((length, PAIR), lambda p, j, s: (0, p))
    return call(
        functools.partial(attend_back_kernel, limit, min(256, block)),
        "attend_back",
        place,
        (query, keys, values, d_mixed, mixed, logs, seg_cols, seg_row),
        (width // PAIR, length // block),
        [
            tile,
            whole,
            whole,
            tile,
            out_tile,
            out_tile,
            pl.BlockSpec((length, PAIR), lambda p, j, s: (0, 0)),
            pl.BlockSpec((1, block), lambda p, j, s: (0, j)),
        ],
        [
            ((length, width), BF16, out_tile),
            ((length, width), BF16, out_whole),
            ((length, width), BF16, out_whole),
        ],
        [pltpu.VMEM((PAIR, length), BF16), pltpu.VMEM((length, PAIR), F32), pltpu.VMEM((length, PAIR), F32)],
        after=after,
        vmem=LESS_VMEM if length <= 1024 else VMEM,
    )


def collect_kernel(group, place, *refs):
    part_refs = refs[:-2]
    rows_ref, sums_ref = refs[-2:]
    count = part_refs[0].shape[0]
    total = None
    for index, part_ref in enumerate(part_refs):
        block, steps = index // group, index % group
        values = part_ref[...]
        spot = block * group + (place[0] + group - steps) % group
        rows_ref[pl.ds(pl.multiple_of(spot * count, count), count)] = values
        part = jnp.sum(values.astype(F32), axis=0, keepdims=True)
        total = part if total is None else total + part
    sums_ref[...] = jnp.concatenate([total, jnp.zeros((7, total.shape[1]), F32)], axis=0)


def collect(place, parts, group, after=()):
    rows, width = parts[0].shape
    length = rows * len(parts)
    whole = pl.BlockSpec((rows, width), lambda i, s: (0, 0))
    return call(
        functools.partial(collect_kernel, group),
        "collect",
        place,
        tuple(parts),
        (1,),
        [whole] * len(parts),
        [
            ((length, width), BF16, pl.BlockSpec((length, width), lambda i, s: (0, 0))),
            ((8, width), F32, pl.BlockSpec((8, width), lambda i, s: (0, 0))),
        ],
        after=after,
        vmem=LESS_VMEM if length <= 1024 else VMEM,
    )


def close_kernel(number, place, x_ref, vec_ref, *refs):
    mixed_refs = refs[:number]
    weight_refs = refs[number : 2 * number]
    middle_ref, own_ref, hidden_ref, ht_ref = refs[2 * number :]
    gain = vec_ref[2:3]
    shift = vec_ref[3:4]
    bias = vec_ref[4:5]
    sub = 256
    for start in range(0, x_ref.shape[0], sub):
        part = pl.ds(start, sub)
        middle = x_ref[part].astype(F32) + bias
        for mixed_ref, weight_ref in zip(mixed_refs, weight_refs):
            middle = middle + dot(mixed_ref[part], weight_ref[...])
        middle_ref[part] = middle
        normal, _ = norm_parts(middle)
        hidden = (normal * gain + shift).astype(BF16)
        hidden_ref[part] = hidden
        ht_ref[:, part] = hidden.T
    count = own_ref.shape[0]
    own_ref[...] = middle_ref[pl.ds(pl.multiple_of(place[0] * count, count), count)]


def close(place, x_rows, mixed_parts, group, out_weight, vectors, slice_rows, after=()):
    length, width = x_rows.shape
    calls = len(mixed_parts)
    number = calls * group
    own = width // number
    rows = slice_rows * group
    vector = pl.BlockSpec((8, width), lambda i, s: (0, 0))
    row = pl.BlockSpec((rows, width), lambda i, s: (i, 0))
    arrays = []
    weights = []
    for j in range(calls):
        for steps in range(group):
            arrays.append(mixed_parts[j][steps])
            weights.append(
                pl.BlockSpec(
                    (own, width),
                    functools.partial(lambda j, t, i, s: (((s[0] + group - t) % group) * calls + j, 0), j, steps),
                )
            )
    return call(
        functools.partial(close_kernel, number),
        "close",
        place,
        (x_rows, vectors)
        + tuple(arrays)
        + (out_weight,) * number,
        (length // rows,),
        [row, vector] + [pl.BlockSpec((rows, own), lambda i, s: (i, 0))] * number + weights,
        [
            ((length, width), F32, row),
            ((length // group, width), F32, pl.BlockSpec((slice_rows, width), lambda i, s: (i, 0))),
            ((length, width), BF16, row, length <= 1024),
            ((width, length), BF16, pl.BlockSpec((width, rows), lambda i, s: (0, i)), length <= 1024),
        ],
        after=after,
    )


def up_specs(width, tile, block, group, number):
    return [
        pl.BlockSpec((width, block), functools.partial(lambda n, t, s: (0, (t * number + n) * group + s[0]), n))
        for n in range(number)
    ]


def feed_up_kernel(number, group, cut, place, h_ref, cot_ref, upb_ref, *refs):
    up_refs = refs[:number]
    active_refs = refs[number : number + group]
    slope_ref, ka_ref, sa_ref, kb_ref, sb_ref, stage_ref, rows_ref = refs[number + group :]
    up = jnp.concatenate([ref[...] for ref in up_refs], axis=1) if number > 1 else up_refs[0][...]
    upper = dot(h_ref[...], up) + upb_ref[...].astype(F32)
    half = 0.5 + 0.5 * lax.erf(upper * 0.7071067811865476)
    bell = jnp.exp2(upper * upper * (-0.5 * LOG2E)) * 0.3989422804014327
    active = (upper * half).astype(BF16)
    hand_out(rows_ref, place[0], active, active_refs)
    slope_ref[...] = (half + upper * bell).astype(BF16)
    stage_ref[...] = dot(active, cot_ref[...], TN).astype(BF16).reshape(stage_ref.shape)
    deal(
        stage_ref,
        place[1] % stage_ref.shape[0],
        [(ka_ref, sa_ref, 1, slice(0, cut)), (kb_ref, sb_ref, 0, slice(cut, None))],
    )


def feed_up(place, hidden, cotangent, up_arrays, up_blocks, upb_own, group, chips, cut, rows, after=()):
    length, width = hidden.shape
    ff = upb_own.shape[1]
    chunk = ff // chips
    tile = min(512 if length <= 1024 else 128, ff)
    parts = tile // chunk
    whole = pl.BlockSpec((length, width), lambda t, s: (0, 0), pipeline_mode=pl.Buffered(1))
    tiled = pl.BlockSpec((length, tile), lambda t, s: (0, t))
    number, specs = up_blocks(tile)

    def piece(columns):
        spec = pl.BlockSpec(
            (parts // 2, chunk, columns), lambda t, s: (jnp.bitwise_xor(t, s[1] // parts), 0, 0)
        )
        return ((chips // 2, chunk, columns), BF16, spec)

    return call(
        functools.partial(feed_up_kernel, number, group, cut),
        "feed_up",
        place,
        (hidden, cotangent, upb_own) + (up_arrays,) * number,
        (ff // tile,),
        [whole, whole, pl.BlockSpec((1, tile), lambda t, s: (0, t))] + specs,
        [
            (
                (length // group, ff),
                BF16,
                pl.BlockSpec((length // group, tile), lambda t, s: (0, t)),
            )
        ]
        * group
        + [((length, ff), BF16, tiled, length <= 1024)]
        + [piece(cut)] * 2
        + [piece(width - cut)] * 2,
        [pltpu.VMEM((parts, chunk, width), BF16), pltpu.VMEM((length // rows, rows, tile), BF16)],
        after=after,
        vmem=LESS_VMEM if length <= 1024 else VMEM,
    )


def feed_back_kernel(number, chips, split, place, ht_ref, cot_ref, slope_ref, down_ref, *refs):
    up_refs = refs[:number]
    dh_refs = refs[number : number + DH_PIECES]
    dub_ref, ka_ref, sa_ref, kb_ref, sb_ref, dh_sum, stage_ref = refs[number + DH_PIECES :]
    step = pl.program_id(0)
    up = jnp.concatenate([ref[...] for ref in up_refs], axis=1) if number > 1 else up_refs[0][...]
    down = down_ref[...]
    down = down.reshape(down.shape[0] * down.shape[2], down.shape[3])
    d_upper = (dot(cot_ref[...], down, NT) * slope_ref[...].astype(F32)).astype(BF16)
    dub_ref[...] = jnp.sum(d_upper.astype(F32), axis=0, keepdims=True)
    length = d_upper.shape[0]
    rows = min(1024, length)

    def add(start):
        part = dot(d_upper[start : start + rows], up, NT)

        @pl.when(step == 0)
        def _():
            dh_sum[start : start + rows] = part

        @pl.when(step > 0)
        def _():
            dh_sum[start : start + rows] += part

    for start in range(0, length, rows):
        add(start)

    rows = ht_ref.shape[0] // chips
    many = max(1, 256 // rows)
    for start in range(0, chips, many):
        grad = dot(ht_ref[start * rows : (start + many) * rows], d_upper).astype(BF16)
        stage_ref[start : start + many] = grad.reshape(many, rows, grad.shape[1])

    @pl.when(step < split)
    def _():
        deal(stage_ref, place[1], [(ka_ref, sa_ref, 1, slice(None))])

    @pl.when(step >= split)
    def _():
        deal(stage_ref, place[1], [(kb_ref, sb_ref, 0, slice(None))])

    @pl.when(step == pl.num_programs(0) - 1)
    def _():
        piece_rows = dh_refs[0].shape[0]
        for index, dh_ref in enumerate(dh_refs):
            dh_ref[...] = dh_sum[index * piece_rows : (index + 1) * piece_rows].astype(BF16)


def feed_back(
    place, hidden_t, cotangent, slope, down_weight, up_arrays, up_blocks, group, chips, share, after=()
):
    width, length = hidden_t.shape
    ff = slope.shape[1]
    chunk = ff // chips
    tile = min(512 if length <= 1024 else 128, ff)
    parts = tile // chunk
    number, specs = up_blocks(tile)
    tiles = ff // tile
    split = max(1, min(tiles - 1, round(tiles * share)))
    some = width // chips

    def piece(first, last):
        spec = pl.BlockSpec(
            (chips // 2, some, tile), lambda t, s: (0, 0, jnp.clip(t, first, last - 1) - first)
        )
        return ((chips // 2, some, (last - first) * tile), BF16, spec)

    return call(
        functools.partial(feed_back_kernel, number, chips, split),
        "feed_back",
        place,
        (hidden_t, cotangent, slope, down_weight.reshape(chips, group, chunk, width)) + (up_arrays,) * number,
        (ff // tile,),
        [
            pl.BlockSpec((width, length), lambda t, s: (0, 0), pipeline_mode=pl.Buffered(1)),
            pl.BlockSpec((length, width), lambda t, s: (0, 0), pipeline_mode=pl.Buffered(1)),
            pl.BlockSpec((length, tile), lambda t, s: (0, t)),
            pl.BlockSpec((parts, 1, chunk, width), lambda t, s: (t, s[0], 0, 0)),
        ]
        + specs,
        [
            ((length // DH_PIECES, width), BF16, pl.BlockSpec((length // DH_PIECES, width), lambda t, s: (0, 0)))
        ]
        * DH_PIECES
        + [((1, ff), F32, pl.BlockSpec((1, tile), lambda t, s: (0, t)))]
        + [piece(0, split)] * 2
        + [piece(split, tiles)] * 2,
        [pltpu.VMEM((length, width), F32), pltpu.VMEM((chips, some, tile), BF16)],
        after=after,
        vmem=LESS_VMEM if length <= 1024 else VMEM,
    )


def feed_down_kernel(group, place, down_ref, middle_ref, vec_ref, *refs):
    active_refs = refs[:group]
    near_ref, far_ref, sum_ref = refs[group:]
    step = pl.program_id(0)
    total = None
    for steps, active_ref in enumerate(active_refs):
        down = down_ref[:, pl.ds((place[0] + group - steps) % group, 1)]
        part = dot(active_ref[...], down.reshape(-1, down.shape[3]))
        total = part if total is None else total + part

    @pl.when(step == 0)
    def _():
        sum_ref[...] = total

    @pl.when(step > 0)
    def _():
        sum_ref[...] += total

    @pl.when(step == pl.num_programs(0) - 1)
    def _():
        half = near_ref.shape[0]
        for start, out_ref in ((0, near_ref), (half, far_ref)):
            part = pl.ds(start, half)
            out_ref[...] = (middle_ref[part] + sum_ref[part] + vec_ref[5:6]).astype(BF16)


def feed_down(place, active_parts, down_weight, middle, vectors, chips, after=()):
    group = len(active_parts)
    rows, ff = active_parts[0].shape
    width = down_weight.shape[1]
    chunk = ff // chips
    tile = min(512, ff)
    out = ((rows // 2, width), BF16, pl.BlockSpec((rows // 2, width), lambda i, s: (0, 0)))
    return call(
        functools.partial(feed_down_kernel, group),
        "feed_down",
        place,
        (down_weight.reshape(chips, group, chunk, width), middle, vectors) + tuple(active_parts),
        (ff // tile,),
        [
            pl.BlockSpec((tile // chunk, group, chunk, width), lambda i, s: (i, 0, 0, 0)),
            pl.BlockSpec((rows, width), lambda i, s: (0, 0)),
            pl.BlockSpec((8, width), lambda i, s: (0, 0)),
        ]
        + [pl.BlockSpec((rows, tile), lambda i, s: (0, i))] * group,
        [out, out],
        [pltpu.VMEM((rows, width), F32)],
        after=after,
    )


def middle_back_kernel(group, span, turn, place, middle_ref, cot_ref, vec_ref, weight_ref, *refs):
    part_refs = refs[: group * DH_PIECES]
    branch_ref, d_middle_ref, d_mixed_ref, sums_ref, sum_ref = refs[group * DH_PIECES :]
    step = pl.program_id(0)

    def gather(piece):
        @pl.when(step // span == piece)
        def _():
            total = part_refs[piece * group][...].astype(F32)
            for ref in part_refs[piece * group + 1 : (piece + 1) * group]:
                total = total + ref[...].astype(F32)
            sum_ref[...] = total

    for piece in range(DH_PIECES):
        gather(piece)
    d_hidden = sum_ref[...]
    normal, inverse = norm_parts(middle_ref[...])
    d_middle = cot_ref[...].astype(F32) + norm_back(d_hidden, normal, inverse, vec_ref[2:3])
    branch = d_middle.astype(BF16)
    branch_ref[...] = branch

    @pl.when(step // turn % group == place[0])
    def _():
        d_middle_ref[...] = d_middle

    d_mixed_ref[...] = dot(branch, weight_ref[...], NT).astype(BF16)
    sums = jnp.concatenate(
        [
            jnp.sum(d_hidden * normal, axis=0, keepdims=True),
            jnp.sum(d_hidden, axis=0, keepdims=True),
            jnp.sum(branch.astype(F32), axis=0, keepdims=True),
            jnp.zeros((5, branch.shape[1]), F32),
        ],
        axis=0,
    )

    @pl.when(step == 0)
    def _():
        sums_ref[...] = sums

    @pl.when(step > 0)
    def _():
        sums_ref[...] += sums


def middle_back(place, middle, cotangent, vectors, out_weight, parts, slice_rows, after=()):
    length, width = middle.shape
    group = len(parts[0])
    own = width // group
    rows = min(256, length // DH_PIECES, slice_rows)
    turn = slice_rows // rows
    span = length // DH_PIECES // rows
    row = pl.BlockSpec((rows, width), lambda i, s: (i, 0))
    specs = [
        pl.BlockSpec(
            (rows, width), functools.partial(lambda k, i, s: (jnp.clip(i - k * span, 0, span - 1), 0), piece)
        )
        for piece in range(DH_PIECES)
        for _ in range(group)
    ]
    return call(
        functools.partial(middle_back_kernel, group, span, turn),
        "middle_back",
        place,
        (middle, cotangent, vectors, out_weight) + tuple(array for piece in parts for array in piece),
        (length // rows,),
        [
            row,
            row,
            pl.BlockSpec((8, width), lambda i, s: (0, 0)),
            pl.BlockSpec((own, width), lambda i, s: (s[0], 0)),
        ]
        + specs,
        [
            ((length, width), BF16, row),
            (
                (length // group, width),
                F32,
                pl.BlockSpec((rows, width), lambda i, s: (i // (turn * group) * turn + i % turn, 0)),
            ),
            ((length, own), BF16, pl.BlockSpec((rows, own), lambda i, s: (i, 0))),
            ((8, width), F32, pl.BlockSpec((8, width), lambda i, s: (0, 0))),
        ],
        [pltpu.VMEM((rows, width), F32)],
        after=after,
        vmem=LESS_VMEM if length <= 1024 else VMEM,
    )


def attention_grad_kernel(group, calls, chips, cut, place, *refs):
    ht_ref, dq_ref, dk_ref, dv_ref = refs[:4]
    mixed_refs = refs[5 : 5 + group * calls]
    side_refs = refs[-6 - group : -6]
    ka_ref, sa_ref, kb_ref, sb_ref, stage_ref, rows_ref = refs[-6:]
    offset = 0
    if calls:
        branch = refs[4][...]
        offset = branch.shape[1]
        share = chips // (group * calls)
        for index, mixed_ref in enumerate(mixed_refs):
            owner = ((place[0] + group - index % group) % group) * calls + index // group
            grad = dot(mixed_ref[...], branch, TN).astype(BF16)
            rows = grad.shape[0] // share
            stage_ref[pl.ds(owner * share, share), :, :offset] = grad.reshape(share, rows, offset)
    side = jnp.concatenate([dq_ref[...], dk_ref[...], dv_ref[...]], axis=1)
    hand_out(rows_ref, place[0], side, side_refs)
    rows = ht_ref.shape[0] // chips
    many = max(1, 256 // rows)
    for start in range(0, chips, many):
        grad = dot(ht_ref[start * rows : (start + many) * rows], side).astype(BF16)
        stage_ref[start : start + many, :, offset:] = grad.reshape(many, rows, grad.shape[1])
    for relative in range(chips):
        values = stage_ref[jnp.bitwise_xor(jnp.int32(relative), place[1])]
        (sa_ref if relative & 2 else ka_ref)[without_bit(relative, 1)] = values[:, :cut]
        (sb_ref if relative & 1 else kb_ref)[without_bit(relative, 0)] = values[:, cut:]


def attention_grad(place, hidden_t, triple, group, chips, slice_rows, branch=None, mixed_parts=(), after=()):
    width, length = hidden_t.shape
    own = triple[0].shape[1]
    some = width // chips
    calls = len(mixed_parts)
    columns = 3 * own + (width // group if calls else 0)
    cut = columns // 2
    args = [hidden_t, *triple]
    specs = [pl.BlockSpec((width, length), lambda i, s: (0, 0))]
    specs += [pl.BlockSpec((length, own), lambda i, s: (0, 0))] * 3
    if calls:
        arrays = [mixed_parts[j][s] for j in range(calls) for s in range(group)]
        args += [branch, *arrays]
        specs.append(pl.BlockSpec((length, width // group), lambda i, s: (0, s[0])))
        specs += [pl.BlockSpec(array.shape, lambda i, s: (0, 0)) for array in arrays]
    sides = (length // group, 3 * own)

    def piece(rows, columns):
        shape = (chips // 2, rows, columns)
        return (shape, BF16, pl.BlockSpec(shape, lambda i, s: (0, 0, 0)))

    return call(
        functools.partial(attention_grad_kernel, group, calls, chips, cut),
        "attention_grad",
        place,
        tuple(args),
        (1,),
        specs,
        [(sides, BF16, pl.BlockSpec(sides, lambda i, s: (0, 0)))] * group
        + [piece(some, cut)] * 2
        + [piece(some, columns - cut)] * 2,
        [
            pltpu.VMEM((chips, some, columns), BF16),
            pltpu.VMEM((length // slice_rows, slice_rows, 3 * own), BF16),
        ],
        after=after,
        vmem=LESS_VMEM if length <= 1024 else VMEM,
    )


def hidden_back_kernel(group, calls, place, x_ref, base_ref, vec_ref, *refs):
    number = group * calls
    side_refs = refs[:number]
    weight_refs = refs[number : 4 * number]
    near_ref, far_ref, sums_ref = refs[4 * number :]
    total = None
    for index, side_ref in enumerate(side_refs):
        side = side_ref[...]
        each = side.shape[1] // 3
        row_sums = jnp.sum(side.astype(F32), axis=0, keepdims=True)
        spot = ((place[0] + group - index % group) % group) * calls + index // group
        spot = pl.ds(pl.multiple_of(spot * each, each), each)
        sums_ref[2:3, spot] = row_sums[:, :each]
        sums_ref[3:4, spot] = row_sums[:, 2 * each :]
        for third in range(3):
            part = dot(side[:, third * each : (third + 1) * each], weight_refs[3 * index + third][...], NT)
            total = part if total is None else total + part
    normal, inverse = norm_parts(x_ref[...].reshape(total.shape).astype(F32))
    sums_ref[0:1] = jnp.sum(total * normal, axis=0, keepdims=True)
    sums_ref[1:2] = jnp.sum(total, axis=0, keepdims=True)
    sums_ref[4:8] = jnp.zeros((4, total.shape[1]), F32)
    result = (base_ref[...] + norm_back(total, normal, inverse, vec_ref[0:1])).astype(BF16)
    half = near_ref.shape[0]
    near_ref[...] = result[:half]
    far_ref[...] = result[half:]


def hidden_back(place, x_rows, d_middle, vectors, side_parts, qkv_weight, slice_rows, after=()):
    calls = len(side_parts)
    group = len(side_parts[0])
    rows, columns = side_parts[0][0].shape
    each = columns // 3
    length, width = x_rows.shape
    slices = length // group // slice_rows
    whole = pl.BlockSpec((rows, width), lambda i, s: (0, 0))
    arrays = []
    weights = []
    for j in range(calls):
        for steps in range(group):
            arrays.append(side_parts[j][steps])
            for third in range(3):
                weights.append(
                    pl.BlockSpec(
                        (width, each),
                        functools.partial(
                            lambda j, t, third, i, s: (
                                0,
                                third * group * calls + ((s[0] + group - t) % group) * calls + j,
                            ),
                            j,
                            steps,
                            third,
                        ),
                    )
                )
    out = ((rows // 2, width), BF16, pl.BlockSpec((rows // 2, width), lambda i, s: (0, 0)))
    return call(
        functools.partial(hidden_back_kernel, group, calls),
        "hidden_back",
        place,
        (x_rows.reshape(slices, group, slice_rows, width), d_middle, vectors)
        + tuple(arrays)
        + (qkv_weight,) * len(weights),
        (1,),
        [
            pl.BlockSpec((slices, 1, slice_rows, width), lambda i, s: (0, s[0], 0, 0)),
            whole,
            pl.BlockSpec((8, width), lambda i, s: (0, 0)),
        ]
        + [pl.BlockSpec((rows, columns), lambda i, s: (0, 0))] * len(arrays)
        + weights,
        [out, out, ((8, width), F32, pl.BlockSpec((8, width), lambda i, s: (0, 0)))],
        after=after,
        vmem=LESS_VMEM if length <= 1024 else VMEM,
    )


def part_kernel(takes, whole, place, *refs):
    arrays = (len(refs) - 2 - bool(whole)) // 2
    own_ref, send_ref = refs[2 * arrays : 2 * arrays + 2]
    rows = own_ref.shape[0]
    mine = place[0] == 0
    start = 0

    def total(index, first, count):
        part = pl.ds(first, count)
        return refs[2 * index][0, part].astype(F32) + refs[2 * index + 1][0, part].astype(F32)

    for index, first in takes:
        both = total(index, first, 2 * rows)
        columns = both.shape[1]
        own_ref[:, start : start + columns] = jnp.where(mine, both[:rows], both[rows:])
        send_ref[:, start : start + columns] = jnp.where(mine, both[rows:], both[:rows]).astype(BF16)
        start += columns
    if whole:
        out_ref = refs[-1]
        start = 0
        for index, first in whole:
            value = total(index, first, out_ref.shape[0])
            out_ref[:, start : start + value.shape[1]] = value
            start += value.shape[1]


def part_rows(place, arrays, takes, rows, whole=(), whole_rows=0, after=()):
    columns = sum(arrays[2 * index].shape[2] for index, _ in takes)
    out = pl.BlockSpec((rows, columns), lambda i, s: (0, 0))
    outs = [((rows, columns), F32, out), ((rows, columns), BF16, out)]
    if whole:
        shape = (whole_rows, sum(arrays[2 * index].shape[2] for index, _ in whole))
        outs.append((shape, F32, pl.BlockSpec(shape, lambda i, s: (0, 0))))
    return call(
        functools.partial(part_kernel, takes, whole),
        "part_rows",
        place,
        tuple(arrays),
        (1,),
        [pl.BlockSpec(array.shape, lambda i, s: (0, 0, 0)) for array in arrays],
        outs,
        after=after,
    )


def emit_kernel(moves, place, own_ref, came_ref, *out_refs):
    member = place[0]
    for source, size, out, column, stride in moves:
        for ref, who in ((own_ref, member), (came_ref, 1 - member)):
            spot = pl.ds(pl.multiple_of(column + who * stride, 128), size)
            out_refs[out][:, spot] = ref[:, source : source + size].astype(F32)


def emit(place, own, came, moves, widths, after=()):
    rows, columns = own.shape
    block = pl.BlockSpec((rows, columns), lambda i, s: (0, 0))
    return call(
        functools.partial(emit_kernel, moves),
        "emit",
        place,
        (own, came),
        (1,),
        [block, block],
        [((rows, width), F32, pl.BlockSpec((rows, width), lambda i, s: (0, 0))) for width in widths],
        after=after,
    )


def body(
    inputs,
    cotangent,
    image_lengths,
    norm1_gain,
    norm1_bias,
    qkv_weight,
    qv_bias,
    out_weight,
    out_bias,
    norm2_gain,
    norm2_bias,
    up_weight,
    up_bias,
    down_weight,
    down_bias,
):
    rows, width = inputs.shape[2:]
    limit = image_lengths.shape[-1]
    ff = up_weight.shape[1]
    dp_size = lax.axis_size("dp")
    ctx_size = lax.axis_size("ctx")
    group = ctx_size // 2
    dp_index = lax.axis_index("dp")
    ctx_index = lax.axis_index("ctx")
    half = ctx_index // group
    member = ctx_index % group
    length = rows * ctx_size
    chips = dp_size * 2
    dp_bits = dp_size.bit_length() - 1
    own_width = width // group
    own_ff = ff // group
    chunk = own_ff // chips
    place = Place(jnp.stack([member, dp_index * 2 + half]).astype(jnp.int32))

    def across(value):
        pairs = [(i, (i + group) % ctx_size) for i in range(ctx_size)]
        return lax.ppermute(value, "ctx", pairs)

    def around(value, steps):
        pairs = [
            (h * group + g, h * group + (g + steps) % group) for h in range(2) for g in range(group)
        ]
        return lax.ppermute(value, "ctx", pairs)

    def all_around(value):
        return [value] + [around(value, steps) for steps in range(1, group)]

    def in_order(parts, axis=0):
        if group == 2:
            first = member == 0
            return jnp.stack(
                [jnp.where(first, parts[0], parts[1]), jnp.where(first, parts[1], parts[0])], axis=axis
            )
        return jnp.roll(jnp.stack(parts[::-1], axis=axis), member + 1, axis=axis)

    def gather(value):
        return in_order(all_around(value))

    def pick(value, index, axis):
        return lax.dynamic_index_in_dim(value, index, axis, keepdims=False)

    def group_sum_scatter(value, axis):
        total = pick(value, member, axis).astype(F32)
        for steps in range(1, group):
            total = total + around(pick(value, (member + steps) % group, axis), steps).astype(F32)
        return total

    def swap_bit(value, bit):
        if bit < 0:
            return across(value)
        return lax.ppermute(value, "dp", [(i, i ^ (1 << bit)) for i in range(dp_size)])

    all_bits = list(range(dp_bits - 1, -1, -1)) + [-1]
    rest_bits = list(range(1, dp_bits))

    class Halving:
        def __init__(self, keep, send, bits, order):
            self.order = list(order)
            self.left = list(bits)
            self.keep = keep
            self.came = swap_bit(send, self.order[0])
            self.order.pop(0)

    def pair(pieces):
        first = [bit for bit in all_bits if bit != 0]
        second = [bit for bit in all_bits if bit != -1]
        return [
            Halving(*pieces[:2], first, [0, -1] + rest_bits),
            Halving(*pieces[2:], second, [-1, 0] + rest_bits),
        ]

    def step(after, *jobs):
        asked = []
        for halvings in jobs:
            first = halvings[0]
            bit = first.order[0]
            arrays = [array for halving in halvings for array in (halving.keep, halving.came)]
            asked.append((arrays, len(first.left) - 1 - first.left.index(bit)))
        sums = step_call(place, asked, after)
        results = []
        for index, halvings in enumerate(jobs):
            first = halvings[0]
            left = [bit for bit in first.left if bit != first.order[0]]
            results.append(Halving(sums[2 * index], sums[2 * index + 1], left, first.order))
        return list(sums[:1]), results

    slices = 2 if group > 2 else 1
    slice_rows = rows // slices

    def sliced(value):
        return [value[c * slice_rows : (c + 1) * slice_rows] for c in range(slices)]

    own_inputs = pick(inputs, half, 0)[0]
    far_inputs = across(pick(inputs, 1 - half, 0)[0])
    vectors = jnp.stack([norm1_gain, norm1_bias, norm2_gain, norm2_bias, out_bias, down_bias, out_bias, out_bias])
    vectors = vectors.astype(F32)
    filled = ()
    for side, both_of in enumerate((own_inputs, far_inputs)):
        for c, part in enumerate(sliced(both_of)):
            start = (side * slices + c) * (length // (2 * slices))
            copied = cotangent if not filled else None
            filled = project(
                place, all_around(part), start, length, vectors, qkv_weight, qv_bias, filled, copied
            )
            if copied is not None:
                *filled, own_cot, far_cot = filled
    x_rows, hidden1_t, query, keys, values = filled
    cot_parts = [part for value in sliced(own_cot) for part in all_around(value)]
    far_cot = across(far_cot)
    cot_parts += [part for value in sliced(far_cot) for part in all_around(value)]

    spots = jnp.arange(length, dtype=jnp.int32).reshape(2, group, slices, rows // slices)
    spots = jnp.swapaxes(spots, 1, 2)
    positions = jnp.where(half == 0, spots, spots[::-1]).reshape(length)
    ends = jnp.cumsum(pick(image_lengths, half, 0)[0])
    segment = jnp.sum((positions[:, None] >= ends[None, :]).astype(jnp.int32), axis=1)
    seg_row = segment.reshape(1, length)
    seg_cols = jnp.broadcast_to(segment[:, None], (length, PAIR))

    if chunk % 128 == 0:
        up_arrays = up_weight

        def up_blocks(tile):
            return tile // chunk, up_specs(width, tile, chunk, group, tile // chunk)

    else:
        up_arrays = pick(up_weight.reshape(width, chips, group, chunk), member, 2).reshape(width, own_ff)

        def up_blocks(tile):
            return 1, [pl.BlockSpec((width, tile), lambda t, s: (0, t))]

    upb_own = pick(up_bias.reshape(chips, group, chunk), member, 1).reshape(1, own_ff)

    pairs = own_width // PAIR
    calls = min(2, pairs)
    each = pairs // calls
    mixed = []
    logs = []
    mixed_parts = []
    ready = []
    for j in range(calls):
        mixed_j, logs_j = attend(
            place, j * each, each, query, keys, values, seg_cols, seg_row, limit, after=ready
        )
        mixed.append(mixed_j)
        logs.append(logs_j)
        mixed_parts.append(all_around(mixed_j))
        ready = [mixed_j]
    cot_rows, cot_sums = collect(place, cot_parts, group, after=ready)
    middle, middle_own, hidden2, hidden2_t = close(
        place, x_rows, mixed_parts, group, out_weight, vectors, slice_rows, after=[cot_rows]
    )
    up_out = feed_up(
        place,
        hidden2,
        cot_rows,
        up_arrays,
        up_blocks,
        upb_own,
        group,
        chips,
        width // 2,
        slice_rows,
    )
    active_parts = up_out[:group]
    slope, *down_pieces = up_out[group:]
    active_parts = [active_parts[0]] + [around(active_parts[steps], steps) for steps in range(1, group)]
    down = pair(down_pieces)
    back = feed_back(
        place,
        hidden2_t,
        cot_rows,
        slope,
        down_weight,
        up_arrays,
        up_blocks,
        group,
        chips,
        0.5,
        after=down_pieces[:1],
    )
    dh_pieces = back[:DH_PIECES]
    upb_grad, *up_pieces = back[DH_PIECES:]
    dh_parts = [all_around(piece) for piece in dh_pieces]
    up = pair(up_pieces)

    ready, down = step(dh_pieces[:1], [down[0]], [down[1]])
    branch, d_middle, d_mixed, sums = middle_back(
        place, middle, cot_rows, vectors, out_weight, dh_parts, slice_rows, after=ready
    )

    def back_of(j, after):
        return attend_back(
            place, j * each, query, keys, values, d_mixed, mixed[j], logs[j], seg_cols, seg_row, limit, after=after
        )

    def grad_of(j, triple, after):
        results = attention_grad(
            place,
            hidden1_t,
            triple,
            group,
            chips,
            slice_rows,
            branch if j == 0 else None,
            mixed_parts if j == 0 else (),
            after=after,
        )
        sides = results[:group]
        sides = [sides[0]] + [around(sides[steps], steps) for steps in range(1, group)]
        return pair(results[group:]), sides, list(results[:1])

    triple = back_of(0, [branch])
    early, sides, ready = grad_of(0, triple, triple[:1])
    sides_of = [sides]
    ready, (down,) = step(ready, down)
    if calls > 1:
        ready, up = step(ready, [up[0]], [up[1]])
        triple = back_of(1, ready)
        late, sides, ready = grad_of(1, triple, triple[:1])
        sides_of.append(sides)
        ready, (up, down, *early) = step(ready, up, [down], [early[0]], [early[1]])
    else:
        ready, (*up, down) = step(ready, [up[0]], [up[1]], [down])
        ready, (up, *early) = step(ready, up, [early[0]], [early[1]])
    input_near, input_far, own_sums = hidden_back(
        place, x_rows, d_middle, vectors, sides_of, qkv_weight, slice_rows, after=ready
    )

    own = width // (chips * group)
    both = 1.0 / group
    member_is = (jnp.arange(group, dtype=jnp.int32) == member).astype(F32)
    sums_of = jnp.concatenate([own_sums[:4], sums[2:3] * both, sums[:2] * both, cot_sums[:1] * both])
    small = jnp.transpose(sums_of.reshape(8, chips * group, own), (1, 0, 2)).reshape(chips * group, 8 * own)
    upb_full = (upb_grad.reshape(chips, 1, chunk) * member_is[None, :, None]).reshape(chips * group, chunk)
    small = jnp.concatenate([small, upb_full], axis=1)
    small = lax.all_to_all(small, ("dp", "ctx"), 0, 0, tiled=True)
    small = jnp.sum(small, axis=0)
    small_rows = small[: 8 * own].reshape(8, own)
    upb_out = small[8 * own :]

    ready = [input_near]
    if calls > 1:
        ready, (*late, up, early) = step(ready, [late[0]], [late[1]], [up], early)
    else:
        ready, (early,) = step(ready, early)
    out_near, out_far = feed_down(place, active_parts, down_weight, middle_own, vectors, chips, after=ready)
    ready = [out_near]
    if calls > 1:
        ready, (late, early) = step(ready, late, [early])
        tails = [down, up, early, late]
    else:
        tails = [down, up, early]
    while any(tail.order for tail in tails):
        active = [tail for tail in tails if tail.order]
        ready, stepped = step(ready, *[[tail] for tail in active])
        for tail, new in zip(active, stepped):
            tails[tails.index(tail)] = new

    def hand_back(near, far):
        came = across(far)
        first = half == 0
        return jnp.stack([jnp.where(first, near, came), jnp.where(first, came, near)])[:, None]

    block_output = hand_back(out_near, out_far)
    input_grad = hand_back(input_near, input_far)

    some = width // chips

    def exchange(value):
        value = value.reshape(group, own, value.shape[1])
        parts = [pick(value, member, 0)] + [
            around(pick(value, (member + steps) % group, 0).astype(BF16), steps).astype(F32)
            for steps in range(1, group)
        ]
        return in_order(parts, 1)

    def sums_in(tail):
        return tail.keep[0].astype(F32) + tail.came[0].astype(F32)

    down, up, *rest = tails
    if group == 2 and own % 16 == 0:
        columns = up.keep.shape[2]
        up_own, up_send, down_out = part_rows(
            place,
            [down.keep, down.came, up.keep, up.came],
            [(1, k * some) for k in range(own_ff // columns)],
            own,
            [(0, k * chunk) for k in range(2)],
            chunk,
            ready,
        )
        moves = [(k * chunk, chunk, 0, k * 2 * chunk, chunk) for k in range(chips)]
        (up_out,) = emit(place, up_own, around(up_send, 1), moves, [ff])
        rest_own, rest_send = part_rows(
            place,
            [array for tail in rest for array in (tail.keep, tail.came)],
            [(index, first) for index in range(calls) for first in (0, some)],
            own,
            after=[up_out],
        )
        moves = [(0, own_width, 0, 0, own_width)] + [
            (own_width + (j * 3 + t) * each * PAIR, each * PAIR, 1, t * width + j * each * PAIR, own_width)
            for j in range(calls)
            for t in range(3)
        ]
        out_out, qkv_out = emit(place, rest_own, around(rest_send, 1), moves, [width, 3 * width])
    else:

        def blocks_of(tail, rows):
            value = sums_in(tail)
            return [value[start : start + rows] for start in range(0, value.shape[0], rows)]

        down_out = jnp.concatenate(blocks_of(down, chunk), axis=1)
        up_out = exchange(jnp.concatenate(blocks_of(up, some), axis=1)).reshape(own, group, chips, chunk)
        up_out = jnp.swapaxes(up_out, 1, 2).reshape(own, ff)
        parts = [part for tail in rest for part in blocks_of(tail, some)]
        rest = exchange(jnp.concatenate(parts, axis=1))
        out_out = rest[:, :, :own_width].reshape(own, width)
        qkv_out = rest[:, :, own_width:].reshape(own, group, calls, 3, each * PAIR)
        qkv_out = jnp.transpose(qkv_out, (0, 3, 1, 2, 4)).reshape(own, 3 * width)
    return (
        block_output,
        input_grad,
        small_rows[0],
        small_rows[1],
        qkv_out,
        small_rows[2:4],
        out_out,
        small_rows[4],
        small_rows[5],
        small_rows[6],
        up_out,
        upb_out,
        down_out,
        small_rows[7],
    )


def solution(mesh):
    split = P(None, "dp", "ctx", None)
    both = ("dp", "ctx")
    return jax.shard_map(
        body,
        mesh=mesh,
        in_specs=(split, split, P(None, "dp", None)) + (P(),) * 12,
        out_specs=(
            split,
            split,
            P(both),
            P(both),
            P(both, None),
            P(None, both),
            P(both, None),
            P(both),
            P(both),
            P(both),
            P(both, None),
            P(both),
            P(both, None),
            P(both),
        ),
        check_vma=False,
    )
```

```python
import functools

import jax
import jax.numpy as jnp
from jax import lax
from jax.experimental import pallas as pl
from jax.experimental.pallas import tpu as pltpu
from jax.sharding import PartitionSpec as P

HEADS = 16
HIDES = {"step": 20, "attend": 40, "project": 6}
HEAD_DIM = 64
PAIR = 2 * HEAD_DIM
NEG = -1e30
EPS = 1e-06
LOG2E = 1.4426950408889634
SCALE = HEAD_DIM ** (-0.5)
BF16 = jnp.bfloat16
F32 = jnp.float32
VMEM = 60 * 1024 * 1024
LESS_VMEM = 26 * 1024 * 1024
DH_PIECES = 1
PIN = True
KEEP = False
COST = 6 * 1150 * 1000 * 1000

NT = (((1,), (1,)), ((), ()))
NN = (((1,), (0,)), ((), ()))
TN = (((0,), (0,)), ((), ()))


def dot(left, right, dims=NN):
    return lax.dot_general(left, right, dims, preferred_element_type=F32)


def call(kernel, name, place, args, grid, in_specs, outs, scratch=(), after=(), fill=(), cost=0):
    known = len(args)
    skipped = len(after) + len(fill)
    stays = [len(out) > 3 and out[3] and not place.long for out in outs]

    def settled(array):
        pinned = any(array is other for other in place.pinned)
        if not pinned and any(array is other for other in place.free):
            return array
        return pltpu.with_memory_space_constraint(array, pltpu.VMEM if pinned else pltpu.HBM)

    def inner(place_ref, *refs):
        kernel(place_ref, *refs[:known], *refs[known + skipped :])

    anywhere = pl.BlockSpec(memory_space=pl.ANY)
    first = 1 + known + len(after)
    results = pl.pallas_call(
        inner,
        grid_spec=pltpu.PrefetchScalarGridSpec(
            num_scalar_prefetch=1,
            grid=grid,
            in_specs=list(in_specs) + [anywhere] * skipped,
            out_specs=[out[2] for out in outs],
            scratch_shapes=list(scratch),
        ),
        out_shape=[(pltpu.VMEM if stay else pltpu.HBM)(out[0], out[1]) for out, stay in zip(outs, stays)],
        input_output_aliases={first + index: index for index in range(len(fill))},
        compiler_params=pltpu.CompilerParams(vmem_limit_bytes=VMEM if place.long else LESS_VMEM),
        cost_estimate=pl.CostEstimate(flops=int(1.15e9 * HIDES.get(name, 0)), bytes_accessed=0, transcendentals=0),
        name=name,
    )(place.numbers, *[settled(array) for array in (*args, *after, *fill)])
    place.pinned += [array for array, stay in zip(results, stays) if stay]
    return results


class Place:
    def __init__(self, numbers, long):
        self.numbers = numbers
        self.long = long
        self.pinned = []
        self.free = []


def without_bit(number, spot):
    return ((number >> (spot + 1)) << spot) | (number & ((1 << spot) - 1))


def deal(stage_ref, me, pieces):
    for relative in range(stage_ref.shape[0]):
        rows = stage_ref[jnp.bitwise_xor(jnp.int32(relative), me)]
        for keep_ref, send_ref, bit, columns in pieces:
            target = send_ref if (relative >> bit) & 1 else keep_ref
            target[without_bit(relative, bit)] = rows[:, columns]


def norm_parts(values):
    centred = values - jnp.mean(values, axis=-1, keepdims=True)
    inverse = lax.rsqrt(jnp.mean(centred * centred, axis=-1, keepdims=True) + EPS)
    return centred * inverse, inverse


def norm_back(grad, normal, inverse, gain):
    scaled = grad * gain
    inner = (
        scaled
        - jnp.mean(scaled, axis=-1, keepdims=True)
        - normal * jnp.mean(scaled * normal, axis=-1, keepdims=True)
    )
    return inverse * inner


def step_kernel(jobs, place, *refs):
    ins = sum(len(layout) for _, layout, _ in jobs) * 2
    sources = refs[:ins]
    targets = refs[ins:]
    for spot, layout, parts in jobs:
        if spot is None:
            old_ref, came_ref = sources[:2]
            sources = sources[2:]
            targets[0][...] = old_ref[0].astype(F32) + came_ref[0].astype(F32)
            targets = targets[1:]
            continue
        if parts == 2:
            old_ref, came_ref = sources[:2]
            sources = sources[2:]
            for index in range(2):
                rows = pl.ds(index * targets[0].shape[1], targets[0].shape[1])
                for number in range(old_ref.shape[0]):
                    value = old_ref[number, rows].astype(F32) + came_ref[number, rows].astype(F32)
                    target = targets[(number >> spot) & 1]
                    target[without_bit(number, spot)] = value.astype(target.dtype)
                targets = targets[2:]
            continue
        keep_ref, send_ref = targets[:2]
        targets = targets[2:]
        columns = keep_ref.shape[2]
        base = 0
        for rows, width in layout:
            old_ref, came_ref = sources[:2]
            sources = sources[2:]
            for number in range(old_ref.shape[0]):
                value = (old_ref[number].astype(F32) + came_ref[number].astype(F32)).astype(keep_ref.dtype)
                target = send_ref if (number >> spot) & 1 else keep_ref
                spare = without_bit(number, spot)
                for part in range(width // columns):
                    start = base + part * rows
                    target[spare, start : start + rows] = value[:, part * columns : (part + 1) * columns]
            base += rows * (width // columns)


def step_call(place, jobs, after=(), cost=0):
    ins = []
    outs = []
    layouts = []
    for arrays, spot, parts in jobs:
        columns = min(array.shape[2] for array in arrays)
        layout = [array.shape[1:] for array in arrays[::2]]
        if spot is None:
            layouts.append((None, layout, 1))
            ins += arrays
            outs.append((layout[0], F32, pl.BlockSpec(layout[0], lambda i, s: (0, 0))))
            continue
        rows = sum(rows * (width // columns) for rows, width in layout)
        shape = (arrays[0].shape[0] // 2, rows // parts, columns)
        layouts.append((spot, layout, parts))
        ins += arrays
        spec = pl.BlockSpec(shape, lambda i, s: (0, 0, 0))
        outs += [(shape, arrays[0].dtype, spec, KEEP), (shape, arrays[0].dtype, spec, PIN)] * parts
    return call(
        functools.partial(step_kernel, layouts),
        "step",
        place,
        tuple(ins),
        (1,),
        [pl.BlockSpec(array.shape, lambda i, s: (0, 0, 0)) for array in ins],
        outs,
        after=after,
        cost=cost,
    )


def hand_out(stage_ref, group, member, value, out_refs):
    rows = stage_ref.shape[1]
    stage_ref[...] = value.reshape(stage_ref.shape)
    for steps, out_ref in enumerate(out_refs):
        first = out_ref.shape[1] - stage_ref.shape[2]
        for block in range(stage_ref.shape[0] // group):
            part = stage_ref[block * group + (member + steps) % group]
            out_ref[block * rows : (block + 1) * rows, first:] = part


def project_kernel(group, copies, place, *refs):
    part_refs = refs[:group]
    vec_ref, wq_ref, wk_ref, wv_ref, qvb_ref = refs[group : group + 5]
    refs = refs[group + 5 :]
    if copies:
        refs[-2][...] = refs[0][...].reshape(refs[-2].shape)
        refs[-1][...] = refs[1][...].reshape(refs[-1].shape)
        refs = refs[2:-2]
    x_ref, ht_ref, q_ref, k_ref, v_ref = refs
    gain = vec_ref[0:1]
    shift = vec_ref[1:2]
    qvb = qvb_ref[...].astype(F32)
    rows = part_refs[0].shape[0]
    for steps, part_ref in enumerate(part_refs):
        base = ((place[0] + group - steps) % group) * rows
        spot = pl.ds(pl.multiple_of(base, rows), rows)
        values = part_ref[...]
        x_ref[spot] = values
        normal, _ = norm_parts(values.astype(F32))
        hidden = (normal * gain + shift).astype(BF16)
        ht_ref[:, spot] = hidden.T
        q_ref[spot] = (dot(hidden, wq_ref[...]) + qvb[0:1]).astype(BF16)
        k_ref[spot] = dot(hidden, wk_ref[...]).astype(BF16)
        v_ref[spot] = (dot(hidden, wv_ref[...]) + qvb[1:2]).astype(BF16)


def project(place, parts, first_row, length, vectors, qkv_weight, qv_bias, fill, copied=None):
    group = len(parts)
    rows, width = parts[0].shape
    own = width // group
    rows = rows * group
    index = first_row // rows
    extra = ()
    extra_in = []
    extra_out = []
    if copied is not None:
        shape = copied.shape[2:]
        extra = (copied, copied)
        extra_in = [
            pl.BlockSpec((1, 1) + shape, lambda i, s: (s[1] % 2, 0, 0, 0)),
            pl.BlockSpec((1, 1) + shape, lambda i, s: (1 - s[1] % 2, 0, 0, 0)),
        ]
        extra_out = [(shape, BF16, pl.BlockSpec(shape, lambda i, s: (0, 0)))] * 2
    vector = pl.BlockSpec((8, width), lambda i, s: (0, 0))
    part = pl.BlockSpec((rows // group, width), lambda i, s: (0, 0))
    row = pl.BlockSpec((rows, own), lambda i, s: (index, 0))
    weights = [
        pl.BlockSpec((width, own), functools.partial(lambda t, i, s: (0, t * group + s[0]), t))
        for t in range(3)
    ]
    return call(
        functools.partial(project_kernel, group, copied is not None),
        "project",
        place,
        tuple(parts) + (vectors, qkv_weight, qkv_weight, qkv_weight, qv_bias) + extra,
        (1,),
        [part] * group
        + [vector]
        + weights
        + [pl.BlockSpec((2, own), lambda i, s: (0, s[0]))]
        + extra_in,
        [
            ((length, width), BF16, pl.BlockSpec((rows, width), lambda i, s: (index, 0))),
            ((width, length), BF16, pl.BlockSpec((width, rows), lambda i, s: (0, index))),
        ]
        + [((length, own), BF16, row)] * 3
        + extra_out,
        fill=fill,
    )


def attend_kernel(limit, sub, place, q_ref, k_ref, v_ref, segc_ref, segr_ref, mixed_ref, lse_ref):
    keys = k_ref[...]
    keys = jnp.concatenate([keys, keys], axis=1)
    values = v_ref[...]
    values = jnp.concatenate([values, jnp.ones(values.shape, BF16)], axis=1)
    lane = lax.broadcasted_iota(jnp.int32, (sub, PAIR), 1)
    zero = jnp.zeros((), BF16)
    segr = segr_ref[...]
    for start in range(0, q_ref.shape[0], sub):
        part = pl.ds(start, sub)
        scaled = q_ref[part].astype(F32) * (SCALE * LOG2E)
        high = scaled.astype(BF16)
        low = (scaled - high.astype(F32)).astype(BF16)
        segc = segc_ref[part]
        valid = segc < limit
        bias = jnp.where(jnp.where(valid, segc, -1)[:, :1] == segr, 0.0, NEG)
        mixed = []
        logs = []
        for head in range(2):
            own = (lane < HEAD_DIM) == (head == 0)
            query = jnp.concatenate([jnp.where(own, high, zero), jnp.where(own, low, zero)], axis=1)
            scores = dot(query, keys, NT) + bias
            largest = jnp.max(scores, axis=1, keepdims=True)
            weights = jnp.exp2(scores - largest).astype(BF16)
            summed = dot(weights, values)
            total = summed[:, PAIR:]
            mixed.append(summed[:, :PAIR] / total)
            logs.append(largest + jnp.log2(total))
        first = lane < HEAD_DIM
        mixed_ref[part] = jnp.where(valid, jnp.where(first, mixed[0], mixed[1]), 0.0).astype(BF16)
        lse_ref[part] = jnp.where(valid, jnp.where(first, logs[0], logs[1]), 0.0)


def attend(place, first, count, query, keys, values, seg_cols, seg_row, limit, after=()):
    length = query.shape[0]
    width = count * PAIR
    block = min(1024, length)
    tile = pl.BlockSpec((block, PAIR), lambda p, j, s: (j, first + p))
    whole = pl.BlockSpec((length, PAIR), lambda p, j, s: (0, first + p))
    out_tile = pl.BlockSpec((block, PAIR), lambda p, j, s: (j, p))
    return call(
        functools.partial(attend_kernel, limit, min(256, block)),
        "attend",
        place,
        (query, keys, values, seg_cols, seg_row),
        (width // PAIR, length // block),
        [
            tile,
            whole,
            whole,
            pl.BlockSpec((block, PAIR), lambda p, j, s: (j, 0)),
            pl.BlockSpec((1, length), lambda p, j, s: (0, 0)),
        ],
        [((length, width), BF16, out_tile), ((length, width), F32, out_tile)],
        after=after,
    )


def attend_back_kernel(
    limit,
    sub,
    grads,
    place,
    q_ref,
    k_ref,
    v_ref,
    do_ref,
    mixed_ref,
    lse_ref,
    segc_ref,
    segr_ref,
    *refs,
):
    kt_ref, dk_sum, dv_sum, side_ref, stage_ref, rows_ref = refs[-6:]
    pair = pl.program_id(0)
    step = pl.program_id(1)
    steps = pl.num_programs(1)
    own_width = side_ref.shape[1] // 3
    length = k_ref.shape[0]
    keys = k_ref[...]
    kt_ref[...] = keys.T
    zero = jnp.zeros((), BF16)
    minus = -jnp.ones((), BF16)
    values = v_ref[...]
    key_lane = lax.broadcasted_iota(jnp.int32, (length, PAIR), 1)
    lane = lax.broadcasted_iota(jnp.int32, (sub, PAIR), 1)
    spot = lane & (HEAD_DIM - 1)
    ones = jnp.where((key_lane & (HEAD_DIM - 1)) < 3, minus, zero)
    key_sides = []
    value_sides = []
    for head in range(2):
        own = (key_lane < HEAD_DIM) == (head == 0)
        key_sides.append(jnp.concatenate([jnp.where(own, keys, ones), keys], axis=1))
        value_sides.append(jnp.where(own, values, ones))
    segc = segc_ref[...]
    segc = jnp.where(segc < limit, segc, -1)[:, :1]

    def in_three(value):
        high = value.astype(BF16)
        rest = value - high.astype(F32)
        middle = rest.astype(BF16)
        low = (rest - middle.astype(F32)).astype(BF16)
        return jnp.where(spot == 0, high, jnp.where(spot == 1, middle, jnp.where(spot == 2, low, zero)))

    dk_all = dv_all = None
    for start in range(0, q_ref.shape[0], sub):
        part = pl.ds(start, sub)
        query = q_ref[part]
        scaled = query.astype(F32) * (SCALE * LOG2E)
        high = scaled.astype(BF16)
        low = (scaled - high.astype(F32)).astype(BF16)
        grad = do_ref[part]
        product = grad.astype(F32) * mixed_ref[part].astype(F32)
        logs = lse_ref[part]
        same = segc == segr_ref[:, part]
        dq_rows = []
        for head in range(2):
            own = (lane < HEAD_DIM) == (head == 0)
            log = jnp.broadcast_to(logs[:, head * HEAD_DIM : head * HEAD_DIM + 1], logs.shape)
            delta = jnp.sum(jnp.where(own, product, 0.0), axis=1, keepdims=True)
            delta = jnp.broadcast_to(delta, logs.shape)
            query_side = jnp.concatenate(
                [jnp.where(own, high, in_three(log)), jnp.where(own, low, zero)], axis=1
            )
            grad_side = jnp.where(own, grad, in_three(delta))
            scores = dot(key_sides[head], query_side, NT)
            probs = jnp.where(same, jnp.exp2(scores), 0.0).astype(BF16)
            d_probs = dot(value_sides[head], grad_side, NT)
            d_scores = probs * d_probs.astype(BF16)
            dv_part = dot(probs, jnp.where(own, grad, zero))
            dk_part = dot(d_scores, jnp.where(own, query, zero))
            dv_all = dv_part if dv_all is None else dv_all + dv_part
            dk_all = dk_part if dk_all is None else dk_all + dk_part
            dq_rows.append(dot(kt_ref[head * HEAD_DIM : (head + 1) * HEAD_DIM], d_scores))
        target = pl.ds(pl.multiple_of(step * q_ref.shape[0] + start, sub), sub)
        columns = pl.ds(pl.multiple_of(pair * PAIR, PAIR), PAIR)
        side_ref[target, columns] = (jnp.concatenate(dq_rows, axis=0).T * SCALE).astype(BF16)
    dk_all = dk_all * SCALE

    @pl.when(step == 0)
    def _():
        dk_sum[...] = dk_all
        dv_sum[...] = dv_all

    @pl.when(step > 0)
    def _():
        dk_sum[...] += dk_all
        dv_sum[...] += dv_all

    @pl.when(step == steps - 1)
    def _():
        for place_of, sum_ref in ((1, dk_sum), (2, dv_sum)):
            columns = pl.ds(pl.multiple_of(place_of * own_width + pair * PAIR, PAIR), PAIR)
            side_ref[:, columns] = sum_ref[...].astype(BF16)

    @pl.when((step == steps - 1) & (pair == pl.num_programs(0) - 1))
    def _():
        grads(place, side_ref, stage_ref, rows_ref, *refs[:-6])


def attend_back(
    place,
    first,
    count,
    query,
    keys,
    values,
    d_mixed,
    mixed,
    logs,
    seg_cols,
    seg_row,
    limit,
    hidden_t,
    group,
    chips,
    slice_rows,
    branch=None,
    mixed_parts=(),
    earlier=(),
    split=True,
    after=(),
):
    length = mixed.shape[0]
    own = count * PAIR
    block = length if length <= 1024 else 256
    tile = pl.BlockSpec((block, PAIR), lambda p, j, s: (j, first + p))
    whole = pl.BlockSpec((length, PAIR), lambda p, j, s: (0, first + p))
    width = hidden_t.shape[0]
    some = width // chips
    calls = len(mixed_parts)
    columns = 3 * own + (width // group if calls else 0)
    cut = columns // 2 if split else columns
    sides = (length // group, 3 * own + (earlier[0].shape[1] if earlier else 0))
    args = [hidden_t]
    specs = [pl.BlockSpec((width, length), lambda p, j, s: (0, 0), pipeline_mode=pl.Buffered(1))]
    if calls:
        arrays = [mixed_parts[j][s] for j in range(calls) for s in range(group)]
        args += [branch, *arrays]
        specs.append(
            pl.BlockSpec((length, width // group), lambda p, j, s: (0, s[0]), pipeline_mode=pl.Buffered(1))
        )
        specs += [
            pl.BlockSpec(array.shape, lambda p, j, s: (0, 0), pipeline_mode=pl.Buffered(1)) for array in arrays
        ]
    args += earlier
    specs += [
        pl.BlockSpec(array.shape, lambda p, j, s: (0, 0), pipeline_mode=pl.Buffered(1)) for array in earlier
    ]

    def pieces(columns):
        shape = (chips // 2, some, columns)
        spec = pl.BlockSpec(shape, lambda p, j, s: (0, 0, 0))
        return [(shape, BF16, spec, KEEP), (shape, BF16, spec, PIN)]

    return call(
        functools.partial(
            attend_back_kernel,
            limit,
            min(256, block),
            functools.partial(attention_grads, group, calls, chips, cut, bool(earlier)),
        ),
        "attend_back",
        place,
        (query, keys, values, d_mixed, mixed, logs, seg_cols, seg_row, *args),
        (own // PAIR, length // block),
        [
            tile,
            whole,
            whole,
            tile,
            tile,
            tile,
            pl.BlockSpec((length, PAIR), lambda p, j, s: (0, 0)),
            pl.BlockSpec((1, block), lambda p, j, s: (0, j)),
        ]
        + specs,
        [(sides, BF16, pl.BlockSpec(sides, lambda p, j, s: (0, 0)))] * group
        + pieces(cut)
        + (pieces(columns - cut) if split else []),
        [
            pltpu.VMEM((PAIR, length), BF16),
            pltpu.VMEM((length, PAIR), F32),
            pltpu.VMEM((length, PAIR), F32),
            pltpu.VMEM((length, 3 * own), BF16),
            pltpu.VMEM((chips, some, columns), BF16),
            pltpu.VMEM((length // slice_rows, slice_rows, 3 * own), BF16),
        ],
        after=after,
    )


def collect_kernel(group, place, *refs):
    part_refs = refs[:-2]
    rows_ref, sums_ref = refs[-2:]
    count = part_refs[0].shape[0]
    total = None
    for index, part_ref in enumerate(part_refs):
        block, steps = index // group, index % group
        values = part_ref[...]
        spot = block * group + (place[0] + group - steps) % group
        rows_ref[pl.ds(pl.multiple_of(spot * count, count), count)] = values
        part = jnp.sum(values.astype(F32), axis=0, keepdims=True)
        total = part if total is None else total + part
    sums_ref[...] = jnp.concatenate([total, jnp.zeros((7, total.shape[1]), F32)], axis=0)


def collect(place, parts, group, after=()):
    rows, width = parts[0].shape
    length = rows * len(parts)
    whole = pl.BlockSpec((rows, width), lambda i, s: (0, 0))
    return call(
        functools.partial(collect_kernel, group),
        "collect",
        place,
        tuple(parts),
        (1,),
        [whole] * len(parts),
        [
            ((length, width), BF16, pl.BlockSpec((length, width), lambda i, s: (0, 0)), length <= 1024),
            ((8, width), F32, pl.BlockSpec((8, width), lambda i, s: (0, 0))),
        ],
        after=after,
    )


def close_kernel(number, place, x_ref, vec_ref, *refs):
    mixed_refs = refs[:number]
    weight_refs = refs[number : 2 * number]
    middle_ref, own_ref, hidden_ref, ht_ref = refs[2 * number :]
    gain = vec_ref[2:3]
    shift = vec_ref[3:4]
    bias = vec_ref[4:5]
    sub = 256
    for start in range(0, x_ref.shape[0], sub):
        part = pl.ds(start, sub)
        middle = x_ref[part].astype(F32) + bias
        for mixed_ref, weight_ref in zip(mixed_refs, weight_refs):
            middle = middle + dot(mixed_ref[part], weight_ref[...])
        middle_ref[part] = middle
        normal, _ = norm_parts(middle)
        hidden = (normal * gain + shift).astype(BF16)
        hidden_ref[part] = hidden
        ht_ref[:, part] = hidden.T
    count = own_ref.shape[0]
    own_ref[...] = middle_ref[pl.ds(pl.multiple_of(place[0] * count, count), count)]


def close(place, x_rows, mixed_parts, group, out_weight, vectors, slice_rows, after=()):
    length, width = x_rows.shape
    calls = len(mixed_parts)
    number = calls * group
    own = width // number
    rows = slice_rows * group
    vector = pl.BlockSpec((8, width), lambda i, s: (0, 0))
    row = pl.BlockSpec((rows, width), lambda i, s: (i, 0))
    arrays = []
    weights = []
    for j in range(calls):
        for steps in range(group):
            arrays.append(mixed_parts[j][steps])
            weights.append(
                pl.BlockSpec(
                    (own, width),
                    functools.partial(lambda j, t, i, s: (((s[0] + group - t) % group) * calls + j, 0), j, steps),
                )
            )
    return call(
        functools.partial(close_kernel, number),
        "close",
        place,
        (x_rows, vectors)
        + tuple(arrays)
        + (out_weight,) * number,
        (length // rows,),
        [row, vector] + [pl.BlockSpec((rows, own), lambda i, s: (i, 0))] * number + weights,
        [
            ((length, width), F32, row),
            ((length // group, width), F32, pl.BlockSpec((slice_rows, width), lambda i, s: (i, 0))),
            ((length, width), BF16, row, length <= 1024),
            ((width, length), BF16, pl.BlockSpec((width, rows), lambda i, s: (0, i)), length <= 1024),
        ],
        after=after,
    )


def up_specs(width, tile, block, group, number):
    return [
        pl.BlockSpec((width, block), functools.partial(lambda n, t, s: (0, (t * number + n) * group + s[0]), n))
        for n in range(number)
    ]


def feed_up_kernel(number, group, cut, place, h_ref, cot_ref, upb_ref, *refs):
    up_refs = refs[:number]
    active_refs = refs[number : number + group]
    slope_ref, ka_ref, sa_ref, kb_ref, sb_ref, stage_ref, rows_ref = refs[number + group :]
    up = jnp.concatenate([ref[...] for ref in up_refs], axis=1) if number > 1 else up_refs[0][...]
    upper = dot(h_ref[...], up) + upb_ref[...].astype(F32)
    half = 0.5 + 0.5 * lax.erf(upper * 0.7071067811865476)
    bell = jnp.exp2(upper * upper * (-0.5 * LOG2E)) * 0.3989422804014327
    active = (upper * half).astype(BF16)
    hand_out(rows_ref, group, place[0], active, active_refs)
    slope_ref[...] = (half + upper * bell).astype(BF16)
    stage_ref[...] = dot(active, cot_ref[...], TN).astype(BF16).reshape(stage_ref.shape)
    deal(
        stage_ref,
        place[1] % stage_ref.shape[0],
        [(ka_ref, sa_ref, 1, slice(0, cut)), (kb_ref, sb_ref, 0, slice(cut, None))],
    )


def feed_up(place, hidden, cotangent, up_arrays, up_blocks, upb_own, group, chips, cut, rows, after=()):
    length, width = hidden.shape
    ff = upb_own.shape[1]
    chunk = ff // chips
    tile = min(512 if length <= 1024 else 128, ff)
    parts = tile // chunk
    whole = pl.BlockSpec((length, width), lambda t, s: (0, 0), pipeline_mode=pl.Buffered(1))
    tiled = pl.BlockSpec((length, tile), lambda t, s: (0, t))
    number, specs = up_blocks(tile)

    def piece(columns):
        spec = pl.BlockSpec(
            (parts // 2, chunk, columns), lambda t, s: (jnp.bitwise_xor(t, s[1] // parts), 0, 0)
        )
        return ((chips // 2, chunk, columns), BF16, spec, PIN)

    return call(
        functools.partial(feed_up_kernel, number, group, cut),
        "feed_up",
        place,
        (hidden, cotangent, upb_own) + (up_arrays,) * number,
        (ff // tile,),
        [whole, whole, pl.BlockSpec((1, tile), lambda t, s: (0, t))] + specs,
        [
            (
                (length // group, ff),
                BF16,
                pl.BlockSpec((length // group, tile), lambda t, s: (0, t)),
            )
        ]
        * group
        + [((length, ff), BF16, tiled, length <= 1024)]
        + [piece(cut)] * 2
        + [piece(width - cut)] * 2,
        [pltpu.VMEM((parts, chunk, width), BF16), pltpu.VMEM((length // rows, rows, tile), BF16)],
        after=after,
    )


def feed_back_kernel(number, chips, split, place, ht_ref, cot_ref, slope_ref, down_ref, *refs):
    up_refs = refs[:number]
    dh_refs = refs[number : number + DH_PIECES]
    dub_ref, ka_ref, sa_ref, kb_ref, sb_ref, dh_sum, stage_ref = refs[number + DH_PIECES :]
    step = pl.program_id(0)
    up = jnp.concatenate([ref[...] for ref in up_refs], axis=1) if number > 1 else up_refs[0][...]
    down = down_ref[...]
    down = down.reshape(down.shape[0] * down.shape[2], down.shape[3])
    d_upper = (dot(cot_ref[...], down, NT) * slope_ref[...].astype(F32)).astype(BF16)
    dub_ref[...] = jnp.sum(d_upper.astype(F32), axis=0, keepdims=True)
    length = d_upper.shape[0]
    rows = min(1024, length)

    def add(start):
        part = dot(d_upper[start : start + rows], up, NT)

        @pl.when(step == 0)
        def _():
            dh_sum[start : start + rows] = part

        @pl.when(step > 0)
        def _():
            dh_sum[start : start + rows] += part

    for start in range(0, length, rows):
        add(start)

    rows = ht_ref.shape[0] // chips
    many = max(1, 256 // rows)
    for start in range(0, chips, many):
        grad = dot(ht_ref[start * rows : (start + many) * rows], d_upper).astype(BF16)
        stage_ref[start : start + many] = grad.reshape(many, rows, grad.shape[1])

    @pl.when(step < split)
    def _():
        deal(stage_ref, place[1], [(ka_ref, sa_ref, 1, slice(None))])

    @pl.when(step >= split)
    def _():
        deal(stage_ref, place[1], [(kb_ref, sb_ref, 0, slice(None))])

    @pl.when(step == pl.num_programs(0) - 1)
    def _():
        piece_rows = dh_refs[0].shape[0]
        for index, dh_ref in enumerate(dh_refs):
            dh_ref[...] = dh_sum[index * piece_rows : (index + 1) * piece_rows].astype(BF16)


def feed_back(
    place, hidden_t, cotangent, slope, down_weight, up_arrays, up_blocks, group, chips, share, after=()
):
    width, length = hidden_t.shape
    ff = slope.shape[1]
    chunk = ff // chips
    tile = min(512 if length <= 1024 else 128, ff)
    parts = tile // chunk
    number, specs = up_blocks(tile)
    tiles = ff // tile
    split = max(1, min(tiles - 1, round(tiles * share)))
    some = width // chips

    def piece(first, last, pin):
        spec = pl.BlockSpec(
            (chips // 2, some, tile), lambda t, s: (0, 0, jnp.clip(t, first, last - 1) - first)
        )
        return ((chips // 2, some, (last - first) * tile), BF16, spec, pin)

    return call(
        functools.partial(feed_back_kernel, number, chips, split),
        "feed_back",
        place,
        (hidden_t, cotangent, slope, down_weight.reshape(chips, group, chunk, width)) + (up_arrays,) * number,
        (ff // tile,),
        [
            pl.BlockSpec((width, length), lambda t, s: (0, 0), pipeline_mode=pl.Buffered(1)),
            pl.BlockSpec((length, width), lambda t, s: (0, 0), pipeline_mode=pl.Buffered(1)),
            pl.BlockSpec((length, tile), lambda t, s: (0, t)),
            pl.BlockSpec((parts, 1, chunk, width), lambda t, s: (t, s[0], 0, 0)),
        ]
        + specs,
        [
            ((length // DH_PIECES, width), BF16, pl.BlockSpec((length // DH_PIECES, width), lambda t, s: (0, 0)))
        ]
        * DH_PIECES
        + [((1, ff), F32, pl.BlockSpec((1, tile), lambda t, s: (0, t)))]
        + [piece(0, split, KEEP), piece(0, split, PIN)]
        + [piece(split, tiles, KEEP), piece(split, tiles, PIN)],
        [pltpu.VMEM((length, width), F32), pltpu.VMEM((chips, some, tile), BF16)],
        after=after,
    )


def feed_down_kernel(group, place, middle_ref, vec_ref, *refs):
    down_refs = refs[group : 2 * group]
    active_refs = refs[:group]
    near_ref, far_ref, sum_ref = refs[2 * group :]
    step = pl.program_id(0)
    total = None
    for active_ref, down_ref in zip(active_refs, down_refs):
        down = down_ref[...]
        part = dot(active_ref[...], down.reshape(-1, down.shape[3]))
        total = part if total is None else total + part

    @pl.when(step == 0)
    def _():
        sum_ref[...] = total

    @pl.when(step > 0)
    def _():
        sum_ref[...] += total

    @pl.when(step == pl.num_programs(0) - 1)
    def _():
        half = near_ref.shape[0]
        for start, out_ref in ((0, near_ref), (half, far_ref)):
            part = pl.ds(start, half)
            out_ref[...] = (middle_ref[part] + sum_ref[part] + vec_ref[5:6]).astype(BF16)


def feed_down(place, active_parts, down_weight, middle, vectors, chips, after=()):
    group = len(active_parts)
    rows, ff = active_parts[0].shape
    width = down_weight.shape[1]
    chunk = ff // chips
    tile = min(512, ff)
    out = ((rows // 2, width), BF16, pl.BlockSpec((rows // 2, width), lambda i, s: (0, 0)))
    return call(
        functools.partial(feed_down_kernel, group),
        "feed_down",
        place,
        (middle, vectors) + tuple(active_parts) + (down_weight.reshape(chips, group, chunk, width),) * group,
        (ff // tile,),
        [
            pl.BlockSpec((rows, width), lambda i, s: (0, 0)),
            pl.BlockSpec((8, width), lambda i, s: (0, 0)),
        ]
        + [pl.BlockSpec((rows, tile), lambda i, s: (0, i))] * group
        + [
            pl.BlockSpec(
                (tile // chunk, 1, chunk, width),
                functools.partial(lambda t, i, s: (i, (s[0] + group - t) % group, 0, 0), steps),
            )
            for steps in range(group)
        ],
        [out, out],
        [pltpu.VMEM((rows, width), F32)],
        after=after,
    )


def middle_back_kernel(group, span, turn, place, middle_ref, cot_ref, vec_ref, weight_ref, *refs):
    part_refs = refs[: group * DH_PIECES]
    branch_ref, d_middle_ref, d_mixed_ref, sums_ref, sum_ref = refs[group * DH_PIECES :]
    step = pl.program_id(0)

    def gather(piece):
        @pl.when(step // span == piece)
        def _():
            total = part_refs[piece * group][...].astype(F32)
            for ref in part_refs[piece * group + 1 : (piece + 1) * group]:
                total = total + ref[...].astype(F32)
            sum_ref[...] = total

    for piece in range(DH_PIECES):
        gather(piece)
    d_hidden = sum_ref[...]
    normal, inverse = norm_parts(middle_ref[...])
    d_middle = cot_ref[...].astype(F32) + norm_back(d_hidden, normal, inverse, vec_ref[2:3])
    branch = d_middle.astype(BF16)
    branch_ref[...] = branch

    @pl.when(step // turn % group == place[0])
    def _():
        d_middle_ref[...] = d_middle

    d_mixed_ref[...] = dot(branch, weight_ref[...], NT).astype(BF16)
    sums = jnp.concatenate(
        [
            jnp.sum(d_hidden * normal, axis=0, keepdims=True),
            jnp.sum(d_hidden, axis=0, keepdims=True),
            jnp.sum(branch.astype(F32), axis=0, keepdims=True),
            jnp.zeros((5, branch.shape[1]), F32),
        ],
        axis=0,
    )

    @pl.when(step == 0)
    def _():
        sums_ref[...] = sums

    @pl.when(step > 0)
    def _():
        sums_ref[...] += sums


def middle_back(place, middle, cotangent, vectors, out_weight, parts, slice_rows, after=()):
    length, width = middle.shape
    group = len(parts[0])
    own = width // group
    rows = min(256, length // DH_PIECES, slice_rows)
    turn = slice_rows // rows
    span = length // DH_PIECES // rows
    row = pl.BlockSpec((rows, width), lambda i, s: (i, 0))
    specs = [
        pl.BlockSpec(
            (rows, width), functools.partial(lambda k, i, s: (jnp.clip(i - k * span, 0, span - 1), 0), piece)
        )
        for piece in range(DH_PIECES)
        for _ in range(group)
    ]
    return call(
        functools.partial(middle_back_kernel, group, span, turn),
        "middle_back",
        place,
        (middle, cotangent, vectors, out_weight) + tuple(array for piece in parts for array in piece),
        (length // rows,),
        [
            row,
            row,
            pl.BlockSpec((8, width), lambda i, s: (0, 0)),
            pl.BlockSpec((own, width), lambda i, s: (s[0], 0)),
        ]
        + specs,
        [
            ((length, width), BF16, row, length <= 1024),
            (
                (length // group, width),
                F32,
                pl.BlockSpec((rows, width), lambda i, s: (i // (turn * group) * turn + i % turn, 0)),
            ),
            ((length, own), BF16, pl.BlockSpec((rows, own), lambda i, s: (i, 0)), length <= 1024),
            ((8, width), F32, pl.BlockSpec((8, width), lambda i, s: (0, 0))),
        ],
        [pltpu.VMEM((rows, width), F32)],
        after=after,
    )


def attention_grads(group, calls, chips, cut, earlier, place, side_ref, stage_ref, rows_ref, ht_ref, *refs):
    number = group * calls
    mixed_refs = refs[1 : 1 + number]
    outs = refs[1 + number :] if calls else refs
    if earlier:
        before_refs, outs = outs[:group], outs[group:]
        for before_ref, out_ref in zip(before_refs, outs):
            out_ref[:, : before_ref.shape[1]] = before_ref[...]
    side_refs = outs[:group]
    piece_refs = outs[group:]
    offset = 0
    if calls:
        branch = refs[0][...]
        offset = branch.shape[1]
        share = chips // number
        for index, mixed_ref in enumerate(mixed_refs):
            owner = ((place[0] + group - index % group) % group) * calls + index // group
            grad = dot(mixed_ref[...], branch, TN).astype(BF16)
            rows = grad.shape[0] // share
            stage_ref[pl.ds(owner * share, share), :, :offset] = grad.reshape(share, rows, offset)
    side = side_ref[...]
    hand_out(rows_ref, group, place[0], side, side_refs)
    rows = ht_ref.shape[0] // chips
    many = max(1, 256 // rows)
    for start in range(0, chips, many):
        grad = dot(ht_ref[start * rows : (start + many) * rows], side).astype(BF16)
        stage_ref[start : start + many, :, offset:] = grad.reshape(many, rows, grad.shape[1])
    columns = stage_ref.shape[2]
    for relative in range(chips):
        values = stage_ref[jnp.bitwise_xor(jnp.int32(relative), place[1])]
        if len(piece_refs) > 2:
            piece_refs[bool(relative & 2)][without_bit(relative, 1)] = values[:, :cut]
        piece_refs[(relative & 1) - 2][without_bit(relative, 0)] = values[:, cut % columns :]


def hidden_back_kernel(number, side_spot, share, place, x_ref, base_ref, vec_ref, *refs):
    side_refs = refs[:number]
    weight_refs = refs[number : number + 3]
    small_refs = refs[number + 3 : number + 5]
    near_ref, far_ref, sums_ref, sum_ref = refs[number + 5 :]
    step = pl.program_id(0)
    each = side_refs[0].shape[1] // 3
    half = near_ref.shape[0]

    @pl.when(step == 0)
    def _():
        sum_ref[...] = jnp.zeros_like(sum_ref)
        sums_ref[...] = jnp.zeros_like(sums_ref)

    def add(index):
        @pl.when(step == index)
        def _():
            side = side_refs[index][...]
            row_sums = jnp.sum(side.astype(F32), axis=0, keepdims=True)
            spot = pl.ds(pl.multiple_of(side_spot(index, place) * each, each), each)
            sums_ref[2:3, spot] = row_sums[:, :each]
            sums_ref[3:4, spot] = row_sums[:, 2 * each :]
            total = None
            for third, weight_ref in enumerate(weight_refs):
                part = dot(side[:, third * each : (third + 1) * each], weight_ref[...], NT)
                total = part if total is None else total + part
            sum_ref[...] += total

    for index in range(number):
        add(index)

    @pl.when(step == number - 1)
    def _():
        sums = []
        for start, out_ref, block in ((0, near_ref, 0), (half, far_ref, x_ref.shape[0] // 2)):
            total = sum_ref[start : start + half]
            rows = x_ref[block : block + x_ref.shape[0] // 2].reshape(total.shape)
            normal, inverse = norm_parts(rows.astype(F32))
            sums.append(jnp.sum(total * normal, axis=0, keepdims=True))
            sums.append(jnp.sum(total, axis=0, keepdims=True))
            result = base_ref[start : start + half] + norm_back(total, normal, inverse, vec_ref[0:1])
            out_ref[...] = result.astype(BF16)
        sums_ref[0:1] = sums[0] + sums[2]
        sums_ref[1:2] = sums[1] + sums[3]
        sums_ref[4:5] = small_refs[0][2:3] * share
        sums_ref[5:7] = small_refs[0][0:2] * share
        sums_ref[7:8] = small_refs[1][0:1] * share


def hidden_back(
    place, x_rows, d_middle, vectors, sides, calls, qkv_weight, sums, cot_sums, slice_rows, after=()
):
    group = len(sides)
    rows, columns = sides[0].shape
    columns = columns // calls
    each = columns // 3
    length, width = x_rows.shape
    slices = length // group // slice_rows
    whole = pl.BlockSpec((rows, width), lambda i, s: (0, 0))
    count = calls * group
    eight = pl.BlockSpec((8, width), lambda i, s: (0, 0))

    def side_spot(index, numbers):
        return ((numbers[0] + group - index % group) % group) * calls + index // group

    weights = [
        pl.BlockSpec(
            (width, each),
            functools.partial(lambda third, i, s: (0, third * group * calls + side_spot(i, s)), third),
        )
        for third in range(3)
    ]
    out = ((rows // 2, width), BF16, pl.BlockSpec((rows // 2, width), lambda i, s: (0, 0)))
    return call(
        functools.partial(hidden_back_kernel, count, side_spot, 1.0 / group),
        "hidden_back",
        place,
        (x_rows.reshape(slices, group, slice_rows, width), d_middle, vectors)
        + tuple(sides) * calls
        + (qkv_weight,) * 3
        + (sums, cot_sums),
        (count,),
        [
            pl.BlockSpec((slices, 1, slice_rows, width), lambda i, s: (0, s[0], 0, 0)),
            whole,
            pl.BlockSpec((8, width), lambda i, s: (0, 0)),
        ]
        + [
            pl.BlockSpec((rows, columns), functools.partial(lambda j, i, s: (0, j), index // group))
            for index in range(count)
        ]
        + weights
        + [eight, eight],
        [out, out, ((8, width), F32, pl.BlockSpec((8, width), lambda i, s: (0, 0)))],
        [pltpu.VMEM((rows, width), F32)],
        after=after,
    )


def join_kernel(place, near_ref, far_ref, out_ref):
    half = place[1] % 2
    out_ref[half, 0] = near_ref[...]
    out_ref[1 - half, 0] = far_ref[...]


def join(place, near, far, after=()):
    shape = (2, 1) + near.shape
    whole = pl.BlockSpec(near.shape, lambda i, s: (0, 0))
    return call(
        join_kernel,
        "join",
        place,
        (near, far),
        (1,),
        [whole, whole],
        [(shape, BF16, pl.BlockSpec(shape, lambda i, s: (0, 0, 0, 0)))],
        after=after,
    )[0]


def later(place, array, after):
    return call(
        lambda place_ref, out_ref: None,
        "later",
        place,
        (),
        (1,),
        [],
        [(array.shape, array.dtype, pl.BlockSpec(memory_space=pl.ANY))],
        after=after,
        fill=[array],
    )[0]


def part_kernel(counts, takes, whole, place, *refs):
    sources = []
    for count in counts:
        sources.append(refs[:count])
        refs = refs[count:]
    own_ref, send_ref = refs[:2]
    rows = own_ref.shape[0]
    mine = place[0] == 0
    start = 0

    def total(index, first, count):
        part = pl.ds(first, count)
        if len(sources[index]) == 1:
            return sources[index][0][part]
        return sources[index][0][0, part].astype(F32) + sources[index][1][0, part].astype(F32)

    for index, first in takes:
        both = total(index, first, 2 * rows)
        columns = both.shape[1]
        own_ref[:, start : start + columns] = jnp.where(mine, both[:rows], both[rows:])
        send_ref[:, start : start + columns] = jnp.where(mine, both[rows:], both[:rows]).astype(BF16)
        start += columns
    out_ref = refs[2]
    start = 0
    for index, first in whole:
        value = total(index, first, out_ref.shape[0])
        out_ref[:, start : start + value.shape[1]] = value
        start += value.shape[1]


def part_rows(place, sources, takes, rows, whole, whole_rows, after=()):
    columns = sum(sources[index][0].shape[-1] for index, _ in takes)
    out = pl.BlockSpec((rows, columns), lambda i, s: (0, 0))
    shape = (whole_rows, sum(sources[index][0].shape[-1] for index, _ in whole))
    arrays = [array for parts in sources for array in parts]
    return call(
        functools.partial(part_kernel, [len(parts) for parts in sources], takes, whole),
        "part_rows",
        place,
        tuple(arrays),
        (1,),
        [
            pl.BlockSpec(array.shape, functools.partial(lambda n, i, s: (0,) * n, array.ndim))
            for array in arrays
        ],
        [
            ((rows, columns), F32, out),
            ((rows, columns), BF16, out),
            (shape, F32, pl.BlockSpec(shape, lambda i, s: (0, 0))),
        ],
        after=after,
    )


def emit_kernel(moves, place, own_ref, came_ref, *out_refs):
    member = place[0]
    for source, size, out, column, stride in moves:
        for ref, who in ((own_ref, member), (came_ref, 1 - member)):
            spot = pl.ds(pl.multiple_of(column + who * stride, 128), size)
            out_refs[out][:, spot] = ref[:, source : source + size].astype(F32)


def emit(place, own, came, moves, widths, after=()):
    rows, columns = own.shape
    block = pl.BlockSpec((rows, columns), lambda i, s: (0, 0))
    return call(
        functools.partial(emit_kernel, moves),
        "emit",
        place,
        (own, came),
        (1,),
        [block, block],
        [((rows, width), F32, pl.BlockSpec((rows, width), lambda i, s: (0, 0))) for width in widths],
        after=after,
    )


def body(
    inputs,
    cotangent,
    image_lengths,
    norm1_gain,
    norm1_bias,
    qkv_weight,
    qv_bias,
    out_weight,
    out_bias,
    norm2_gain,
    norm2_bias,
    up_weight,
    up_bias,
    down_weight,
    down_bias,
):
    rows, width = inputs.shape[2:]
    limit = image_lengths.shape[-1]
    ff = up_weight.shape[1]
    dp_size = lax.axis_size("dp")
    ctx_size = lax.axis_size("ctx")
    group = ctx_size // 2
    dp_index = lax.axis_index("dp")
    ctx_index = lax.axis_index("ctx")
    half = ctx_index // group
    member = ctx_index % group
    length = rows * ctx_size
    chips = dp_size * 2
    dp_bits = dp_size.bit_length() - 1
    own_width = width // group
    own_ff = ff // group
    chunk = own_ff // chips
    place = Place(jnp.stack([member, dp_index * 2 + half]).astype(jnp.int32), length > 1024)

    def moved(value):
        place.free.append(value)
        return value

    def across(value):
        pairs = [(i, (i + group) % ctx_size) for i in range(ctx_size)]
        return moved(lax.ppermute(value, "ctx", pairs))

    def around(value, steps):
        pairs = [
            (h * group + g, h * group + (g + steps) % group) for h in range(2) for g in range(group)
        ]
        return moved(lax.ppermute(value, "ctx", pairs))

    def all_around(value):
        return [value] + [around(value, steps) for steps in range(1, group)]

    def in_order(parts, axis=0):
        if group == 2:
            first = member == 0
            return jnp.stack(
                [jnp.where(first, parts[0], parts[1]), jnp.where(first, parts[1], parts[0])], axis=axis
            )
        return jnp.roll(jnp.stack(parts[::-1], axis=axis), member + 1, axis=axis)

    def gather(value):
        return in_order(all_around(value))

    def pick(value, index, axis):
        return lax.dynamic_index_in_dim(value, index, axis, keepdims=False)

    def group_sum_scatter(value, axis):
        total = pick(value, member, axis).astype(F32)
        for steps in range(1, group):
            total = total + around(pick(value, (member + steps) % group, axis), steps).astype(F32)
        return total

    def swap_bit(value, bit):
        if bit < 0:
            return across(value)
        return moved(lax.ppermute(value, "dp", [(i, i ^ (1 << bit)) for i in range(dp_size)]))

    all_bits = list(range(dp_bits - 1, -1, -1)) + [-1]
    rest_bits = list(range(1, dp_bits))

    class Halving:
        def __init__(self, keep, send, bits, order, then=()):
            self.order = list(order)
            self.then = then
            self.left = list(bits)
            self.keep = keep
            self.came = swap_bit(send, self.order[0])
            if not place.long:
                place.pinned.append(self.came)
            self.order.pop(0)

    def crossed(pieces):
        first = [bit for bit in all_bits if bit != 0]
        second = [bit for bit in all_bits if bit != -1]
        return [
            Halving(*pieces[:2], first, [0] + rest_bits, (-1, 0)),
            Halving(*pieces[2:], second, [-1] + rest_bits, (-1, 0)),
        ]

    def pair(pieces):
        first = [bit for bit in all_bits if bit != 0]
        second = [bit for bit in all_bits if bit != -1]
        return [
            Halving(*pieces[:2], first, [0, -1] + rest_bits),
            Halving(*pieces[2:], second, [-1, 0] + rest_bits),
        ]

    def lone(pieces):
        return Halving(*pieces, [bit for bit in all_bits if bit != -1], [-1, 0] + rest_bits)

    state = {}

    def go(after, *names):
        jobs = []
        counts = []
        for name in names:
            item = state[name]
            if isinstance(item, list) and item[0].order[:1] != item[1].order[:1]:
                jobs += [[item[0]], [item[1]]]
                counts.append(2)
            else:
                jobs.append(item if isinstance(item, list) else [item])
                counts.append(1)
        ready, results = step(after, *jobs, cost=COST)
        for name, count in zip(names, counts):
            state[name] = [results.pop(0), results.pop(0)] if count == 2 else results.pop(0)
        return ready

    def step(after, *jobs, cost=0):
        asked = []
        for halvings in jobs:
            first = halvings[0]
            arrays = [array for halving in halvings for array in (halving.keep, halving.came)]
            if first.order:
                asked.append((arrays, len(first.left) - 1 - first.left.index(first.order[0]), 1))
            elif first.then:
                asked.append((arrays, 0, 2))
            else:
                asked.append((arrays, None, 1))
        sums = list(step_call(place, asked, after, cost))
        ready = sums[:1]
        results = []
        for halvings in jobs:
            first = halvings[0]
            if first.order:
                left = [bit for bit in first.left if bit != first.order[0]]
                results.append(Halving(sums.pop(0), sums.pop(0), left, first.order, first.then))
            elif first.then:
                results.append([Halving(sums.pop(0), sums.pop(0), [], [bit]) for bit in first.then])
            else:
                results.append(sums.pop(0))
        return ready, results

    slices = 2 if group > 2 else 1
    slice_rows = rows // slices

    def sliced(value):
        return [value[c * slice_rows : (c + 1) * slice_rows] for c in range(slices)]

    own_inputs = pick(inputs, half, 0)[0]
    far_inputs = across(pick(inputs, 1 - half, 0)[0])
    vectors = jnp.stack([norm1_gain, norm1_bias, norm2_gain, norm2_bias, out_bias, down_bias, out_bias, out_bias])
    vectors = vectors.astype(F32)
    filled = ()
    for side, both_of in enumerate((own_inputs, far_inputs)):
        if filled:
            both_of = later(place, both_of, filled[3:4])
        for c, part in enumerate(sliced(both_of)):
            start = (side * slices + c) * (length // (2 * slices))
            copied = cotangent if side == 1 and c == 0 else None
            filled = project(
                place, all_around(part), start, length, vectors, qkv_weight, qv_bias, filled, copied
            )
            if copied is not None:
                *filled, own_cot, far_cot = filled
    x_rows, hidden1_t, query, keys, values = filled
    cot_parts = [part for value in sliced(own_cot) for part in all_around(value)]
    far_cot = across(far_cot)
    cot_parts += [part for value in sliced(far_cot) for part in all_around(value)]

    spots = jnp.arange(length, dtype=jnp.int32).reshape(2, group, slices, rows // slices)
    spots = jnp.swapaxes(spots, 1, 2)
    positions = jnp.where(half == 0, spots, spots[::-1]).reshape(length)
    ends = jnp.cumsum(pick(image_lengths, half, 0)[0])
    segment = jnp.sum((positions[:, None] >= ends[None, :]).astype(jnp.int32), axis=1)
    seg_row = segment.reshape(1, length)
    seg_cols = jnp.broadcast_to(segment[:, None], (length, PAIR))

    if chunk % 128 == 0:
        up_arrays = up_weight

        def up_blocks(tile):
            return tile // chunk, up_specs(width, tile, chunk, group, tile // chunk)

    else:
        up_arrays = pick(up_weight.reshape(width, chips, group, chunk), member, 2).reshape(width, own_ff)

        def up_blocks(tile):
            return 1, [pl.BlockSpec((width, tile), lambda t, s: (0, t))]

    upb_own = pick(up_bias.reshape(chips, group, chunk), member, 1).reshape(1, own_ff)

    pairs = own_width // PAIR
    calls = min(2, pairs)
    each = pairs // calls
    mixed, logs = attend(place, 0, pairs, query, keys, values, seg_cols, seg_row, limit)
    mixed_parts = [all_around(mixed)]
    cot_rows, cot_sums = collect(place, cot_parts, group, after=[mixed])
    middle, middle_own, hidden2, hidden2_t = close(
        place, x_rows, mixed_parts, group, out_weight, vectors, slice_rows, after=[cot_rows]
    )
    up_out = feed_up(
        place,
        hidden2,
        cot_rows,
        up_arrays,
        up_blocks,
        upb_own,
        group,
        chips,
        width // 2,
        slice_rows,
    )
    active_parts = up_out[:group]
    slope, *down_pieces = up_out[group:]
    active_parts = [active_parts[0]] + [around(active_parts[steps], steps) for steps in range(1, group)]
    state["down"] = crossed(down_pieces)
    back = feed_back(
        place,
        hidden2_t,
        cot_rows,
        slope,
        down_weight,
        up_arrays,
        up_blocks,
        group,
        chips,
        0.5,
        after=down_pieces[:1],
    )
    dh_pieces = back[:DH_PIECES]
    upb_grad, *up_pieces = back[DH_PIECES:]
    dh_parts = [all_around(piece) for piece in dh_pieces]
    state["up"] = pair(up_pieces)

    ready = go(dh_pieces[:1], "down")
    branch, d_middle, d_mixed, sums = middle_back(
        place, middle, cot_rows, vectors, out_weight, dh_parts, slice_rows, after=ready
    )

    out_near, out_far = feed_down(place, active_parts, down_weight, middle_own, vectors, chips, after=[branch])
    out_far = across(out_far)

    def back_of(j, earlier, after):
        results = attend_back(
            place,
            j * each,
            each,
            query,
            keys,
            values,
            d_mixed,
            mixed,
            logs,
            seg_cols,
            seg_row,
            limit,
            hidden1_t,
            group,
            chips,
            slice_rows,
            branch if j == 0 else None,
            mixed_parts if j == 0 else (),
            earlier,
            after=after,
        )
        pieces = results[group:]
        halvings = pair(pieces) if len(pieces) > 2 else [lone(pieces)]
        halvings = halvings if len(halvings) > 1 else halvings[0]
        return halvings, list(results[:group]), list(results[:1])

    state["early"], sides, ready = back_of(0, [], [out_near])
    block_output = join(place, out_near, out_far, after=ready)
    ready = [block_output]
    ready = go(ready, "down", "up")
    if calls > 1:
        state["late"], sides, ready = back_of(1, sides, ready)
    else:
        state["late"] = state.pop("early")
    others = [name for name in ("early",) if name in state]
    sides = [sides[0]] + [around(sides[steps], steps) for steps in range(1, group)]
    ready = go(ready, "up", "down", *others)
    input_near, input_far, own_sums = hidden_back(
        place, x_rows, d_middle, vectors, sides, calls, qkv_weight, sums, cot_sums, slice_rows, after=ready
    )
    ready = go([input_near], "late", "up", *others)

    own = width // (chips * group)
    member_is = (jnp.arange(group, dtype=jnp.int32) == member).astype(F32)
    small = jnp.transpose(own_sums.reshape(8, chips * group, own), (1, 0, 2)).reshape(chips * group, 8 * own)
    upb_full = (upb_grad.reshape(chips, 1, chunk) * member_is[None, :, None]).reshape(chips * group, chunk)
    small = jnp.concatenate([small, upb_full], axis=1)
    small = lax.all_to_all(small, ("dp", "ctx"), 0, 0, tiled=True)
    small = jnp.sum(small, axis=0)
    small_rows = small[: 8 * own].reshape(8, own)
    upb_out = small[8 * own :]

    input_far = across(input_far)
    ready = go(ready, "late", "up", *others)
    input_grad = join(place, input_near, input_far, after=ready)
    ready = [input_grad]

    def waits(item):
        return isinstance(item, Halving) and (item.order or item.then)

    while any(waits(item) for item in state.values()):
        ready = go(ready, *[name for name in state if waits(state[name])])

    some = width // chips

    def exchange(value):
        value = value.reshape(group, own, value.shape[1])
        parts = [pick(value, member, 0)] + [
            around(pick(value, (member + steps) % group, 0).astype(BF16), steps).astype(F32)
            for steps in range(1, group)
        ]
        return in_order(parts, 1)

    def parts_of(item):
        return [item.keep, item.came] if isinstance(item, Halving) else [item]

    def sums_in(item):
        parts = parts_of(item)
        return parts[0] if len(parts) == 1 else parts[0][0].astype(F32) + parts[1][0].astype(F32)

    rest = others + ["late"]
    if group == 2 and own % 16 == 0:
        sources = [parts_of(item) for item in state["down"] + [state[name] for name in ["up"] + rest]]
        own_rows, send_rows, down_out = part_rows(
            place,
            sources,
            [(2, k * some) for k in range(own_ff // sources[2][0].shape[-1])]
            + [
                (index, first)
                for index in range(3, len(sources))
                for first in range(0, sources[index][0].shape[-2], some)
            ],
            own,
            [(0, 0), (1, 0)],
            chunk,
            ready,
        )
        moves = [(k * chunk, chunk, 0, k * 2 * chunk, chunk) for k in range(chips)]
        moves += [(own_ff, own_width, 1, 0, own_width)]
        moves += [
            (own_ff + own_width + (j * 3 + t) * each * PAIR, each * PAIR, 2, t * width + j * each * PAIR, own_width)
            for j in range(calls)
            for t in range(3)
        ]
        up_out, out_out, qkv_out = emit(place, own_rows, around(send_rows, 1), moves, [ff, width, 3 * width])
    else:

        def blocks_of(value, rows):
            return [value[start : start + rows] for start in range(0, value.shape[0], rows)]

        down_out = jnp.concatenate([sums_in(item) for item in state["down"]], axis=1)
        up_out = jnp.concatenate(blocks_of(sums_in(state["up"]), some), axis=1)
        up_out = exchange(up_out).reshape(own, group, chips, chunk)
        up_out = jnp.swapaxes(up_out, 1, 2).reshape(own, ff)
        parts = [part for name in rest for part in blocks_of(sums_in(state[name]), some)]
        rest = exchange(jnp.concatenate(parts, axis=1))
        out_out = rest[:, :, :own_width].reshape(own, width)
        qkv_out = rest[:, :, own_width:].reshape(own, group, calls, 3, each * PAIR)
        qkv_out = jnp.transpose(qkv_out, (0, 3, 1, 2, 4)).reshape(own, 3 * width)
    return (
        block_output,
        input_grad,
        small_rows[0],
        small_rows[1],
        qkv_out,
        small_rows[2:4],
        out_out,
        small_rows[4],
        small_rows[5],
        small_rows[6],
        up_out,
        upb_out,
        down_out,
        small_rows[7],
    )


def solution(mesh):
    split = P(None, "dp", "ctx", None)
    both = ("dp", "ctx")
    return jax.shard_map(
        body,
        mesh=mesh,
        in_specs=(split, split, P(None, "dp", None)) + (P(),) * 12,
        out_specs=(
            split,
            split,
            P(both),
            P(both),
            P(both, None),
            P(None, both),
            P(both, None),
            P(both),
            P(both),
            P(both),
            P(both, None),
            P(both),
            P(both, None),
            P(both),
        ),
        check_vma=False,
    )
```

```python
import functools

import jax
import jax.numpy as jnp
from jax import lax
from jax.experimental import pallas as pl
from jax.experimental.pallas import tpu as pltpu
from jax.sharding import PartitionSpec as P

HEADS = 16
HIDES = {"step": 20, "attend": 40, "project": 6}
HEAD_DIM = 64
PAIR = 2 * HEAD_DIM
NEG = -1e30
EPS = 1e-06
LOG2E = 1.4426950408889634
SCALE = HEAD_DIM ** (-0.5)
BF16 = jnp.bfloat16
F32 = jnp.float32
VMEM = 60 * 1024 * 1024
LESS_VMEM = 26 * 1024 * 1024
DH_PIECES = 1
PIN = True
KEEP = False
COST = 6 * 1150 * 1000 * 1000

NT = (((1,), (1,)), ((), ()))
NN = (((1,), (0,)), ((), ()))
TN = (((0,), (0,)), ((), ()))


def dot(left, right, dims=NN):
    return lax.dot_general(left, right, dims, preferred_element_type=F32)


def call(kernel, name, place, args, grid, in_specs, outs, scratch=(), after=(), fill=(), lazy=(), cost=0):
    known = len(args)
    skipped = len(after) + len(fill)
    slow = len(lazy)
    stays = [len(out) > 3 and out[3] and not place.long for out in outs]

    def settled(array):
        pinned = any(array is other for other in place.pinned)
        if not pinned and any(array is other for other in place.free):
            return array
        return pltpu.with_memory_space_constraint(array, pltpu.VMEM if pinned else pltpu.HBM)

    def inner(place_ref, *refs):
        known_refs = refs[:known]
        sources = refs[known : known + slow]
        rest = refs[known + slow + skipped :]
        if not slow:
            kernel(place_ref, *known_refs, *rest)
            return
        buffers = rest[len(rest) - slow - 1 : -1]
        sems = rest[-1]
        copies = []
        for index, (source, buffer) in enumerate(zip(sources, buffers)):
            source = lazy[index][1](source, place_ref)
            copies.append(pltpu.make_async_copy(source, buffer, sems.at[index]))
        first = last = True
        for axis, size in enumerate(grid):
            first = first & (pl.program_id(axis) == 0)
            last = last & (pl.program_id(axis) == size - 1)

        @pl.when(first)
        def _():
            for copy in copies:
                copy.start()

        def arrive():
            for copy in copies:
                copy.wait()

        kernel(place_ref, *known_refs, *rest[: len(rest) - slow - 1], lazy=(arrive, buffers))

    anywhere = pl.BlockSpec(memory_space=pl.ANY)
    first = 1 + known + slow + len(after)
    results = pl.pallas_call(
        inner,
        grid_spec=pltpu.PrefetchScalarGridSpec(
            num_scalar_prefetch=1,
            grid=grid,
            in_specs=list(in_specs) + [anywhere] * (slow + skipped),
            out_specs=[out[2] for out in outs],
            scratch_shapes=list(scratch)
            + [pltpu.VMEM(shape, array.dtype) for array, _, shape in lazy]
            + ([pltpu.SemaphoreType.DMA((slow,))] if slow else []),
        ),
        out_shape=[(pltpu.VMEM if stay else pltpu.HBM)(out[0], out[1]) for out, stay in zip(outs, stays)],
        input_output_aliases={first + index: index for index in range(len(fill))},
        compiler_params=pltpu.CompilerParams(vmem_limit_bytes=VMEM if place.long else LESS_VMEM),
        cost_estimate=pl.CostEstimate(flops=int(1.15e9 * HIDES.get(name, 0)), bytes_accessed=0, transcendentals=0),
        name=name,
    )(place.numbers, *[settled(array) for array in (*args, *[array for array, _, _ in lazy], *after, *fill)])
    place.pinned += [array for array, stay in zip(results, stays) if stay]
    return results


class Place:
    def __init__(self, numbers, long):
        self.numbers = numbers
        self.long = long
        self.pinned = []
        self.free = []


def without_bit(number, spot):
    return ((number >> (spot + 1)) << spot) | (number & ((1 << spot) - 1))


def deal(stage_ref, me, pieces):
    for relative in range(stage_ref.shape[0]):
        rows = stage_ref[jnp.bitwise_xor(jnp.int32(relative), me)]
        for keep_ref, send_ref, bit, columns in pieces:
            target = send_ref if (relative >> bit) & 1 else keep_ref
            target[without_bit(relative, bit)] = rows[:, columns]


def norm_parts(values):
    centred = values - jnp.mean(values, axis=-1, keepdims=True)
    inverse = lax.rsqrt(jnp.mean(centred * centred, axis=-1, keepdims=True) + EPS)
    return centred * inverse, inverse


def norm_back(grad, normal, inverse, gain):
    scaled = grad * gain
    inner = (
        scaled
        - jnp.mean(scaled, axis=-1, keepdims=True)
        - normal * jnp.mean(scaled * normal, axis=-1, keepdims=True)
    )
    return inverse * inner


def step_kernel(jobs, place, *refs):
    ins = sum(len(layout) for _, layout, _ in jobs) * 2
    sources = refs[:ins]
    targets = refs[ins:]
    for spot, layout, parts in jobs:
        if spot is None:
            old_ref, came_ref = sources[:2]
            sources = sources[2:]
            targets[0][...] = old_ref[0].astype(F32) + came_ref[0].astype(F32)
            targets = targets[1:]
            continue
        if spot < 0:
            base = 0
            for rows, _ in layout:
                old_ref, came_ref = sources[:2]
                sources = sources[2:]
                for number in range(old_ref.shape[0]):
                    value = old_ref[number].astype(F32) + came_ref[number].astype(F32)
                    target = targets[number // -spot]
                    target[number % -spot, base : base + rows] = value.astype(target.dtype)
                base += rows
            targets = targets[old_ref.shape[0] // -spot :]
            continue
        if parts == 2:
            terms = sources[: 2 * len(layout)]
            sources = sources[2 * len(layout) :]
            for index in range(2):
                rows = pl.ds(index * targets[0].shape[1], targets[0].shape[1])
                for number in range(terms[0].shape[0]):
                    value = sum(term[number, rows].astype(F32) for term in terms)
                    target = targets[(number >> spot) & 1]
                    target[without_bit(number, spot)] = value.astype(target.dtype)
                targets = targets[2:]
            continue
        keep_ref, send_ref = targets[:2]
        targets = targets[2:]
        columns = keep_ref.shape[2]
        base = 0
        for rows, width in layout:
            old_ref, came_ref = sources[:2]
            sources = sources[2:]
            for number in range(old_ref.shape[0]):
                value = (old_ref[number].astype(F32) + came_ref[number].astype(F32)).astype(keep_ref.dtype)
                target = send_ref if (number >> spot) & 1 else keep_ref
                spare = without_bit(number, spot)
                for part in range(width // columns):
                    start = base + part * rows
                    target[spare, start : start + rows] = value[:, part * columns : (part + 1) * columns]
            base += rows * (width // columns)


def step_call(place, jobs, after=(), cost=0):
    ins = []
    outs = []
    layouts = []
    for arrays, spot, parts in jobs:
        columns = min(array.shape[2] for array in arrays)
        layout = [array.shape[1:] for array in arrays[::2]]
        if spot is None:
            layouts.append((None, layout, 1))
            ins += arrays
            outs.append((layout[0], F32, pl.BlockSpec(layout[0], lambda i, s: (0, 0))))
            continue
        rows = sum(rows * (width // columns) for rows, width in layout)
        if parts == 2:
            rows = arrays[0].shape[1]
        if spot < 0:
            shape = (-spot, rows, columns)
            spec = pl.BlockSpec(shape, lambda i, s: (0, 0, 0))
            layouts.append((spot, layout, 1))
            ins += arrays
            outs += [(shape, arrays[0].dtype, spec, KEEP)]
            outs += [(shape, arrays[0].dtype, spec, PIN)] * (arrays[0].shape[0] // -spot - 1)
            continue
        shape = (arrays[0].shape[0] // 2, rows // parts, columns)
        layouts.append((spot, layout, parts))
        ins += arrays
        spec = pl.BlockSpec(shape, lambda i, s: (0, 0, 0))
        outs += [(shape, arrays[0].dtype, spec, KEEP), (shape, arrays[0].dtype, spec, PIN)] * parts
    return call(
        functools.partial(step_kernel, layouts),
        "step",
        place,
        tuple(ins),
        (1,),
        [pl.BlockSpec(array.shape, lambda i, s: (0, 0, 0)) for array in ins],
        outs,
        after=after,
        cost=cost,
    )


def hand_out(stage_ref, group, member, value, out_refs):
    rows = stage_ref.shape[1]
    stage_ref[...] = value.reshape(stage_ref.shape)
    for steps, out_ref in enumerate(out_refs):
        first = out_ref.shape[1] - stage_ref.shape[2]
        for block in range(stage_ref.shape[0] // group):
            part = stage_ref[block * group + (member + steps) % group]
            out_ref[block * rows : (block + 1) * rows, first:] = part


def project_kernel(group, copies, place, *refs):
    part_refs = refs[:group]
    vec_ref, wq_ref, wk_ref, wv_ref, qvb_ref = refs[group : group + 5]
    refs = refs[group + 5 :]
    if copies:
        refs[-2][...] = refs[0][...].reshape(refs[-2].shape)
        refs[-1][...] = refs[1][...].reshape(refs[-1].shape)
        refs = refs[2:-2]
    x_ref, ht_ref, q_ref, k_ref, v_ref = refs
    gain = vec_ref[0:1]
    shift = vec_ref[1:2]
    qvb = qvb_ref[...].astype(F32)
    rows = part_refs[0].shape[0]
    for steps, part_ref in enumerate(part_refs):
        base = ((place[0] + group - steps) % group) * rows
        spot = pl.ds(pl.multiple_of(base, rows), rows)
        values = part_ref[...]
        x_ref[spot] = values
        normal, _ = norm_parts(values.astype(F32))
        hidden = (normal * gain + shift).astype(BF16)
        ht_ref[:, spot] = hidden.T
        q_ref[spot] = (dot(hidden, wq_ref[...]) + qvb[0:1]).astype(BF16)
        k_ref[spot] = dot(hidden, wk_ref[...]).astype(BF16)
        v_ref[spot] = (dot(hidden, wv_ref[...]) + qvb[1:2]).astype(BF16)


def project(place, parts, first_row, length, vectors, qkv_weight, qv_bias, fill, copied=None):
    group = len(parts)
    rows, width = parts[0].shape
    own = width // group
    rows = rows * group
    index = first_row // rows
    extra = ()
    extra_in = []
    extra_out = []
    if copied is not None:
        shape = copied.shape[2:]
        extra = (copied, copied)
        extra_in = [
            pl.BlockSpec((1, 1) + shape, lambda i, s: (s[1] % 2, 0, 0, 0)),
            pl.BlockSpec((1, 1) + shape, lambda i, s: (1 - s[1] % 2, 0, 0, 0)),
        ]
        extra_out = [(shape, BF16, pl.BlockSpec(shape, lambda i, s: (0, 0)))] * 2
    vector = pl.BlockSpec((8, width), lambda i, s: (0, 0))
    part = pl.BlockSpec((rows // group, width), lambda i, s: (0, 0))
    row = pl.BlockSpec((rows, own), lambda i, s: (index, 0))
    weights = [
        pl.BlockSpec((width, own), functools.partial(lambda t, i, s: (0, t * group + s[0]), t))
        for t in range(3)
    ]
    return call(
        functools.partial(project_kernel, group, copied is not None),
        "project",
        place,
        tuple(parts) + (vectors, qkv_weight, qkv_weight, qkv_weight, qv_bias) + extra,
        (1,),
        [part] * group
        + [vector]
        + weights
        + [pl.BlockSpec((2, own), lambda i, s: (0, s[0]))]
        + extra_in,
        [
            ((length, width), BF16, pl.BlockSpec((rows, width), lambda i, s: (index, 0))),
            ((width, length), BF16, pl.BlockSpec((width, rows), lambda i, s: (0, index))),
        ]
        + [((length, own), BF16, row)] * 3
        + extra_out,
        fill=fill,
    )


def attend_kernel(limit, sub, place, q_ref, k_ref, v_ref, segc_ref, segr_ref, mixed_ref, lse_ref):
    keys = k_ref[...]
    keys = jnp.concatenate([keys, keys], axis=1)
    values = v_ref[...]
    values = jnp.concatenate([values, jnp.ones(values.shape, BF16)], axis=1)
    lane = lax.broadcasted_iota(jnp.int32, (sub, PAIR), 1)
    zero = jnp.zeros((), BF16)
    segr = segr_ref[...]
    for start in range(0, q_ref.shape[0], sub):
        part = pl.ds(start, sub)
        scaled = q_ref[part].astype(F32) * (SCALE * LOG2E)
        high = scaled.astype(BF16)
        low = (scaled - high.astype(F32)).astype(BF16)
        segc = segc_ref[part]
        valid = segc < limit
        bias = jnp.where(jnp.where(valid, segc, -1)[:, :1] == segr, 0.0, NEG)
        mixed = []
        logs = []
        for head in range(2):
            own = (lane < HEAD_DIM) == (head == 0)
            query = jnp.concatenate([jnp.where(own, high, zero), jnp.where(own, low, zero)], axis=1)
            scores = dot(query, keys, NT) + bias
            largest = jnp.max(scores, axis=1, keepdims=True)
            weights = jnp.exp2(scores - largest).astype(BF16)
            summed = dot(weights, values)
            total = summed[:, PAIR:]
            mixed.append(summed[:, :PAIR] / total)
            logs.append(largest + jnp.log2(total))
        first = lane < HEAD_DIM
        mixed_ref[part] = jnp.where(valid, jnp.where(first, mixed[0], mixed[1]), 0.0).astype(BF16)
        lse_ref[part] = jnp.where(valid, jnp.where(first, logs[0], logs[1]), 0.0)


def attend(place, first, count, query, keys, values, seg_cols, seg_row, limit, after=()):
    length = query.shape[0]
    width = count * PAIR
    block = min(1024, length)
    tile = pl.BlockSpec((block, PAIR), lambda p, j, s: (j, first + p))
    whole = pl.BlockSpec((length, PAIR), lambda p, j, s: (0, first + p))
    out_tile = pl.BlockSpec((block, PAIR), lambda p, j, s: (j, p))
    return call(
        functools.partial(attend_kernel, limit, min(256, block)),
        "attend",
        place,
        (query, keys, values, seg_cols, seg_row),
        (width // PAIR, length // block),
        [
            tile,
            whole,
            whole,
            pl.BlockSpec((block, PAIR), lambda p, j, s: (j, 0)),
            pl.BlockSpec((1, length), lambda p, j, s: (0, 0)),
        ],
        [((length, width), BF16, out_tile), ((length, width), F32, out_tile)],
        after=after,
    )


def attend_back_kernel(
    limit,
    sub,
    grads,
    place,
    q_ref,
    k_ref,
    v_ref,
    do_ref,
    mixed_ref,
    lse_ref,
    segc_ref,
    segr_ref,
    *refs,
    lazy,
):
    kt_ref, dk_sum, dv_sum, side_ref, stage_ref, rows_ref = refs[-6:]
    pair = pl.program_id(0)
    step = pl.program_id(1)
    steps = pl.num_programs(1)
    own_width = side_ref.shape[1] // 3
    length = k_ref.shape[0]
    keys = k_ref[...]
    kt_ref[...] = keys.T
    zero = jnp.zeros((), BF16)
    minus = -jnp.ones((), BF16)
    values = v_ref[...]
    key_lane = lax.broadcasted_iota(jnp.int32, (length, PAIR), 1)
    lane = lax.broadcasted_iota(jnp.int32, (sub, PAIR), 1)
    spot = lane & (HEAD_DIM - 1)
    ones = jnp.where((key_lane & (HEAD_DIM - 1)) < 3, minus, zero)
    key_sides = []
    value_sides = []
    for head in range(2):
        own = (key_lane < HEAD_DIM) == (head == 0)
        key_sides.append(jnp.concatenate([jnp.where(own, keys, ones), keys], axis=1))
        value_sides.append(jnp.where(own, values, ones))
    segc = segc_ref[...]
    segc = jnp.where(segc < limit, segc, -1)[:, :1]

    def in_three(value):
        high = value.astype(BF16)
        rest = value - high.astype(F32)
        middle = rest.astype(BF16)
        low = (rest - middle.astype(F32)).astype(BF16)
        return jnp.where(spot == 0, high, jnp.where(spot == 1, middle, jnp.where(spot == 2, low, zero)))

    dk_all = dv_all = None
    for start in range(0, q_ref.shape[0], sub):
        part = pl.ds(start, sub)
        query = q_ref[part]
        scaled = query.astype(F32) * (SCALE * LOG2E)
        high = scaled.astype(BF16)
        low = (scaled - high.astype(F32)).astype(BF16)
        grad = do_ref[part]
        product = grad.astype(F32) * mixed_ref[part].astype(F32)
        logs = lse_ref[part]
        same = segc == segr_ref[:, part]
        dq_rows = []
        for head in range(2):
            own = (lane < HEAD_DIM) == (head == 0)
            log = jnp.broadcast_to(logs[:, head * HEAD_DIM : head * HEAD_DIM + 1], logs.shape)
            delta = jnp.sum(jnp.where(own, product, 0.0), axis=1, keepdims=True)
            delta = jnp.broadcast_to(delta, logs.shape)
            query_side = jnp.concatenate(
                [jnp.where(own, high, in_three(log)), jnp.where(own, low, zero)], axis=1
            )
            grad_side = jnp.where(own, grad, in_three(delta))
            scores = dot(key_sides[head], query_side, NT)
            probs = jnp.where(same, jnp.exp2(scores), 0.0).astype(BF16)
            d_probs = dot(value_sides[head], grad_side, NT)
            d_scores = probs * d_probs.astype(BF16)
            dv_part = dot(probs, jnp.where(own, grad, zero))
            dk_part = dot(d_scores, jnp.where(own, query, zero))
            dv_all = dv_part if dv_all is None else dv_all + dv_part
            dk_all = dk_part if dk_all is None else dk_all + dk_part
            dq_rows.append(dot(kt_ref[head * HEAD_DIM : (head + 1) * HEAD_DIM], d_scores))
        target = pl.ds(pl.multiple_of(step * q_ref.shape[0] + start, sub), sub)
        columns = pl.ds(pl.multiple_of(pair * PAIR, PAIR), PAIR)
        side_ref[target, columns] = (jnp.concatenate(dq_rows, axis=0).T * SCALE).astype(BF16)
    dk_all = dk_all * SCALE

    @pl.when(step == 0)
    def _():
        dk_sum[...] = dk_all
        dv_sum[...] = dv_all

    @pl.when(step > 0)
    def _():
        dk_sum[...] += dk_all
        dv_sum[...] += dv_all

    @pl.when(step == steps - 1)
    def _():
        for place_of, sum_ref in ((1, dk_sum), (2, dv_sum)):
            columns = pl.ds(pl.multiple_of(place_of * own_width + pair * PAIR, PAIR), PAIR)
            side_ref[:, columns] = sum_ref[...].astype(BF16)

    @pl.when((step == steps - 1) & (pair == pl.num_programs(0) - 1))
    def _():
        arrive, buffers = lazy
        arrive()
        grads(place, side_ref, stage_ref, rows_ref, *buffers, *refs[:-6])


def attend_back(
    place,
    first,
    count,
    query,
    keys,
    values,
    d_mixed,
    mixed,
    logs,
    seg_cols,
    seg_row,
    limit,
    hidden_t,
    group,
    chips,
    slice_rows,
    branch=None,
    mixed_parts=(),
    earlier=(),
    split=True,
    after=(),
):
    length = mixed.shape[0]
    own = count * PAIR
    block = length if length <= 1024 else 256
    tile = pl.BlockSpec((block, PAIR), lambda p, j, s: (j, first + p))
    whole = pl.BlockSpec((length, PAIR), lambda p, j, s: (0, first + p))
    width = hidden_t.shape[0]
    some = width // chips
    calls = len(mixed_parts)
    columns = 3 * own + (width // group if calls else 0)
    cut = columns // 2 if split else columns
    sides = (length // group, 3 * own + (earlier[0].shape[1] if earlier else 0))
    lazy = [(hidden_t, lambda ref, s: ref, hidden_t.shape)]
    if calls:
        share = width // group
        lazy.append(
            (
                branch,
                lambda ref, s: ref.at[:, pl.ds(pl.multiple_of(s[0] * share, share), share)],
                (length, share),
            )
        )
        lazy += [
            (mixed_parts[j][s], lambda ref, s: ref, mixed_parts[j][s].shape)
            for j in range(calls)
            for s in range(group)
        ]
    lazy += [(array, lambda ref, s: ref, array.shape) for array in earlier]

    def pieces(columns):
        shape = (chips // 2, some, columns)
        spec = pl.BlockSpec(shape, lambda p, j, s: (0, 0, 0))
        return [(shape, BF16, spec, KEEP), (shape, BF16, spec, PIN)]

    return call(
        functools.partial(
            attend_back_kernel,
            limit,
            min(256, block),
            functools.partial(attention_grads, group, calls, chips, cut, bool(earlier)),
        ),
        "attend_back",
        place,
        (query, keys, values, d_mixed, mixed, logs, seg_cols, seg_row),
        (own // PAIR, length // block),
        [
            tile,
            whole,
            whole,
            tile,
            tile,
            tile,
            pl.BlockSpec((length, PAIR), lambda p, j, s: (0, 0)),
            pl.BlockSpec((1, block), lambda p, j, s: (0, j)),
        ],
        [(sides, BF16, pl.BlockSpec(sides, lambda p, j, s: (0, 0)))] * group
        + pieces(cut)
        + (pieces(columns - cut) if split else []),
        [
            pltpu.VMEM((PAIR, length), BF16),
            pltpu.VMEM((length, PAIR), F32),
            pltpu.VMEM((length, PAIR), F32),
            pltpu.VMEM((length, 3 * own), BF16),
            pltpu.VMEM((chips, some, columns), BF16),
            pltpu.VMEM((length // slice_rows, slice_rows, 3 * own), BF16),
        ],
        lazy=lazy,
        after=after,
    )


def collect(group, place, part_refs, rows_ref, sums_ref):
    count = part_refs[0].shape[0]
    total = None
    for index, part_ref in enumerate(part_refs):
        block, steps = index // group, index % group
        values = part_ref[...]
        spot = block * group + (place[0] + group - steps) % group
        rows_ref[pl.ds(pl.multiple_of(spot * count, count), count)] = values
        part = jnp.sum(values.astype(F32), axis=0, keepdims=True)
        total = part if total is None else total + part
    sums_ref[...] = jnp.concatenate([total, jnp.zeros((7, total.shape[1]), F32)], axis=0)


def close_kernel(number, place, x_ref, vec_ref, *refs):
    mixed_refs = refs[:number]
    weight_refs = refs[number : 2 * number]
    keep_ref, scale_ref, own_ref, hidden_ref, ht_ref, middle_ref = refs[2 * number :]
    gain = vec_ref[2:3]
    shift = vec_ref[3:4]
    bias = vec_ref[4:5]
    sub = 256
    for start in range(0, x_ref.shape[0], sub):
        part = pl.ds(start, sub)
        middle = x_ref[part].astype(F32) + bias
        for mixed_ref, weight_ref in zip(mixed_refs, weight_refs):
            middle = middle + dot(mixed_ref[part], weight_ref[...])
        middle_ref[part] = middle
        normal, inverse = norm_parts(middle)
        keep_ref[part] = normal.astype(BF16)
        scale_ref[part] = jnp.broadcast_to(inverse, (sub, scale_ref.shape[1]))
        hidden = (normal * gain + shift).astype(BF16)
        hidden_ref[part] = hidden
        ht_ref[:, part] = hidden.T
    count = own_ref.shape[0]
    own_ref[...] = middle_ref[pl.ds(pl.multiple_of(place[0] * count, count), count)]


def close(place, x_rows, mixed_parts, group, out_weight, vectors, slice_rows, after=()):
    length, width = x_rows.shape
    calls = len(mixed_parts)
    number = calls * group
    own = width // number
    rows = slice_rows * group
    vector = pl.BlockSpec((8, width), lambda i, s: (0, 0))
    row = pl.BlockSpec((rows, width), lambda i, s: (i, 0))
    arrays = []
    weights = []
    for j in range(calls):
        for steps in range(group):
            arrays.append(mixed_parts[j][steps])
            weights.append(
                pl.BlockSpec(
                    (own, width),
                    functools.partial(lambda j, t, i, s: (((s[0] + group - t) % group) * calls + j, 0), j, steps),
                )
            )
    return call(
        functools.partial(close_kernel, number),
        "close",
        place,
        (x_rows, vectors)
        + tuple(arrays)
        + (out_weight,) * number,
        (length // rows,),
        [row, vector] + [pl.BlockSpec((rows, own), lambda i, s: (i, 0))] * number + weights,
        [
            ((length, width), BF16, row),
            ((length, 128), F32, pl.BlockSpec((rows, 128), lambda i, s: (i, 0))),
            ((length // group, width), F32, pl.BlockSpec((slice_rows, width), lambda i, s: (i, 0))),
            ((length, width), BF16, row, length <= 1024),
            ((width, length), BF16, pl.BlockSpec((width, rows), lambda i, s: (0, i)), length <= 1024),
        ],
        [pltpu.VMEM((rows, width), F32)],
        after=after,
    )


def up_specs(width, tile, block, group, number):
    return [
        pl.BlockSpec((width, block), functools.partial(lambda n, t, s: (0, (t * number + n) * group + s[0]), n))
        for n in range(number)
    ]


def feed_up_kernel(number, group, count, cut, place, h_ref, upb_ref, *refs):
    part_refs = refs[:count]
    refs = refs[count:]
    up_refs = refs[:number]
    cot_ref, cot_sums_ref = refs[-4:-2]
    refs = refs[:-4] + refs[-2:]

    @pl.when(pl.program_id(0) == 0)
    def _():
        collect(group, place, part_refs, cot_ref, cot_sums_ref)

    active_refs = refs[number : number + group]
    slope_ref, ka_ref, sa_ref, kb_ref, sb_ref, stage_ref, rows_ref = refs[number + group :]
    up = jnp.concatenate([ref[...] for ref in up_refs], axis=1) if number > 1 else up_refs[0][...]
    upper = dot(h_ref[...], up) + upb_ref[...].astype(F32)
    half = 0.5 + 0.5 * lax.erf(upper * 0.7071067811865476)
    bell = jnp.exp2(upper * upper * (-0.5 * LOG2E)) * 0.3989422804014327
    active = (upper * half).astype(BF16)
    hand_out(rows_ref, group, place[0], active, active_refs)
    slope_ref[...] = (half + upper * bell).astype(BF16)
    stage_ref[...] = dot(active, cot_ref[...], TN).astype(BF16).reshape(stage_ref.shape)
    deal(
        stage_ref,
        place[1] % stage_ref.shape[0],
        [(ka_ref, sa_ref, 1, slice(0, cut)), (kb_ref, sb_ref, 0, slice(cut, None))],
    )


def feed_up(place, hidden, cot_parts, up_arrays, up_blocks, upb_own, group, chips, cut, rows, after=()):
    length, width = hidden.shape
    ff = upb_own.shape[1]
    chunk = ff // chips
    tile = min(512 if length <= 1024 else 128, ff)
    parts = tile // chunk
    whole = pl.BlockSpec((length, width), lambda t, s: (0, 0), pipeline_mode=pl.Buffered(1))
    tiled = pl.BlockSpec((length, tile), lambda t, s: (0, t))
    number, specs = up_blocks(tile)

    def piece(columns):
        spec = pl.BlockSpec(
            (parts // 2, chunk, columns), lambda t, s: (jnp.bitwise_xor(t, s[1] // parts), 0, 0)
        )
        return ((chips // 2, chunk, columns), BF16, spec, PIN)

    return call(
        functools.partial(feed_up_kernel, number, group, len(cot_parts), cut),
        "feed_up",
        place,
        (hidden, upb_own) + tuple(cot_parts) + (up_arrays,) * number,
        (ff // tile,),
        [whole, pl.BlockSpec((1, tile), lambda t, s: (0, t))]
        + [
            pl.BlockSpec(part.shape, lambda t, s: (0, 0), pipeline_mode=pl.Buffered(1)) for part in cot_parts
        ]
        + specs,
        [
            (
                (length // group, ff),
                BF16,
                pl.BlockSpec((length // group, tile), lambda t, s: (0, t)),
            )
        ]
        * group
        + [((length, ff), BF16, tiled, length <= 1024)]
        + [piece(cut)] * 2
        + [piece(width - cut)] * 2
        + [
            ((length, width), BF16, pl.BlockSpec((length, width), lambda t, s: (0, 0)), True),
            ((8, width), F32, pl.BlockSpec((8, width), lambda t, s: (0, 0))),
        ],
        [pltpu.VMEM((parts, chunk, width), BF16), pltpu.VMEM((length // rows, rows, tile), BF16)],
        after=after,
    )


def feed_back_kernel(number, chips, split, place, ht_ref, cot_ref, slope_ref, down_ref, *refs):
    up_refs = refs[:number]
    dh_refs = refs[number : number + DH_PIECES]
    dub_ref, ka_ref, sa_ref, kb_ref, sb_ref, dh_sum, stage_ref = refs[number + DH_PIECES :]
    step = pl.program_id(0)
    up = jnp.concatenate([ref[...] for ref in up_refs], axis=1) if number > 1 else up_refs[0][...]
    down = down_ref[...]
    down = down.reshape(down.shape[0] * down.shape[2], down.shape[3])
    d_upper = (dot(cot_ref[...], down, NT) * slope_ref[...].astype(F32)).astype(BF16)
    dub_ref[...] = jnp.sum(d_upper.astype(F32), axis=0, keepdims=True)
    length = d_upper.shape[0]
    rows = min(1024, length)

    def add(start):
        part = dot(d_upper[start : start + rows], up, NT)

        @pl.when(step == 0)
        def _():
            dh_sum[start : start + rows] = part

        @pl.when(step > 0)
        def _():
            dh_sum[start : start + rows] += part

    for start in range(0, length, rows):
        add(start)

    rows = ht_ref.shape[0] // chips
    many = max(1, 256 // rows)
    for start in range(0, chips, many):
        grad = dot(ht_ref[start * rows : (start + many) * rows], d_upper).astype(BF16)
        stage_ref[start : start + many] = grad.reshape(many, rows, grad.shape[1])

    @pl.when(step < split)
    def _():
        deal(stage_ref, place[1], [(ka_ref, sa_ref, 1, slice(None))])

    @pl.when(step >= split)
    def _():
        deal(stage_ref, place[1], [(kb_ref, sb_ref, 0, slice(None))])

    @pl.when(step == pl.num_programs(0) - 1)
    def _():
        piece_rows = dh_refs[0].shape[0]
        for index, dh_ref in enumerate(dh_refs):
            dh_ref[...] = dh_sum[index * piece_rows : (index + 1) * piece_rows].astype(BF16)


def feed_back(
    place, hidden_t, cotangent, slope, down_weight, up_arrays, up_blocks, group, chips, share, after=()
):
    width, length = hidden_t.shape
    ff = slope.shape[1]
    chunk = ff // chips
    tile = min(512 if length <= 1024 else 128, ff)
    parts = tile // chunk
    number, specs = up_blocks(tile)
    tiles = ff // tile
    split = max(1, min(tiles - 1, round(tiles * share)))
    some = width // chips

    def piece(first, last, pin):
        spec = pl.BlockSpec(
            (chips // 2, some, tile), lambda t, s: (0, 0, jnp.clip(t, first, last - 1) - first)
        )
        return ((chips // 2, some, (last - first) * tile), BF16, spec, pin)

    return call(
        functools.partial(feed_back_kernel, number, chips, split),
        "feed_back",
        place,
        (hidden_t, cotangent, slope, down_weight.reshape(chips, group, chunk, width)) + (up_arrays,) * number,
        (ff // tile,),
        [
            pl.BlockSpec((width, length), lambda t, s: (0, 0), pipeline_mode=pl.Buffered(1)),
            pl.BlockSpec((length, width), lambda t, s: (0, 0), pipeline_mode=pl.Buffered(1)),
            pl.BlockSpec((length, tile), lambda t, s: (0, t)),
            pl.BlockSpec((parts, 1, chunk, width), lambda t, s: (t, s[0], 0, 0)),
        ]
        + specs,
        [
            (
                (length // DH_PIECES, width),
                BF16,
                pl.BlockSpec((length // DH_PIECES, width), lambda t, s: (0, 0)),
                True,
            )
        ]
        * DH_PIECES
        + [((1, ff), F32, pl.BlockSpec((1, tile), lambda t, s: (0, t)))]
        + [piece(0, split, KEEP), piece(0, split, PIN)]
        + [piece(split, tiles, KEEP), piece(split, tiles, PIN)],
        [pltpu.VMEM((length, width), F32), pltpu.VMEM((chips, some, tile), BF16)],
        after=after,
    )


def feed_down_kernel(group, place, vec_ref, *refs, lazy):
    down_refs = refs[group : 2 * group]
    active_refs = refs[:group]
    near_ref, far_ref, sum_ref = refs[2 * group :]
    step = pl.program_id(0)
    total = None
    for active_ref, down_ref in zip(active_refs, down_refs):
        down = down_ref[...]
        part = dot(active_ref[...], down.reshape(-1, down.shape[3]))
        total = part if total is None else total + part

    @pl.when(step == 0)
    def _():
        sum_ref[...] = total

    @pl.when(step > 0)
    def _():
        sum_ref[...] += total

    @pl.when(step == pl.num_programs(0) - 1)
    def _():
        arrive, (middle_ref,) = lazy
        arrive()
        half = near_ref.shape[0]
        for start, out_ref in ((0, near_ref), (half, far_ref)):
            part = pl.ds(start, half)
            out_ref[...] = (middle_ref[part] + sum_ref[part] + vec_ref[5:6]).astype(BF16)


def feed_down(place, active_parts, down_weight, middle, vectors, chips, after=()):
    group = len(active_parts)
    rows, ff = active_parts[0].shape
    width = down_weight.shape[1]
    chunk = ff // chips
    tile = min(512, ff)
    out = ((rows // 2, width), BF16, pl.BlockSpec((rows // 2, width), lambda i, s: (0, 0)))
    return call(
        functools.partial(feed_down_kernel, group),
        "feed_down",
        place,
        (vectors,) + tuple(active_parts) + (down_weight.reshape(chips, group, chunk, width),) * group,
        (ff // tile,),
        [pl.BlockSpec((8, width), lambda i, s: (0, 0))]
        + [pl.BlockSpec((rows, tile), lambda i, s: (0, i))] * group
        + [
            pl.BlockSpec(
                (tile // chunk, 1, chunk, width),
                functools.partial(lambda t, i, s: (i, (s[0] + group - t) % group, 0, 0), steps),
            )
            for steps in range(group)
        ],
        [out, out],
        [pltpu.VMEM((rows, width), F32)],
        lazy=[(middle, lambda ref, s: ref, (rows, width))],
        after=after,
    )


def middle_back_kernel(group, span, turn, place, normal_ref, scale_ref, cot_ref, vec_ref, weight_ref, *refs):
    part_refs = refs[: group * DH_PIECES]
    branch_ref, d_middle_ref, d_mixed_ref, sums_ref, sum_ref = refs[group * DH_PIECES :]
    step = pl.program_id(0)

    def gather(piece):
        @pl.when(step // span == piece)
        def _():
            total = part_refs[piece * group][...].astype(F32)
            for ref in part_refs[piece * group + 1 : (piece + 1) * group]:
                total = total + ref[...].astype(F32)
            sum_ref[...] = total

    for piece in range(DH_PIECES):
        gather(piece)
    d_hidden = sum_ref[...]
    normal = normal_ref[...].astype(F32)
    inverse = scale_ref[...][:, :1]
    d_middle = cot_ref[...].astype(F32) + norm_back(d_hidden, normal, inverse, vec_ref[2:3])
    branch = d_middle.astype(BF16)
    branch_ref[...] = branch

    @pl.when(step // turn % group == place[0])
    def _():
        d_middle_ref[...] = d_middle

    d_mixed_ref[...] = dot(branch, weight_ref[...], NT).astype(BF16)
    sums = jnp.concatenate(
        [
            jnp.sum(d_hidden * normal, axis=0, keepdims=True),
            jnp.sum(d_hidden, axis=0, keepdims=True),
            jnp.sum(branch.astype(F32), axis=0, keepdims=True),
            jnp.zeros((5, branch.shape[1]), F32),
        ],
        axis=0,
    )

    @pl.when(step == 0)
    def _():
        sums_ref[...] = sums

    @pl.when(step > 0)
    def _():
        sums_ref[...] += sums


def middle_back(place, normal, scale, cotangent, vectors, out_weight, parts, slice_rows, after=()):
    length, width = normal.shape
    group = len(parts[0])
    own = width // group
    rows = min(256, length // DH_PIECES, slice_rows)
    turn = slice_rows // rows
    span = length // DH_PIECES // rows
    row = pl.BlockSpec((rows, width), lambda i, s: (i, 0))
    specs = [
        pl.BlockSpec(
            (rows, width), functools.partial(lambda k, i, s: (jnp.clip(i - k * span, 0, span - 1), 0), piece)
        )
        for piece in range(DH_PIECES)
        for _ in range(group)
    ]
    return call(
        functools.partial(middle_back_kernel, group, span, turn),
        "middle_back",
        place,
        (normal, scale, cotangent, vectors, out_weight) + tuple(array for piece in parts for array in piece),
        (length // rows,),
        [
            row,
            pl.BlockSpec((rows, 128), lambda i, s: (i, 0)),
            row,
            pl.BlockSpec((8, width), lambda i, s: (0, 0)),
            pl.BlockSpec((own, width), lambda i, s: (s[0], 0)),
        ]
        + specs,
        [
            ((length, width), BF16, row, length <= 1024),
            (
                (length // group, width),
                F32,
                pl.BlockSpec((rows, width), lambda i, s: (i // (turn * group) * turn + i % turn, 0)),
            ),
            ((length, own), BF16, pl.BlockSpec((rows, own), lambda i, s: (i, 0)), length <= 1024),
            ((8, width), F32, pl.BlockSpec((8, width), lambda i, s: (0, 0))),
        ],
        [pltpu.VMEM((rows, width), F32)],
        after=after,
    )


def attention_grads(group, calls, chips, cut, earlier, place, side_ref, stage_ref, rows_ref, ht_ref, *refs):
    number = group * calls
    mixed_refs = refs[1 : 1 + number]
    outs = refs[1 + number :] if calls else refs
    if earlier:
        before_refs, outs = outs[:group], outs[group:]
        for before_ref, out_ref in zip(before_refs, outs):
            out_ref[:, : before_ref.shape[1]] = before_ref[...]
    side_refs = outs[:group]
    piece_refs = outs[group:]
    offset = 0
    if calls:
        branch = refs[0][...]
        offset = branch.shape[1]
        share = chips // number
        for index, mixed_ref in enumerate(mixed_refs):
            owner = ((place[0] + group - index % group) % group) * calls + index // group
            grad = dot(mixed_ref[...], branch, TN).astype(BF16)
            rows = grad.shape[0] // share
            stage_ref[pl.ds(owner * share, share), :, :offset] = grad.reshape(share, rows, offset)
    side = side_ref[...]
    hand_out(rows_ref, group, place[0], side, side_refs)
    rows = ht_ref.shape[0] // chips
    many = max(1, 256 // rows)
    for start in range(0, chips, many):
        grad = dot(ht_ref[start * rows : (start + many) * rows], side).astype(BF16)
        stage_ref[start : start + many, :, offset:] = grad.reshape(many, rows, grad.shape[1])
    columns = stage_ref.shape[2]
    for relative in range(chips):
        values = stage_ref[jnp.bitwise_xor(jnp.int32(relative), place[1])]
        if len(piece_refs) > 2:
            piece_refs[bool(relative & 2)][without_bit(relative, 1)] = values[:, :cut]
        piece_refs[(relative & 1) - 2][without_bit(relative, 0)] = values[:, cut % columns :]


def hidden_back_kernel(number, side_spot, share, place, vec_ref, *refs, lazy):
    side_refs = refs[:number]
    weight_refs = refs[number : number + 3]
    small_refs = refs[number + 3 : number + 5]
    near_ref, far_ref, sums_ref, sum_ref = refs[number + 5 :]
    step = pl.program_id(0)
    each = side_refs[0].shape[1] // 3
    half = near_ref.shape[0]

    @pl.when(step == 0)
    def _():
        sum_ref[...] = jnp.zeros_like(sum_ref)
        sums_ref[...] = jnp.zeros_like(sums_ref)

    def add(index):
        @pl.when(step == index)
        def _():
            side = side_refs[index][...]
            row_sums = jnp.sum(side.astype(F32), axis=0, keepdims=True)
            spot = pl.ds(pl.multiple_of(side_spot(index, place) * each, each), each)
            sums_ref[2:3, spot] = row_sums[:, :each]
            sums_ref[3:4, spot] = row_sums[:, 2 * each :]
            total = None
            for third, weight_ref in enumerate(weight_refs):
                part = dot(side[:, third * each : (third + 1) * each], weight_ref[...], NT)
                total = part if total is None else total + part
            sum_ref[...] += total

    for index in range(number):
        add(index)

    @pl.when(step == number - 1)
    def _():
        arrive, (x_ref, base_ref) = lazy
        arrive()
        sums = []
        for start, out_ref, block in ((0, near_ref, 0), (half, far_ref, x_ref.shape[0] // 2)):
            total = sum_ref[start : start + half]
            rows = x_ref[block : block + x_ref.shape[0] // 2].reshape(total.shape)
            normal, inverse = norm_parts(rows.astype(F32))
            sums.append(jnp.sum(total * normal, axis=0, keepdims=True))
            sums.append(jnp.sum(total, axis=0, keepdims=True))
            result = base_ref[start : start + half] + norm_back(total, normal, inverse, vec_ref[0:1])
            out_ref[...] = result.astype(BF16)
        sums_ref[0:1] = sums[0] + sums[2]
        sums_ref[1:2] = sums[1] + sums[3]
        sums_ref[4:5] = small_refs[0][2:3] * share
        sums_ref[5:7] = small_refs[0][0:2] * share
        sums_ref[7:8] = small_refs[1][0:1] * share


def hidden_back(
    place, x_rows, d_middle, vectors, sides, calls, qkv_weight, sums, cot_sums, slice_rows, after=()
):
    group = len(sides)
    rows, columns = sides[0].shape
    columns = columns // calls
    each = columns // 3
    length, width = x_rows.shape
    slices = length // group // slice_rows
    count = calls * group
    eight = pl.BlockSpec((8, width), lambda i, s: (0, 0))

    def side_spot(index, numbers):
        return ((numbers[0] + group - index % group) % group) * calls + index // group

    weights = [
        pl.BlockSpec(
            (width, each),
            functools.partial(lambda third, i, s: (0, third * group * calls + side_spot(i, s)), third),
        )
        for third in range(3)
    ]
    out = ((rows // 2, width), BF16, pl.BlockSpec((rows // 2, width), lambda i, s: (0, 0)))
    return call(
        functools.partial(hidden_back_kernel, count, side_spot, 1.0 / group),
        "hidden_back",
        place,
        (vectors,)
        + tuple(sides) * calls
        + (qkv_weight,) * 3
        + (sums, cot_sums),
        (count,),
        [
            pl.BlockSpec((8, width), lambda i, s: (0, 0)),
        ]
        + [
            pl.BlockSpec((rows, columns), functools.partial(lambda j, i, s: (0, j), index // group))
            for index in range(count)
        ]
        + weights
        + [eight, eight],
        [out, out, ((8, width), F32, pl.BlockSpec((8, width), lambda i, s: (0, 0)))],
        [pltpu.VMEM((rows, width), F32)],
        after=after,
        lazy=[
            (
                x_rows.reshape(slices, group, slice_rows, width),
                lambda ref, s: ref.at[:, s[0]],
                (slices, slice_rows, width),
            ),
            (d_middle, lambda ref, s: ref, (rows, width)),
        ],
    )


def join_kernel(place, near_ref, far_ref, out_ref):
    half = place[1] % 2
    out_ref[half, 0] = near_ref[...]
    out_ref[1 - half, 0] = far_ref[...]


def join(place, near, far, after=()):
    shape = (2, 1) + near.shape
    whole = pl.BlockSpec(near.shape, lambda i, s: (0, 0))
    return call(
        join_kernel,
        "join",
        place,
        (near, far),
        (1,),
        [whole, whole],
        [(shape, BF16, pl.BlockSpec(shape, lambda i, s: (0, 0, 0, 0)))],
        after=after,
    )[0]


def later(place, array, after):
    return call(
        lambda place_ref, out_ref: None,
        "later",
        place,
        (),
        (1,),
        [],
        [(array.shape, array.dtype, pl.BlockSpec(memory_space=pl.ANY))],
        after=after,
        fill=[array],
    )[0]


def part_kernel(counts, takes, whole, place, *refs):
    sources = []
    for count in counts:
        sources.append(refs[:count])
        refs = refs[count:]
    own_ref, send_ref = refs[:2]
    rows = own_ref.shape[0]
    mine = place[0] == 0
    start = 0

    def total(index, first, count):
        part = pl.ds(first, count)
        if len(sources[index]) == 1:
            return sources[index][0][part]
        return sum(source[0, part].astype(F32) for source in sources[index])

    for index, first in takes:
        both = total(index, first, 2 * rows)
        columns = both.shape[1]
        own_ref[:, start : start + columns] = jnp.where(mine, both[:rows], both[rows:])
        send_ref[:, start : start + columns] = jnp.where(mine, both[rows:], both[:rows]).astype(BF16)
        start += columns
    out_ref = refs[2]
    start = 0
    for index, first in whole:
        value = total(index, first, out_ref.shape[0])
        out_ref[:, start : start + value.shape[1]] = value
        start += value.shape[1]


def part_rows(place, sources, takes, rows, whole, whole_rows, after=()):
    columns = sum(sources[index][0].shape[-1] for index, _ in takes)
    out = pl.BlockSpec((rows, columns), lambda i, s: (0, 0))
    shape = (whole_rows, sum(sources[index][0].shape[-1] for index, _ in whole))
    arrays = [array for parts in sources for array in parts]
    return call(
        functools.partial(part_kernel, [len(parts) for parts in sources], takes, whole),
        "part_rows",
        place,
        tuple(arrays),
        (1,),
        [
            pl.BlockSpec(array.shape, functools.partial(lambda n, i, s: (0,) * n, array.ndim))
            for array in arrays
        ],
        [
            ((rows, columns), F32, out, True),
            ((rows, columns), BF16, out, True),
            (shape, F32, pl.BlockSpec(shape, lambda i, s: (0, 0))),
        ],
        after=after,
    )


def emit_kernel(moves, place, own_ref, came_ref, *out_refs):
    member = place[0]
    for source, size, out, column, stride in moves:
        for ref, who in ((own_ref, member), (came_ref, 1 - member)):
            spot = pl.ds(pl.multiple_of(column + who * stride, 128), size)
            out_refs[out][:, spot] = ref[:, source : source + size].astype(F32)


def emit(place, own, came, moves, widths, after=()):
    rows, columns = own.shape
    block = pl.BlockSpec((rows, columns), lambda i, s: (0, 0))
    return call(
        functools.partial(emit_kernel, moves),
        "emit",
        place,
        (own, came),
        (1,),
        [block, block],
        [((rows, width), F32, pl.BlockSpec((rows, width), lambda i, s: (0, 0))) for width in widths],
        after=after,
    )


def body(
    inputs,
    cotangent,
    image_lengths,
    norm1_gain,
    norm1_bias,
    qkv_weight,
    qv_bias,
    out_weight,
    out_bias,
    norm2_gain,
    norm2_bias,
    up_weight,
    up_bias,
    down_weight,
    down_bias,
):
    rows, width = inputs.shape[2:]
    limit = image_lengths.shape[-1]
    ff = up_weight.shape[1]
    dp_size = lax.axis_size("dp")
    ctx_size = lax.axis_size("ctx")
    group = ctx_size // 2
    dp_index = lax.axis_index("dp")
    ctx_index = lax.axis_index("ctx")
    half = ctx_index // group
    member = ctx_index % group
    length = rows * ctx_size
    chips = dp_size * 2
    dp_bits = dp_size.bit_length() - 1
    own_width = width // group
    own_ff = ff // group
    chunk = own_ff // chips
    place = Place(jnp.stack([member, dp_index * 2 + half]).astype(jnp.int32), length > 1024)

    def moved(value):
        place.free.append(value)
        return value

    def across(value):
        pairs = [(i, (i + group) % ctx_size) for i in range(ctx_size)]
        return moved(lax.ppermute(value, "ctx", pairs))

    def around(value, steps):
        pairs = [
            (h * group + g, h * group + (g + steps) % group) for h in range(2) for g in range(group)
        ]
        return moved(lax.ppermute(value, "ctx", pairs))

    def all_around(value):
        return [value] + [around(value, steps) for steps in range(1, group)]

    def in_order(parts, axis=0):
        if group == 2:
            first = member == 0
            return jnp.stack(
                [jnp.where(first, parts[0], parts[1]), jnp.where(first, parts[1], parts[0])], axis=axis
            )
        return jnp.roll(jnp.stack(parts[::-1], axis=axis), member + 1, axis=axis)

    def gather(value):
        return in_order(all_around(value))

    def pick(value, index, axis):
        return lax.dynamic_index_in_dim(value, index, axis, keepdims=False)

    def group_sum_scatter(value, axis):
        total = pick(value, member, axis).astype(F32)
        for steps in range(1, group):
            total = total + around(pick(value, (member + steps) % group, axis), steps).astype(F32)
        return total

    def swap_bit(value, bit):
        if bit < 0:
            return across(value)
        return moved(lax.ppermute(value, "dp", [(i, i ^ (1 << bit)) for i in range(dp_size)]))

    all_bits = list(range(dp_bits - 1, -1, -1)) + [-1]
    rest_bits = list(range(1, dp_bits))

    class Direct:
        order = ()
        direct = False

        def __init__(self, keep, sends, bits, then=()):
            self.then = then
            self.parts = [keep]
            low = min(bit for bit in bits if bit > 0)
            for index, send in enumerate(sends):
                flip = (index + 1) << low
                came = moved(lax.ppermute(send, "dp", [(i, i ^ flip) for i in range(dp_size)]))
                if not place.long:
                    place.pinned.append(came)
                self.parts.append(came)

    class Halving:
        direct = False

        def __init__(self, keep, send, bits, order, then=()):
            self.order = list(order)
            self.then = then
            self.left = list(bits)
            self.keep = keep
            self.came = swap_bit(send, self.order[0])
            if not place.long:
                place.pinned.append(self.came)
            self.order.pop(0)

    def crossed(pieces):
        first = [bit for bit in all_bits if bit != 0]
        second = [bit for bit in all_bits if bit != -1]
        return [
            Halving(*pieces[:2], first, [0] + rest_bits, (-1, 0)),
            Halving(*pieces[2:], second, [-1] + rest_bits, (-1, 0)),
        ]

    def pair(pieces):
        first = [bit for bit in all_bits if bit != 0]
        second = [bit for bit in all_bits if bit != -1]
        return [
            Halving(*pieces[:2], first, [0, -1] + rest_bits),
            Halving(*pieces[2:], second, [-1, 0] + rest_bits),
        ]

    def lone(pieces):
        return Halving(*pieces, [bit for bit in all_bits if bit != -1], [-1, 0] + rest_bits)

    def parts_of(item):
        if isinstance(item, Direct):
            return item.parts
        return [item.keep, item.came] if isinstance(item, Halving) else [item]

    state = {}

    def go(after, *names):
        jobs = []
        counts = []
        for name in names:
            item = state[name]
            if isinstance(item, list) and item[0].order[:1] != item[1].order[:1]:
                jobs += [[item[0]], [item[1]]]
                counts.append(2)
            else:
                jobs.append(item if isinstance(item, list) else [item])
                counts.append(1)
        ready, results = step(after, *jobs, cost=COST)
        for name, count in zip(names, counts):
            state[name] = [results.pop(0), results.pop(0)] if count == 2 else results.pop(0)
            if name == "late" and count == 2:
                state[name][0].direct = True
        return ready

    def step(after, *jobs, cost=0):
        asked = []
        for halvings in jobs:
            first = halvings[0]
            arrays = [array for halving in halvings for array in parts_of(halving)]
            if first.direct:
                asked.append((arrays, -2 if first.then else -1, 1))
            elif first.order:
                asked.append((arrays, len(first.left) - 1 - first.left.index(first.order[0]), 1))
            elif first.then:
                asked.append((arrays, 0, 2))
            else:
                asked.append((arrays, None, 1))
        sums = list(step_call(place, asked, after, cost))
        ready = sums[:1]
        results = []
        for halvings in jobs:
            first = halvings[0]
            if first.direct:
                sends = [sums.pop(0) for _ in range(first.keep.shape[0] // (2 if first.then else 1))]
                results.append(Direct(sends[0], sends[1:], first.left, first.then))
            elif first.order:
                left = [bit for bit in first.left if bit != first.order[0]]
                results.append(Halving(sums.pop(0), sums.pop(0), left, first.order, first.then))
            elif first.then:
                results.append([Halving(sums.pop(0), sums.pop(0), [], [bit]) for bit in first.then])
            else:
                results.append(sums.pop(0))
        return ready, results

    slices = 2 if group > 2 else 1
    slice_rows = rows // slices

    def sliced(value):
        return [value[c * slice_rows : (c + 1) * slice_rows] for c in range(slices)]

    own_inputs = pick(inputs, half, 0)[0]
    far_inputs = across(pick(inputs, 1 - half, 0)[0])
    vectors = jnp.stack([norm1_gain, norm1_bias, norm2_gain, norm2_bias, out_bias, down_bias, out_bias, out_bias])
    vectors = vectors.astype(F32)
    filled = ()
    for side, both_of in enumerate((own_inputs, far_inputs)):
        if filled:
            both_of = later(place, both_of, filled[3:4])
        for c, part in enumerate(sliced(both_of)):
            start = (side * slices + c) * (length // (2 * slices))
            copied = cotangent if side == 1 and c == 0 else None
            filled = project(
                place, all_around(part), start, length, vectors, qkv_weight, qv_bias, filled, copied
            )
            if copied is not None:
                *filled, own_cot, far_cot = filled
    x_rows, hidden1_t, query, keys, values = filled
    cot_parts = [part for value in sliced(own_cot) for part in all_around(value)]
    far_cot = across(far_cot)
    cot_parts += [part for value in sliced(far_cot) for part in all_around(value)]

    spots = jnp.arange(length, dtype=jnp.int32).reshape(2, group, slices, rows // slices)
    spots = jnp.swapaxes(spots, 1, 2)
    positions = jnp.where(half == 0, spots, spots[::-1]).reshape(length)
    ends = jnp.cumsum(pick(image_lengths, half, 0)[0])
    segment = jnp.sum((positions[:, None] >= ends[None, :]).astype(jnp.int32), axis=1)
    seg_row = segment.reshape(1, length)
    seg_cols = jnp.broadcast_to(segment[:, None], (length, PAIR))

    if chunk % 128 == 0:
        up_arrays = up_weight

        def up_blocks(tile):
            return tile // chunk, up_specs(width, tile, chunk, group, tile // chunk)

    else:
        up_arrays = pick(up_weight.reshape(width, chips, group, chunk), member, 2).reshape(width, own_ff)

        def up_blocks(tile):
            return 1, [pl.BlockSpec((width, tile), lambda t, s: (0, t))]

    upb_own = pick(up_bias.reshape(chips, group, chunk), member, 1).reshape(1, own_ff)

    pairs = own_width // PAIR
    calls = min(2, pairs)
    each = pairs // calls
    mixed, logs = attend(place, 0, pairs, query, keys, values, seg_cols, seg_row, limit)
    mixed_parts = [all_around(mixed)]
    normal2, scale2, middle_own, hidden2, hidden2_t = close(
        place, x_rows, mixed_parts, group, out_weight, vectors, slice_rows, after=cot_parts[-1:]
    )
    up_out = feed_up(
        place,
        hidden2,
        cot_parts,
        up_arrays,
        up_blocks,
        upb_own,
        group,
        chips,
        width // 2,
        slice_rows,
    )
    active_parts = up_out[:group]
    slope, *down_pieces, cot_rows, cot_sums = up_out[group:]
    active_parts = [active_parts[0]] + [around(active_parts[steps], steps) for steps in range(1, group)]
    state["down"] = crossed(down_pieces)
    state["down"][0].direct = True
    back = feed_back(
        place,
        hidden2_t,
        cot_rows,
        slope,
        down_weight,
        up_arrays,
        up_blocks,
        group,
        chips,
        0.5,
        after=down_pieces[:1],
    )
    dh_pieces = back[:DH_PIECES]
    upb_grad, *up_pieces = back[DH_PIECES:]
    dh_parts = [all_around(piece) for piece in dh_pieces]
    if not place.long:
        place.pinned += [part for parts in dh_parts for part in parts[1:]]
    state["up"] = pair(up_pieces)

    ready = go(dh_pieces[:1], "down")
    branch, d_middle, d_mixed, sums = middle_back(
        place, normal2, scale2, cot_rows, vectors, out_weight, dh_parts, slice_rows, after=ready
    )

    out_near, out_far = feed_down(place, active_parts, down_weight, middle_own, vectors, chips, after=[branch])
    out_far = across(out_far)

    def back_of(j, earlier, after):
        results = attend_back(
            place,
            j * each,
            each,
            query,
            keys,
            values,
            d_mixed,
            mixed,
            logs,
            seg_cols,
            seg_row,
            limit,
            hidden1_t,
            group,
            chips,
            slice_rows,
            branch if j == 0 else None,
            mixed_parts if j == 0 else (),
            earlier,
            after=after,
        )
        pieces = results[group:]
        halvings = pair(pieces) if len(pieces) > 2 else [lone(pieces)]
        halvings = halvings if len(halvings) > 1 else halvings[0]
        return halvings, list(results[:group]), list(results[:1])

    state["early"], sides, ready = back_of(0, [], [out_near])
    ready = go(ready, "down", "up")
    if calls > 1:
        state["late"], sides, ready = back_of(1, sides, ready)
    else:
        state["late"] = state.pop("early")
    others = [name for name in ("early",) if name in state]
    sides = [sides[0]] + [around(sides[steps], steps) for steps in range(1, group)]
    ready = go(ready, "up", *others)
    input_near, input_far, own_sums = hidden_back(
        place, x_rows, d_middle, vectors, sides, calls, qkv_weight, sums, cot_sums, slice_rows, after=ready
    )
    ready = [input_near]

    own = width // (chips * group)
    member_is = (jnp.arange(group, dtype=jnp.int32) == member).astype(F32)
    small = jnp.transpose(own_sums.reshape(8, chips * group, own), (1, 0, 2)).reshape(chips * group, 8 * own)
    upb_full = (upb_grad.reshape(chips, 1, chunk) * member_is[None, :, None]).reshape(chips * group, chunk)
    small = jnp.concatenate([small, upb_full], axis=1)
    ready = ready + [small]
    small = lax.all_to_all(small, ("dp", "ctx"), 0, 0, tiled=True)
    small = jnp.sum(small, axis=0)
    small_rows = small[: 8 * own].reshape(8, own)
    upb_out = small[8 * own :]

    input_far = across(input_far)
    ready = go(ready, "late", "up", *others)
    block_output = join(place, out_near, out_far, after=ready)
    ready = [block_output]
    ready = go(ready, "late", "up", *others)
    input_grad = join(place, input_near, input_far, after=ready)
    ready = [input_grad]

    def waits(item):
        return isinstance(item, (Halving, Direct)) and (item.order or item.then)

    while any(waits(item) for item in state.values()):
        ready = go(ready, *[name for name in state if waits(state[name])])

    some = width // chips

    def exchange(value):
        value = value.reshape(group, own, value.shape[1])
        parts = [pick(value, member, 0)] + [
            around(pick(value, (member + steps) % group, 0).astype(BF16), steps).astype(F32)
            for steps in range(1, group)
        ]
        return in_order(parts, 1)

    def sums_in(item):
        parts = parts_of(item)
        return parts[0] if len(parts) == 1 else sum(part[0].astype(F32) for part in parts)

    rest = others + ["late"]
    if group == 2 and own % 16 == 0:
        sources = [parts_of(item) for item in state["down"] + [state[name] for name in ["up"] + rest]]
        own_rows, send_rows, down_out = part_rows(
            place,
            sources,
            [(2, k * some) for k in range(own_ff // sources[2][0].shape[-1])]
            + [
                (index, first)
                for index in range(3, len(sources))
                for first in range(0, sources[index][0].shape[-2], some)
            ],
            own,
            [(0, 0), (1, 0)],
            chunk,
            ready,
        )
        moves = [(k * chunk, chunk, 0, k * 2 * chunk, chunk) for k in range(chips)]
        moves += [(own_ff, own_width, 1, 0, own_width)]
        moves += [
            (own_ff + own_width + (j * 3 + t) * each * PAIR, each * PAIR, 2, t * width + j * each * PAIR, own_width)
            for j in range(calls)
            for t in range(3)
        ]
        up_out, out_out, qkv_out = emit(place, own_rows, around(send_rows, 1), moves, [ff, width, 3 * width])
    else:

        def blocks_of(value, rows):
            return [value[start : start + rows] for start in range(0, value.shape[0], rows)]

        down_out = jnp.concatenate([sums_in(item) for item in state["down"]], axis=1)
        up_out = jnp.concatenate(blocks_of(sums_in(state["up"]), some), axis=1)
        up_out = exchange(up_out).reshape(own, group, chips, chunk)
        up_out = jnp.swapaxes(up_out, 1, 2).reshape(own, ff)
        parts = [part for name in rest for part in blocks_of(sums_in(state[name]), some)]
        rest = exchange(jnp.concatenate(parts, axis=1))
        out_out = rest[:, :, :own_width].reshape(own, width)
        qkv_out = rest[:, :, own_width:].reshape(own, group, calls, 3, each * PAIR)
        qkv_out = jnp.transpose(qkv_out, (0, 3, 1, 2, 4)).reshape(own, 3 * width)
    return (
        block_output,
        input_grad,
        small_rows[0],
        small_rows[1],
        qkv_out,
        small_rows[2:4],
        out_out,
        small_rows[4],
        small_rows[5],
        small_rows[6],
        up_out,
        upb_out,
        down_out,
        small_rows[7],
    )


def solution(mesh):
    split = P(None, "dp", "ctx", None)
    both = ("dp", "ctx")
    return jax.shard_map(
        body,
        mesh=mesh,
        in_specs=(split, split, P(None, "dp", None)) + (P(),) * 12,
        out_specs=(
            split,
            split,
            P(both),
            P(both),
            P(both, None),
            P(None, both),
            P(both, None),
            P(both),
            P(both),
            P(both),
            P(both, None),
            P(both),
            P(both, None),
            P(both),
        ),
        check_vma=False,
    )
```
